32 devices in a mesh: grp: 2 (over x), row: 8 (over z, y), col: 2 (over core).
Axes of the slice: x: 2, y: 2, z: 4, core: 2. Of those that a mesh axis runs over, the one named last changes fastest.
Arguments:
- pair: bfloat16 [352, 176, 128], P(('grp', 'row'), 'col'), parts along dimension 0, may hold values from -6 to 6
- cotangent: bfloat16 [352, 176, 128], P(('grp', 'row'), 'col'), parts along dimension 0, may hold values from -6 to 6
- chain_lengths: int32 [16], P('grp'), parts along dimension 0, may hold values from 1 to 22, 132 in all
- input_norm_gain: float32 [128], replicated, may hold values from 0.1 to 1.9
- input_norm_bias: float32 [128], replicated, may hold values from -3 to 3
- w_in: bfloat16 [128, 640], replicated, may hold values from -0.5 to 0.5
- output_norm_gain: float32 [128], replicated, may hold values from 0.1 to 1.9
- output_norm_bias: float32 [128], replicated, may hold values from -3 to 3
- w_out: bfloat16 [128, 128], replicated, may hold values from -0.5 to 0.5
Outputs:
- update: bfloat16 [352, 176, 128], P(('grp', 'row'), 'col'), parts along dimension 0
- pair_gradient: bfloat16 [352, 176, 128], P(('grp', 'row'), 'col'), parts along dimension 0
- grad_w_in: float32 [256, 640], P('grp'), parts along dimension 0
- grad_w_out: float32 [256, 128], P('grp'), parts along dimension 0
The draws below stay inside these ranges and needn't reach their ends.
There are 2 independent parts, one for each index of `grp`. The reference program is written for one: setup_inputs(seed, part) draws one part's arguments, and reference() takes and returns one part's arrays. A program takes and returns all parts, laid end to end along the dimension named above; an argument that names none is the same for every part. Nothing has to cross between parts.
Inputs may be any that keep to these rules, and one draw needn't show every extreme that they name: Chain slot c holds positions c * 22 to c * 22 + chain_lengths[c] - 1; the entries sum to 132 and one of them equals 22.
All inputs are finite; a program needn't handle non-finite values.
Results may differ from the reference program's by a relative error of at most 0.017.
Values may be sent and summed in bfloat16 or wider, within the bound.
No kernel may reach another device: no remote copies, remote signals or barrier semaphores. Data moves between devices by JAX's collectives and lax.ppermute only.
A program may use at most 192 MiB of HBM per device.

```python
import math
import jax
import jax.numpy as jnp
import numpy as np
from jax import lax

C = 128
H = 128
RT = 22
CHAINS = 8
RES = 176
SLOT = 22
PROJ = 640
N_ROW = 8


def block_levels(own_key, shape, pieces, smallest, high):
    level, own = 1.0, jax.random.fold_in(own_key, 6)
    for axis_at, shards_of in pieces:
        steps = jnp.exp(jax.random.uniform(jax.random.fold_in(own, axis_at), (shards_of,), jnp.float32, smallest / len(pieces), high / len(pieces)))
        level = level * jnp.repeat(steps, shape[axis_at] // shards_of).reshape([-1 if axis == axis_at else 1 for axis in range(len(shape))])
    return level


def length_profile(count, total, reach, lean):
    weights = [(1 << 20) // math.isqrt(grade ** lean) + 1 for grade in range(2, count + 1)]
    surplus, counts = total - reach - (count - 1), [1] * (count - 1)
    while surplus > 0:
        free = [i for i in range(count - 1) if counts[i] < reach]
        pool, remaining = sum([weights[i] for i in free]), surplus
        for i in free:
            more = min(reach - counts[i], max(1, remaining * weights[i] // pool), surplus)
            counts[i] = counts[i] + more
            surplus = surplus - more
    return np.array([reach] + counts)


def ragged_sizes(stream_key, count, total, most, skew):
    if count == 2:
        one = jax.random.randint(stream_key, (), max(1, total - most), min(most, total - 1) + 1)
        return jnp.stack([one, total - one])
    lengths = jnp.asarray(length_profile(count, total, most, skew), jnp.int32)
    pairs = (count - 1) // 2
    source_of, taker = lengths[1:1 + 2 * pairs:2], lengths[2:2 + 2 * pairs:2]
    margin = jnp.minimum(source_of - 1, most - taker)
    passed = jax.random.randint(jax.random.fold_in(stream_key, 1), (pairs,), 0, 1 << 20) % (margin + 1)
    lengths = lengths.at[1:1 + 2 * pairs:2].set(source_of - passed).at[2:2 + 2 * pairs:2].set(taker + passed)
    return lengths[jax.random.permutation(jax.random.fold_in(stream_key, 2), count)]


def centred(stream_key, dims, spread, most, split=(), held_as=jnp.bfloat16):
    values = spread * jax.random.normal(stream_key, dims, jnp.float32)
    if split:
        values = values * block_levels(stream_key, dims, split, -0.22, 0.18)
    return jnp.clip(values, -most, most).astype(held_as)


def setup_inputs(seed: int = 0, part: int = 0) -> dict:
    key_of = jax.random.split(jax.random.key(seed), 10)
    part_keys = jax.random.split(jax.random.fold_in(key_of[9], part), 10)
    return {
        "pair": centred(part_keys[0], (RES, RES, C), 1.0, 6.0, ((0, 8), (1, 2))),
        "cotangent": centred(part_keys[1], (RES, RES, C), 1.0, 6.0, ((0, 8), (1, 2))),
        "chain_lengths": ragged_sizes(part_keys[2], CHAINS, 3 * RES // 4, SLOT, 0).astype(jnp.int32),
        "input_norm_gain": jnp.clip(1.0 + 0.18 * jax.random.normal(key_of[3], (C,), jnp.float32), 0.1, 1.9),
        "input_norm_bias": centred(key_of[4], (C,), 0.5, 3.0, (), jnp.float32),
        "w_in": centred(key_of[5], (C, PROJ), C ** -0.5, 0.5),
        "output_norm_gain": jnp.clip(1.0 + 0.18 * jax.random.normal(key_of[6], (H,), jnp.float32), 0.1, 1.9),
        "output_norm_bias": centred(key_of[7], (H,), 0.5, 3.0, (), jnp.float32),
        "w_out": centred(key_of[8], (H, C), H ** -0.5, 0.5),
    }


eps = 1e-05

def layer_norm_forward(values, norm_gain, shift_bias):
    average_value = lax.optimization_barrier(jnp.mean(values, axis=-1, keepdims=True))
    centered_input = values - average_value
    inverse_deviation = lax.rsqrt(lax.optimization_barrier(jnp.mean(centered_input * centered_input, axis=-1, keepdims=True)) + eps)
    standardized_input = centered_input * inverse_deviation
    return (standardized_input * norm_gain + shift_bias, standardized_input, inverse_deviation)

def layer_norm_backward(output_gradient, standardized_input, inverse_deviation, norm_gain):
    scaled_output = output_gradient * norm_gain
    first_operand = lax.optimization_barrier(jnp.mean(scaled_output, axis=-1, keepdims=True))
    second_operand = lax.optimization_barrier(jnp.mean(scaled_output * standardized_input, axis=-1, keepdims=True))
    return inverse_deviation * (scaled_output - first_operand - standardized_input * second_operand)

def residue_present():
    positions = jnp.arange(RES, dtype=jnp.int32)
    chain_ids = positions // SLOT
    return (positions - chain_ids * SLOT, chain_ids)

def reference(pair, cotangent, chain_lengths, input_norm_gain, input_norm_bias, w_in, output_norm_gain, output_norm_bias, w_out):
    offsets, chain_ids = residue_present()
    present = (offsets < chain_lengths[chain_ids]).astype(jnp.float32)
    pair_mask = present[:, None, None] * present[None, :, None]
    normalized_float32, standardized_pair, input_inverse_deviation = layer_norm_forward(pair.astype(jnp.float32), input_norm_gain, input_norm_bias)
    normed = normalized_float32.astype(jnp.bfloat16)
    normed_flat = normed.reshape(RES * RES, C)
    proj = jnp.dot(normed_flat, w_in, preferred_element_type=jnp.float32).reshape(RES, RES, PROJ)
    sig_left = jax.nn.sigmoid(proj[..., 0:H])
    val_left = proj[..., H:2 * H]
    sig_right = jax.nn.sigmoid(proj[..., 2 * H:3 * H])
    val_right = proj[..., 3 * H:4 * H]
    gate = jax.nn.sigmoid(proj[..., 4 * H:])
    left_proj = (pair_mask * sig_left * val_left).astype(jnp.bfloat16)
    right_proj = (pair_mask * sig_right * val_right).astype(jnp.bfloat16)
    triangle_product = jnp.einsum('ikh,jkh->ijh', left_proj.astype(jnp.float32), right_proj.astype(jnp.float32))
    triangle_output, standardized_triangle, triangle_inverse_deviation = layer_norm_forward(triangle_product, output_norm_gain, output_norm_bias)
    tri_norm = triangle_output.astype(jnp.bfloat16)
    tri_flat = tri_norm.reshape(RES * RES, H)
    projected = jnp.dot(tri_flat, w_out, preferred_element_type=jnp.float32).reshape(RES, RES, C)
    update = (gate * projected).astype(jnp.bfloat16)
    grad_up = cotangent.astype(jnp.float32)
    grad_proj_out = (grad_up * gate).astype(jnp.bfloat16)
    grad_gate = grad_up * projected * gate * (1.0 - gate)
    grad_flat = grad_proj_out.reshape(RES * RES, C)
    grad_w_out = lax.dot_general(tri_flat, grad_flat, (((0,), (0,)), ((), ())), preferred_element_type=jnp.float32)
    triangle_norm_gradient = lax.dot_general(grad_flat, w_out, (((1,), (1,)), ((), ())), preferred_element_type=jnp.float32).reshape(RES, RES, H)
    triangle_gradient = layer_norm_backward(triangle_norm_gradient, standardized_triangle, triangle_inverse_deviation, output_norm_gain).astype(jnp.bfloat16)
    grad_left = jnp.einsum('ijh,jkh->ikh', triangle_gradient.astype(jnp.float32), right_proj.astype(jnp.float32))

    def accumulate(total, blocks):
        grad_block, left_block = blocks
        partial_sum = jnp.einsum('ijh,ikh->jkh', grad_block.astype(jnp.float32), left_block.astype(jnp.float32))
        rounded = lax.optimization_barrier(partial_sum.astype(jnp.bfloat16))
        return (total + rounded.astype(jnp.float32), None)
    grad_right, _ = lax.scan(accumulate, jnp.zeros((RES, RES, H), jnp.float32), (triangle_gradient.reshape(N_ROW, RT, RES, H), left_proj.reshape(N_ROW, RT, RES, H)))
    grad_proj = jnp.concatenate([grad_left * pair_mask * val_left * sig_left * (1.0 - sig_left), grad_left * pair_mask * sig_left, grad_right * pair_mask * val_right * sig_right * (1.0 - sig_right), grad_right * pair_mask * sig_right, grad_gate], axis=-1).astype(jnp.bfloat16)
    proj_flat = grad_proj.reshape(RES * RES, PROJ)
    grad_w_in = lax.dot_general(normed_flat, proj_flat, (((0,), (0,)), ((), ())), preferred_element_type=jnp.float32)
    normalized_gradient = lax.dot_general(proj_flat, w_in, (((1,), (1,)), ((), ())), preferred_element_type=jnp.float32).reshape(RES, RES, C)
    pair_gradient = layer_norm_backward(normalized_gradient, standardized_pair, input_inverse_deviation, input_norm_gain).astype(jnp.bfloat16)
    return (update, pair_gradient, grad_w_in, grad_w_out)
```

```python
import jax
import jax.numpy as jnp
from jax import lax
from jax.sharding import PartitionSpec as P

eps = 1e-05


def layer_norm_forward(values, norm_gain, shift_bias):
    average_value = jnp.mean(values, axis=-1, keepdims=True)
    centered_input = values - average_value
    inverse_deviation = lax.rsqrt(
        jnp.mean(centered_input * centered_input, axis=-1, keepdims=True) + eps
    )
    standardized_input = centered_input * inverse_deviation
    return (standardized_input * norm_gain + shift_bias, standardized_input, inverse_deviation)


def layer_norm_backward(output_gradient, standardized_input, inverse_deviation, norm_gain):
    scaled_output = output_gradient * norm_gain
    first_operand = jnp.mean(scaled_output, axis=-1, keepdims=True)
    second_operand = jnp.mean(scaled_output * standardized_input, axis=-1, keepdims=True)
    return inverse_deviation * (scaled_output - first_operand - standardized_input * second_operand)


def present_rows(positions, chain_lengths, slot_size):
    chain_ids = positions // slot_size
    offsets = positions - chain_ids * slot_size
    slots = jnp.arange(chain_lengths.shape[0], dtype=jnp.int32)
    lengths = jnp.sum(
        jnp.where(chain_ids[:, None] == slots[None, :], chain_lengths[None, :], 0), axis=1
    )
    return (offsets < lengths).astype(jnp.float32)


def ring_order(row_count):
    if row_count == 8:
        return [0, 2, 4, 6, 7, 5, 3, 1]
    return list(range(row_count))


def swap_col(x):
    return lax.ppermute(x, "col", [(0, 1), (1, 0)])


def sum_all(x, row_count):
    def add(a, b):
        return (a.astype(jnp.float32) + b.astype(jnp.float32)).astype(jnp.bfloat16)

    x = add(x, swap_col(x))
    step = 1
    while step < row_count:
        x = add(x, lax.ppermute(x, "row", [(r, r ^ step) for r in range(row_count)]))
        step *= 2
    return x


def ring_gather(block, order, place):
    n = len(order)
    forward = [(order[p], order[(p + 1) % n]) for p in range(n)]
    backward = [(order[p], order[(p - 1) % n]) for p in range(n)]
    rows = block.shape[0]
    whole = jnp.zeros((n * rows,) + block.shape[1:], block.dtype)
    ring = jnp.asarray(order, jnp.int32)

    def put(whole, part, position, offset):
        start = ring[position % n] * rows + offset
        return lax.dynamic_update_slice_in_dim(whole, part, start, 0)

    whole = put(whole, block, place, 0)
    ahead = behind = block
    cut = rows // 2
    for step in range(1, n // 2):
        ahead = lax.ppermute(ahead, "row", forward)
        behind = lax.ppermute(behind, "row", backward)
        whole = put(whole, ahead, place - step, 0)
        whole = put(whole, behind, place + step, 0)
    ahead = lax.ppermute(ahead[:cut], "row", forward)
    behind = lax.ppermute(behind[cut:], "row", backward)
    whole = put(whole, ahead, place + n // 2, 0)
    whole = put(whole, behind, place + n // 2, cut)
    return whole


def ring_scatter(part_of, order, place, rows):
    n = len(order)
    forward = [(order[p], order[(p + 1) % n]) for p in range(n)]
    backward = [(order[p], order[(p - 1) % n]) for p in range(n)]
    cut = rows // 2
    far = part_of(place + n // 2).astype(jnp.bfloat16)
    up = lax.ppermute(far[:cut], "row", forward).astype(jnp.float32)
    down = lax.ppermute(far[cut:], "row", backward).astype(jnp.float32)
    for step in range(n // 2 - 1, 0, -1):
        up_part = part_of(place + step)
        down_part = part_of(place - step)
        if up.shape[0] != rows:
            up = jnp.concatenate([up_part[:cut] + up, up_part[cut:]], axis=0)
            down = jnp.concatenate([down_part[:cut], down_part[cut:] + down], axis=0)
        else:
            up, down = up_part + up, down_part + down
        up = lax.ppermute(up.astype(jnp.bfloat16), "row", forward).astype(jnp.float32)
        down = lax.ppermute(down.astype(jnp.bfloat16), "row", backward).astype(jnp.float32)
    return part_of(place) + up + down


def shards(
    pair,
    cotangent,
    chain_lengths,
    input_norm_gain,
    input_norm_bias,
    w_in,
    output_norm_gain,
    output_norm_bias,
    w_out,
):
    rows_here = pair.shape[0]
    half = pair.shape[1]
    channels = pair.shape[2]
    hidden = w_out.shape[0]
    row_count = lax.axis_size("row")
    residues = rows_here * row_count
    slot_size = residues // chain_lengths.shape[0]
    order = ring_order(row_count)
    inverse = [order.index(r) for r in range(row_count)]
    place = jnp.asarray(inverse, jnp.int32)[lax.axis_index("row")] + row_count
    ring = jnp.asarray(order, jnp.int32)
    col = lax.axis_index("col")
    f32 = jnp.float32
    bf16 = jnp.bfloat16

    def dot(a, b, ca, cb):
        return lax.dot_general(a, b, (((ca,), (cb,)), ((), ())), preferred_element_type=f32)

    def shaped(x):
        return x.reshape(rows_here, half, -1)

    row_ids = lax.axis_index("row") * rows_here + jnp.arange(rows_here, dtype=jnp.int32)
    col_ids = col * half + jnp.arange(half, dtype=jnp.int32)
    pair_mask = (
        present_rows(row_ids, chain_lengths, slot_size)[:, None, None]
        * present_rows(col_ids, chain_lengths, slot_size)[None, :, None]
    )
    w_left, w_right = w_in[:, : 2 * hidden], w_in[:, 2 * hidden : 4 * hidden]
    w_gate = w_in[:, 4 * hidden :]
    normalized_float32, standardized_pair, input_inverse_deviation = layer_norm_forward(
        pair.astype(f32), input_norm_gain, input_norm_bias
    )
    normed_flat = normalized_float32.astype(bf16).reshape(rows_here * half, channels)
    proj_right = shaped(dot(normed_flat, w_right, 1, 0))
    sig_right = jax.nn.sigmoid(proj_right[..., :hidden])
    val_right = proj_right[..., hidden:]
    right_proj = (pair_mask * sig_right * val_right).astype(bf16)
    right_all = ring_gather(right_proj, order, place)

    proj_left = shaped(dot(normed_flat, w_left, 1, 0))
    sig_left = jax.nn.sigmoid(proj_left[..., :hidden])
    val_left = proj_left[..., hidden:]
    left_proj = (pair_mask * sig_left * val_left).astype(bf16)
    gate = jax.nn.sigmoid(shaped(dot(normed_flat, w_gate, 1, 0)))
    grad_up = cotangent.astype(f32)
    grad_proj_out = (grad_up * gate).astype(bf16)
    grad_flat = grad_proj_out.reshape(rows_here * half, channels)

    other_out = swap_col(grad_proj_out)
    grad_out_all = jnp.where(
        col == 0,
        jnp.concatenate([grad_proj_out, other_out], axis=1),
        jnp.concatenate([other_out, grad_proj_out], axis=1),
    )
    triangle_norm_gradient = dot(
        grad_out_all.reshape(rows_here * 2 * half, channels), w_out, 1, 1
    ).reshape(rows_here, 2 * half, hidden)

    partial_tri = jnp.einsum(
        "ikh,jkh->ijh", left_proj, right_all, preferred_element_type=f32
    ).astype(bf16)
    triangle_product = partial_tri.astype(f32) + swap_col(partial_tri).astype(f32)
    triangle_output, standardized_triangle, triangle_inverse_deviation = layer_norm_forward(
        triangle_product, output_norm_gain, output_norm_bias
    )
    triangle_gradient = layer_norm_backward(
        triangle_norm_gradient, standardized_triangle, triangle_inverse_deviation, output_norm_gain
    ).astype(bf16)

    grad_right_all = jnp.einsum(
        "ijh,ikh->jkh", triangle_gradient, left_proj, preferred_element_type=f32
    ).astype(bf16)

    def part_of(position):
        start = ring[position % row_count] * rows_here
        return lax.dynamic_slice_in_dim(grad_right_all, start, rows_here, 0).astype(f32)

    grad_right = ring_scatter(part_of, order, place, rows_here)

    tri_norm = lax.dynamic_slice_in_dim(triangle_output, col * half, half, 1).astype(bf16)
    tri_flat = tri_norm.reshape(rows_here * half, hidden)
    projected = shaped(dot(tri_flat, w_out, 1, 0))
    update = (gate * projected).astype(bf16)
    grad_gate = (grad_up * projected * gate * (1.0 - gate)).astype(bf16)
    local_w_out = dot(tri_flat, grad_flat, 0, 0)
    grad_left = jnp.einsum("ijh,jkh->ikh", triangle_gradient, right_all, preferred_element_type=f32)
    early = jnp.concatenate(
        [
            grad_left * pair_mask * val_left * sig_left * (1.0 - sig_left),
            grad_left * pair_mask * sig_left,
        ],
        axis=-1,
    ).astype(bf16)
    early_flat = jnp.concatenate([early, grad_gate], axis=-1).reshape(rows_here * half, -1)
    w_early = jnp.concatenate([w_left, w_gate], axis=1)
    local_early = dot(normed_flat, early_flat, 0, 0)
    summed_early = sum_all(
        jnp.concatenate([local_early, local_w_out], axis=1).astype(bf16), row_count
    ).astype(f32)
    gradient_early = dot(early_flat, w_early, 1, 1)

    late_flat = (
        jnp.concatenate(
            [
                grad_right * pair_mask * val_right * sig_right * (1.0 - sig_right),
                grad_right * pair_mask * sig_right,
            ],
            axis=-1,
        )
        .astype(bf16)
        .reshape(rows_here * half, -1)
    )
    summed_late = sum_all(dot(normed_flat, late_flat, 0, 0).astype(bf16), row_count).astype(f32)
    normalized_gradient = shaped(gradient_early + dot(late_flat, w_right, 1, 1))
    pair_gradient = layer_norm_backward(
        normalized_gradient, standardized_pair, input_inverse_deviation, input_norm_gain
    ).astype(bf16)
    grad_w_in = jnp.concatenate(
        [summed_early[:, : 2 * hidden], summed_late, summed_early[:, 2 * hidden : 3 * hidden]],
        axis=1,
    )
    grad_w_out = summed_early[:, 3 * hidden :]
    return (update, pair_gradient, grad_w_in, grad_w_out)


def solution(mesh):
    placed = (
        P(("grp", "row"), "col", None),
        P(("grp", "row"), "col", None),
        P("grp"),
        P(),
        P(),
        P(),
        P(),
        P(),
        P(),
    )
    return jax.shard_map(
        shards,
        mesh=mesh,
        in_specs=placed,
        out_specs=(
            P(("grp", "row"), "col", None),
            P(("grp", "row"), "col", None),
            P("grp", None),
            P("grp", None),
        ),
        check_vma=False,
    )
```

```python
import functools

import jax
import jax.numpy as jnp
from jax import lax
from jax.experimental import pallas as pl
from jax.experimental.pallas import tpu as pltpu
from jax.sharding import PartitionSpec as P

eps = 1e-05
f32 = jnp.float32
bf16 = jnp.bfloat16
VMEM = pl.BlockSpec(memory_space=pltpu.VMEM)
LIMIT = 48 * 1024 * 1024


def layer_norm_forward(values, norm_gain, shift_bias):
    average_value = jnp.mean(values, axis=-1, keepdims=True)
    centered_input = values - average_value
    inverse_deviation = lax.rsqrt(
        jnp.mean(centered_input * centered_input, axis=-1, keepdims=True) + eps
    )
    standardized_input = centered_input * inverse_deviation
    return (standardized_input * norm_gain + shift_bias, standardized_input, inverse_deviation)


def layer_norm_backward(output_gradient, standardized_input, inverse_deviation, norm_gain):
    scaled_output = output_gradient * norm_gain
    first_operand = jnp.mean(scaled_output, axis=-1, keepdims=True)
    second_operand = jnp.mean(scaled_output * standardized_input, axis=-1, keepdims=True)
    return inverse_deviation * (scaled_output - first_operand - standardized_input * second_operand)


def present_rows(positions, chain_lengths, slot_size):
    chain_ids = positions // slot_size
    offsets = positions - chain_ids * slot_size
    slots = jnp.arange(chain_lengths.shape[0], dtype=jnp.int32)
    lengths = jnp.sum(
        jnp.where(chain_ids[:, None] == slots[None, :], chain_lengths[None, :], 0), axis=1
    )
    return (offsets < lengths).astype(f32)


def ring_order(row_count):
    if row_count == 8:
        return [0, 2, 4, 6, 7, 5, 3, 1]
    return list(range(row_count))


def swap_col(x):
    return lax.ppermute(x, "col", [(0, 1), (1, 0)])


def sum_all(x, row_count):
    def add(a, b):
        return (a.astype(f32) + b.astype(f32)).astype(bf16)

    x = add(x, swap_col(x))
    step = 1
    while step < row_count:
        x = add(x, lax.ppermute(x, "row", [(r, r ^ step) for r in range(row_count)]))
        step *= 2
    return x


def cost(microseconds):
    return pl.CostEstimate(
        flops=int(microseconds * 1.1e9), bytes_accessed=1 << 20, transcendentals=0
    )


def params():
    return pltpu.CompilerParams(vmem_limit_bytes=LIMIT)


def triangle_kernel(count, left_ref, *refs):
    rights, out_ref, wide, rows = refs[:count], refs[count], refs[count + 1], refs[count + 2]
    here, short = left_ref.shape[0], rights[0].shape[0]
    rows[...] = jnp.zeros_like(rows)
    for half in range(count):
        wide[...] = rights[half][...].astype(f32)

        def body(i, carry, half=half):
            left = left_ref[i]
            for j in range(short):
                rows[pl.ds(j, 1), :] = jnp.sum(left * wide[j], axis=0, keepdims=True)
            out_ref[half, i] = rows[...].astype(bf16)
            return carry

        lax.fori_loop(0, here, body, 0)


def triangle(left, rights, padded):
    count, here = len(rights), left.shape[0]
    return pl.pallas_call(
        functools.partial(triangle_kernel, count),
        out_shape=jax.ShapeDtypeStruct((count, here, padded, left.shape[2]), bf16),
        in_specs=[VMEM] * (count + 1),
        out_specs=VMEM,
        scratch_shapes=[
            pltpu.VMEM(rights[0].shape, f32),
            pltpu.VMEM((padded, left.shape[2]), f32),
        ],
        compiler_params=params(),
        cost_estimate=cost(1.0 * count),
        name="triangle",
    )(left, *rights)


def triangle_gradient_kernel(where, mine, other, grads, w_out, gain, out_ref):
    here, padded, hidden = mine.shape[1:]
    flat = (here * padded, hidden)
    total = (mine[0].astype(f32) + other[0].astype(f32)).reshape(flat)
    average = jnp.mean(total, axis=-1, keepdims=True)
    centered = total - average
    inverse = lax.rsqrt(jnp.mean(centered * centered, axis=-1, keepdims=True) + eps)
    standard = centered * inverse
    grad_norm = lax.dot_general(
        grads[0].reshape(flat), w_out[...], (((1,), (1,)), ((), ())), preferred_element_type=f32
    )
    result = layer_norm_backward(grad_norm, standard, inverse, gain[...])
    out_ref[0] = result.astype(bf16).reshape(here, padded, hidden)


def triangle_gradient(where, mine, other, grads, w_out, gain):
    count, here, padded, hidden = mine.shape
    block = (1, here, padded, hidden)
    return pl.pallas_call(
        triangle_gradient_kernel,
        out_shape=jax.ShapeDtypeStruct(mine.shape, bf16),
        grid_spec=pltpu.PrefetchScalarGridSpec(
            num_scalar_prefetch=1,
            grid=(count,),
            in_specs=[
                pl.BlockSpec(block, lambda s, at: (s, 0, 0, 0)),
                pl.BlockSpec(block, lambda s, at: (s, 0, 0, 0)),
                pl.BlockSpec(block, lambda s, at: (at[s], 0, 0, 0)),
                pl.BlockSpec(w_out.shape, lambda s, at: (0, 0)),
                pl.BlockSpec(gain.shape, lambda s, at: (0, 0)),
            ],
            out_specs=pl.BlockSpec(block, lambda s, at: (s, 0, 0, 0)),
        ),
        compiler_params=params(),
        cost_estimate=cost(0.8 * count),
        name="triangle_gradient",
    )(where, mine, other, grads, w_out, gain)


def hop_kernel(count, carried, left_ref, *refs):
    grads, refs = refs[:count], refs[count:]
    arrived, refs = refs[: count * carried], refs[count * carried :]
    outs, wide = refs[:count], refs[count]
    here, short = left_ref.shape[0], outs[0].shape[0]
    for half in range(count):
        wide[...] = grads[half][0].astype(f32)

        def body(j, carry, half=half):
            if carried:
                total = arrived[half][j].astype(f32)
                for more in range(1, carried):
                    total += arrived[half + more * count][j].astype(f32)
            else:
                total = jnp.zeros(left_ref.shape[1:], f32)
            for i in range(here):
                total += wide[i, pl.ds(j, 1), :] * left_ref[i]
            outs[half][j] = total.astype(outs[half].dtype)
            return carry

        lax.fori_loop(0, short, body, 0)


def hop(left, grads, picks, arrived, short, dtype=bf16):
    here, half, hidden = left.shape
    count = len(grads)
    carried = len(arrived) // count
    whole = pl.BlockSpec(left.shape, lambda s: (0, 0, 0))
    part = pl.BlockSpec((short, half, hidden), lambda s: (0, 0, 0))

    def picked(g, pick):
        return pl.BlockSpec((1,) + g.shape[1:], lambda s: (pick, 0, 0, 0))

    return pl.pallas_call(
        functools.partial(hop_kernel, count, carried),
        grid=(1,),
        out_shape=[jax.ShapeDtypeStruct((short, half, hidden), dtype)] * count,
        in_specs=[whole]
        + [picked(g, pick) for g, pick in zip(grads, picks)]
        + [part] * len(arrived),
        out_specs=[part] * count,
        scratch_shapes=[pltpu.VMEM(grads[0].shape[1:], f32)],
        compiler_params=params(),
        cost_estimate=cost(1.0 * count),
        name="scatter_hop",
    )(left, *grads, *arrived)


def left_kernel(count, carried, grads, *refs):
    rights, refs = refs[:count], refs[count:]
    before, (out_ref, wide_right, wide_grad) = refs[:carried], refs[carried:]
    short = rights[0].shape[0]
    for half in range(count):
        wide_right[half] = rights[half][...].astype(f32)
        wide_grad[half] = grads[half].astype(f32)

    def rows(i, carry):
        def add(s, total):
            for j in range(short):
                total += wide_grad[s, i, pl.ds(j, 1), :] * wide_right[s, j]
            return total

        start = before[0][i] if carried else jnp.zeros(out_ref.shape[1:], f32)
        out_ref[i] = lax.fori_loop(0, count, add, start)
        return carry

    lax.fori_loop(0, out_ref.shape[0], rows, 0)


def left_gradient(grads, rights, before):
    count, here = grads.shape[:2]
    short, half, hidden = rights[0].shape
    return pl.pallas_call(
        functools.partial(left_kernel, count, len(before)),
        out_shape=jax.ShapeDtypeStruct((here, half, hidden), f32),
        in_specs=[VMEM] * (1 + count + len(before)),
        out_specs=VMEM,
        scratch_shapes=[
            pltpu.VMEM((count, short, half, hidden), f32),
            pltpu.VMEM(grads.shape, f32),
        ],
        compiler_params=params(),
        cost_estimate=cost(0.8 * count),
        name="left_gradient",
    )(grads, *rights, *before)


def shards(
    pair,
    cotangent,
    chain_lengths,
    input_norm_gain,
    input_norm_bias,
    w_in,
    output_norm_gain,
    output_norm_bias,
    w_out,
):
    rows_here = pair.shape[0]
    half = pair.shape[1]
    channels = pair.shape[2]
    hidden = w_out.shape[0]
    row_count = lax.axis_size("row")
    residues = rows_here * row_count
    slot_size = residues // chain_lengths.shape[0]
    order = ring_order(row_count)
    inverse = [order.index(r) for r in range(row_count)]
    place = jnp.asarray(inverse, jnp.int32)[lax.axis_index("row")]
    ring = jnp.asarray(order, jnp.int32)
    col = lax.axis_index("col")
    short = rows_here // 2
    padded = (short + 15) // 16 * 16
    forward = [(order[p], order[(p + 1) % row_count]) for p in range(row_count)]
    backward = [(order[p], order[(p - 1) % row_count]) for p in range(row_count)]

    def ahead(x):
        return lax.ppermute(x, "row", forward)

    def behind(x):
        return lax.ppermute(x, "row", backward)

    def dot(a, b, ca, cb):
        return lax.dot_general(a, b, (((ca,), (cb,)), ((), ())), preferred_element_type=f32)

    def shaped(x):
        return x.reshape(rows_here, half, -1)

    row_ids = lax.axis_index("row") * rows_here + jnp.arange(rows_here, dtype=jnp.int32)
    col_ids = col * half + jnp.arange(half, dtype=jnp.int32)
    pair_mask = (
        present_rows(row_ids, chain_lengths, slot_size)[:, None, None]
        * present_rows(col_ids, chain_lengths, slot_size)[None, :, None]
    )
    w_left, w_right = w_in[:, : 2 * hidden], w_in[:, 2 * hidden : 4 * hidden]
    w_gate = w_in[:, 4 * hidden :]
    normalized_float32, standardized_pair, input_inverse_deviation = layer_norm_forward(
        pair.astype(f32), input_norm_gain, input_norm_bias
    )
    normed_flat = normalized_float32.astype(bf16).reshape(rows_here * half, channels)
    proj_right = shaped(dot(normed_flat, w_right, 1, 0))
    sig_right = jax.nn.sigmoid(proj_right[..., :hidden])
    val_right = proj_right[..., hidden:]
    right_proj = (pair_mask * sig_right * val_right).astype(bf16)

    own = [right_proj[:short], right_proj[short:]]
    hops = row_count // 2
    chain1, chain2 = [], []
    a, b, c, d = own[0], own[1], own[1], own[0]
    for step in range(hops):
        a, b = ahead(a), behind(b)
        chain1 += [a, b]
        if step < hops - 1:
            c, d = ahead(c), behind(d)
            chain2 += [c, d]

    def half_index(offset, letter):
        return ring[(place + offset + row_count) % row_count] * 2 + letter

    early_hops = hops // 2
    groups = [own + chain1[: 2 * early_hops], chain1[2 * early_hops :], chain2]
    index1 = [half_index(sign * s, x) for s in range(1, hops + 1) for sign, x in ((-1, 0), (1, 1))]
    index2 = [half_index(sign * s, x) for s in range(1, hops) for sign, x in ((-1, 1), (1, 0))]
    indices = [
        [half_index(0, 0), half_index(0, 1)] + index1[: 2 * early_hops],
        index1[2 * early_hops :],
        index2,
    ]

    proj_left = shaped(dot(normed_flat, w_left, 1, 0))
    sig_left = jax.nn.sigmoid(proj_left[..., :hidden])
    val_left = proj_left[..., hidden:]
    left_proj = (pair_mask * sig_left * val_left).astype(bf16).astype(f32)
    gate = jax.nn.sigmoid(shaped(dot(normed_flat, w_gate, 1, 0)))
    grad_up = cotangent.astype(f32)
    grad_proj_out = (grad_up * gate).astype(bf16)
    grad_flat = grad_proj_out.reshape(rows_here * half, channels)

    mine_out = jnp.pad(
        grad_proj_out.reshape(rows_here, row_count, short, channels).transpose(1, 0, 2, 3),
        ((0, 0), (0, 0), (0, padded - short), (0, 0)),
    )
    out_halves = jnp.concatenate([mine_out, swap_col(mine_out)], axis=0)
    gain = output_norm_gain.reshape(1, hidden)

    def local_index(i):
        return (i // row_count) ^ col, i % row_count

    sums, others, grads = [], [], []
    for rights, index in zip(groups, indices):
        partial = triangle(left_proj, rights, padded)
        other = swap_col(partial)
        at = jnp.stack([x * row_count + y for x, y in map(local_index, index)]).astype(jnp.int32)
        sums.append(partial)
        others.append(other)
        grads.append(triangle_gradient(at, partial, other, out_halves, w_out, gain))

    def group1(s):
        at = 2 * (s - 1)
        if s <= early_hops:
            return [grads[0], grads[0]], [at + 2, at + 3]
        at -= 2 * early_hops
        return [grads[1], grads[1]], [at, at + 1]

    arrived1, arrived2 = [], []
    for s in range(hops, 0, -1):
        g, picks = group1(s)
        x, y = hop(left_proj, g, picks, arrived1, short)
        arrived1 = [behind(x), ahead(y)]
    for s in range(hops - 1, 0, -1):
        x, y = hop(left_proj, [grads[2]] * 2, [2 * s - 2, 2 * s - 1], arrived2, short)
        arrived2 = [behind(x), ahead(y)]
    arrived2 = [arrived2[1], arrived2[0]]

    tri_halves = jnp.concatenate(sums, axis=0).astype(f32) + jnp.concatenate(
        others, axis=0
    ).astype(f32)
    flat_index = jnp.stack(sum(indices, []))
    wanted = col * row_count + jnp.arange(row_count, dtype=jnp.int32)
    slot = jnp.argmax(flat_index[None, :] == wanted[:, None], axis=1)
    triangle_product = (
        tri_halves[slot][:, :, :short].transpose(1, 0, 2, 3).reshape(rows_here, half, hidden)
    )
    triangle_output, _, _ = layer_norm_forward(
        triangle_product, output_norm_gain, output_norm_bias
    )
    tri_flat = triangle_output.astype(bf16).reshape(rows_here * half, hidden)
    projected = shaped(dot(tri_flat, w_out, 1, 0))
    update = (gate * projected).astype(bf16)
    grad_gate = (grad_up * projected * gate * (1.0 - gate)).astype(bf16)
    local_w_out = dot(tri_flat, grad_flat, 0, 0)

    before = []
    for g, rights in zip(grads, groups):
        before = [left_gradient(g, rights, before)]
    grad_left = before[0]
    early = jnp.concatenate(
        [
            grad_left * pair_mask * val_left * sig_left * (1.0 - sig_left),
            grad_left * pair_mask * sig_left,
        ],
        axis=-1,
    ).astype(bf16)
    early_flat = jnp.concatenate([early, grad_gate], axis=-1).reshape(rows_here * half, -1)
    w_early = jnp.concatenate([w_left, w_gate], axis=1)
    local_early = dot(normed_flat, early_flat, 0, 0)
    summed_early = sum_all(
        jnp.concatenate([local_early, local_w_out], axis=1).astype(bf16), row_count
    ).astype(f32)
    gradient_early = dot(early_flat, w_early, 1, 1)

    x, y = hop(left_proj, [grads[0]] * 2, [0, 1], arrived1 + arrived2, short, f32)
    grad_right = jnp.concatenate([x, y], axis=0)
    late_flat = (
        jnp.concatenate(
            [
                grad_right * pair_mask * val_right * sig_right * (1.0 - sig_right),
                grad_right * pair_mask * sig_right,
            ],
            axis=-1,
        )
        .astype(bf16)
        .reshape(rows_here * half, -1)
    )
    summed_late = sum_all(dot(normed_flat, late_flat, 0, 0).astype(bf16), row_count).astype(f32)
    normalized_gradient = shaped(gradient_early + dot(late_flat, w_right, 1, 1))
    pair_gradient = layer_norm_backward(
        normalized_gradient, standardized_pair, input_inverse_deviation, input_norm_gain
    ).astype(bf16)
    grad_w_in = jnp.concatenate(
        [summed_early[:, : 2 * hidden], summed_late, summed_early[:, 2 * hidden : 3 * hidden]],
        axis=1,
    )
    grad_w_out = summed_early[:, 3 * hidden :]
    return (update, pair_gradient, grad_w_in, grad_w_out)


def solution(mesh):
    placed = (
        P(("grp", "row"), "col", None),
        P(("grp", "row"), "col", None),
        P("grp"),
        P(),
        P(),
        P(),
        P(),
        P(),
        P(),
    )
    return jax.shard_map(
        shards,
        mesh=mesh,
        in_specs=placed,
        out_specs=(
            P(("grp", "row"), "col", None),
            P(("grp", "row"), "col", None),
            P("grp", None),
            P("grp", None),
        ),
        check_vma=False,
    )
```

```python
import functools

import jax
import jax.numpy as jnp
from jax import lax
from jax.experimental import pallas as pl
from jax.experimental.pallas import tpu as pltpu
from jax.sharding import PartitionSpec as P

eps = 1e-05
f32 = jnp.float32
bf16 = jnp.bfloat16
VMEM = pl.BlockSpec(memory_space=pltpu.VMEM)
SMEM = pl.BlockSpec(memory_space=pltpu.SMEM)
ANY = pl.BlockSpec(memory_space=pl.ANY)
MIB = 1 << 20


def layer_norm_backward(output_gradient, standardized_input, inverse_deviation, norm_gain):
    scaled_output = output_gradient * norm_gain
    first_operand = jnp.mean(scaled_output, axis=-1, keepdims=True)
    second_operand = jnp.mean(scaled_output * standardized_input, axis=-1, keepdims=True)
    return inverse_deviation * (scaled_output - first_operand - standardized_input * second_operand)


def standardize(values):
    centered = values - jnp.mean(values, axis=-1, keepdims=True)
    inverse = lax.rsqrt(jnp.mean(centered * centered, axis=-1, keepdims=True) + eps)
    return centered * inverse, inverse


def dot(a, b, ca, cb):
    return lax.dot_general(a, b, (((ca,), (cb,)), ((), ())), preferred_element_type=f32)


def ring_order(row_count):
    if row_count == 8:
        return [0, 2, 4, 6, 7, 5, 3, 1]
    return list(range(row_count))


def swap_col(x):
    return lax.ppermute(x, "col", [(0, 1), (1, 0)])


def sum_all(x, row_count):
    def add(a, b):
        return (a.astype(f32) + b.astype(f32)).astype(bf16)

    x = add(x, swap_col(x))
    step = 1
    while step < row_count:
        x = add(x, lax.ppermute(x, "row", [(r, r ^ step) for r in range(row_count)]))
        step *= 2
    return x


def call(kernel, name, microseconds, args, specs, outs, scratch=(), after=()):
    held = sum(a.size * a.dtype.itemsize for a, s in zip(args, specs) if s is VMEM)
    held += sum(int(o.size) * o.dtype.itemsize for o in outs)
    held += sum(int(s.inner_aval.size) * 4 for s in scratch)

    def body(*refs):
        kernel(*refs[: len(args)], *refs[len(args) + len(after) :])

    return pl.pallas_call(
        body,
        out_shape=list(outs),
        in_specs=list(specs) + [ANY] * len(after),
        out_specs=[VMEM] * len(outs),
        scratch_shapes=list(scratch),
        compiler_params=pltpu.CompilerParams(vmem_limit_bytes=min(56 * MIB, held * 5 // 4 + 6 * MIB)),
        cost_estimate=pl.CostEstimate(
            flops=int(microseconds * 1.1e9), bytes_accessed=MIB, transcendentals=0
        ),
        name=name,
    )(*args, *after)


def shape_of(dims, dtype):
    return jax.ShapeDtypeStruct(dims, dtype)


def present_row(lengths, slot, position):
    return (position % slot < lengths[position // slot]).astype(f32)


def present_columns(lengths, slot, half):
    at = lax.axis_index("col") * half + lax.broadcasted_iota(jnp.int32, (half, 128), 0)
    chain = at // slot
    held = jnp.zeros((half, 128), jnp.int32)
    for c in range(lengths.shape[0]):
        held = jnp.where(chain == c, lengths[c], held)
    return (at - chain * slot < held).astype(f32)


def first_row(here):
    return lax.axis_index("row") * here


def input_kernel(slot, lengths, pair, gain, bias, w, right_a, right_b, normed, mask):
    here, half, hidden = pair.shape
    short = here // 2
    mask[...] = present_columns(lengths, slot, half)

    def body(t, carry):
        for out, i in ((right_a, t), (right_b, t + short)):
            standard, _ = standardize(pair[i].astype(f32))
            values = (standard * gain[...] + bias[...]).astype(bf16)
            normed[i] = values
            proj = dot(values, w[...], 1, 0)
            shown = mask[...] * present_row(lengths, slot, first_row(here) + i)
            gated = jax.nn.sigmoid(proj[:, :hidden]) * proj[:, hidden:]
            out[t] = (shown * gated).astype(bf16)
        return carry

    lax.fori_loop(0, short, body, 0)


def left_kernel(slot, lengths, normed, cotangent, w, left, outs, mask):
    here, half, hidden = normed.shape
    halves, _, padded, _ = outs.shape
    short = half // halves
    mask[...] = present_columns(lengths, slot, half)

    def body(i, carry):
        proj = dot(normed[i], w[...], 1, 0)
        shown = mask[...] * present_row(lengths, slot, first_row(here) + i)
        gated = shown * jax.nn.sigmoid(proj[:, :hidden]) * proj[:, hidden : 2 * hidden]
        left[i] = gated.astype(bf16).astype(f32)
        grads = cotangent[i].astype(f32) * jax.nn.sigmoid(proj[:, 2 * hidden :])
        empty = jnp.zeros((padded - short, hidden), f32)
        for m in range(halves):
            part = grads[m * short : (m + 1) * short]
            outs[m, i] = jnp.concatenate([part, empty], axis=0).astype(bf16)
        return carry

    lax.fori_loop(0, here, body, 0)


def triangle_kernel(count, present, left, *refs):
    rights, (out, right, partial, rows) = refs[:count], refs[count:]
    here, half, hidden = left.shape
    short = rights[0].shape[0]
    padded = out.shape[2]
    for s in range(count):
        right[...] = rights[s][...].astype(f32)
        rows[...] = jnp.zeros_like(rows)

        def body(j, carry):
            held = right[j]
            for i in range(here):
                product = (left[i] * held).reshape(half // 8, 8, hidden)
                partial[pl.ds(8 * i, 8), :] = jnp.sum(product, axis=0)
            total = partial[pl.ds(0, here, stride=8), :]
            for sub in range(1, 8):
                total += partial[pl.ds(sub, here, stride=8), :]
            rows[pl.ds(j, here, stride=padded), :] = total
            return carry

        lax.fori_loop(0, present[s], body, 0)
        out[s] = rows[...].astype(bf16).reshape(here, padded, hidden)


def triangle(present, left, rights, padded):
    count, (here, half, hidden) = len(rights), left.shape
    return call(
        functools.partial(triangle_kernel, count),
        "triangle",
        0.7 * count,
        [present, left, *rights],
        [SMEM] + [VMEM] * (count + 1),
        [shape_of((count, here, padded, hidden), bf16)],
        [
            pltpu.VMEM(rights[0].shape, f32),
            pltpu.VMEM((here * 8, hidden), f32),
            pltpu.VMEM((here * padded, hidden), f32),
        ],
    )[0]


def triangle_norm_kernel(where, mine, other, outs, w_out, gain, bias, grad, normed):
    count, here, padded, hidden = mine.shape
    flat = (here * padded, hidden)

    def body(s, carry):
        total = (mine[s].astype(f32) + other[s].astype(f32)).reshape(flat)
        standard, inverse = standardize(total)
        normed[s] = (standard * gain[...] + bias[...]).astype(bf16).reshape(here, padded, hidden)
        grad_norm = dot(outs[where[s]].reshape(flat), w_out[...], 1, 1)
        result = layer_norm_backward(grad_norm, standard, inverse, gain[...])
        grad[s] = result.astype(bf16).reshape(here, padded, hidden)
        return carry

    lax.fori_loop(0, count, body, 0)


def triangle_norm(where, mine, other, outs, w_out, gain, bias):
    return call(
        triangle_norm_kernel,
        "triangle_norm",
        0.4 * mine.shape[0],
        [where, mine, other, outs, w_out, gain, bias],
        [SMEM] + [VMEM] * 6,
        [shape_of(mine.shape, bf16)] * 2,
    )


def hop_kernel(picks, carried, present, left, *refs):
    count = len(picks)
    grads, refs = refs[:count], refs[count:]
    arrived, refs = refs[: count * carried], refs[count * carried :]
    outs, wide = refs[:count], refs[count]
    here, half, hidden = left.shape
    short = outs[0].shape[0]
    for s in range(count):
        wide[...] = grads[s][picks[s]].astype(f32)
        out = outs[s]

        def body(pair, carry, s=s, out=out):
            at = [jnp.minimum(2 * pair + x, short - 1) for x in range(2)]
            totals = []
            for j in at:
                total = jnp.zeros((half, hidden), f32)
                for more in range(carried):
                    total += arrived[s + more * count][j].astype(f32)
                totals.append(total)
            for i in range(here):
                held = left[i]
                for x in range(2):
                    totals[x] += wide[i, pl.ds(at[x], 1), :] * held
            for x in range(2):
                out[at[x]] = totals[x].astype(out.dtype)
            return carry

        def clear(j, carry, out=out):
            out[j] = jnp.zeros((half, hidden), out.dtype)
            return carry

        pairs = (present[s] + 1) // 2
        lax.fori_loop(0, pairs, body, 0)
        lax.fori_loop(2 * pairs, short, clear, 0)


def hop(present, left, grads, picks, arrived, short, dtype=bf16, after=()):
    here, half, hidden = left.shape
    count = len(grads)
    carried = len(arrived) // count
    return call(
        functools.partial(hop_kernel, picks, carried),
        "scatter_hop",
        0.7 * count,
        [present, left, *grads, *arrived],
        [SMEM] + [VMEM] * (1 + count + len(arrived)),
        [shape_of((short, half, hidden), dtype)] * count,
        [pltpu.VMEM(grads[0].shape[1:], f32)],
        after,
    )


def left_gradient_kernel(count, carried, present, grads, *refs):
    rights, refs = refs[:count], refs[count:]
    before, (out, right, wide) = refs[:carried], refs[carried:]
    here = out.shape[0]
    short = rights[0].shape[0]
    right[short] = jnp.zeros(right.shape[1:], f32)
    if carried:
        out[...] = before[0][...]
    else:
        out[...] = jnp.zeros_like(out)
    for s in range(count):
        right[pl.ds(0, short)] = rights[s][...].astype(f32)
        wide[...] = grads[s].astype(f32)

        def rows(t, carry):
            def add(pair, totals):
                totals = list(totals)
                for j in (2 * pair, 2 * pair + 1):
                    held = right[j]
                    for x in range(2):
                        totals[x] += wide[2 * t + x, pl.ds(j, 1), :] * held
                return tuple(totals)

            start = (out[2 * t], out[2 * t + 1])
            one, two = lax.fori_loop(0, (present[s] + 1) // 2, add, start)
            out[2 * t] = one
            out[2 * t + 1] = two
            return carry

        lax.fori_loop(0, here // 2, rows, 0)


def left_gradient(present, grads, rights, before, after=()):
    count, here = grads.shape[:2]
    short, half, hidden = rights[0].shape
    return call(
        functools.partial(left_gradient_kernel, count, len(before)),
        "left_gradient",
        0.7 * count,
        [present, grads, *rights, *before],
        [SMEM] + [VMEM] * (1 + count + len(before)),
        [shape_of((here, half, hidden), f32)],
        [pltpu.VMEM((short + 1, half, hidden), f32), pltpu.VMEM(grads.shape[1:], f32)],
        after,
    )[0]


def output_kernel(
    slot, counts, lengths, slots, normed, cotangent, grad_left, w, w_out, outs, *refs
):
    norms, (update, gradient, weights, mask, picked, flat, total) = (
        refs[: len(counts)],
        refs[len(counts) :],
    )
    here, half, hidden = normed.shape
    halves, _, padded, _ = picked.shape
    short = half // halves
    mask[...] = present_columns(lengths, slot, half)
    total[...] = jnp.zeros_like(total)
    for m in range(halves):
        low = 0
        for norm, count in zip(norms, counts):

            @pl.when((slots[m] >= low) & (slots[m] < low + count))
            def _(m=m, norm=norm, low=low):
                picked[m] = norm[slots[m] - low]

            low += count

    def body(i, carry):
        values = normed[i]
        proj = dot(values, w[...], 1, 0)
        sig_left = jax.nn.sigmoid(proj[:, :hidden])
        val_left = proj[:, hidden : 2 * hidden]
        gate = jax.nn.sigmoid(proj[:, 2 * hidden :])
        tri = picked[:, i].reshape(halves * padded, hidden)
        product = dot(tri, w_out[...], 1, 0)
        for m in range(halves):
            flat[pl.ds(m * short, short), :] = product[m * padded : m * padded + short]
        projected = flat[...]
        update[i] = (gate * projected).astype(bf16)
        grad_gate = cotangent[i].astype(f32) * projected * gate * (1.0 - gate)
        shown = mask[...] * present_row(lengths, slot, first_row(here) + i)
        masked = grad_left[i] * shown
        grads = jnp.concatenate(
            [masked * val_left * sig_left * (1.0 - sig_left), masked * sig_left, grad_gate], axis=1
        ).astype(bf16)
        gradient[i] = dot(grads, w[...], 1, 1)
        total[:, : 3 * hidden] += dot(values, grads, 0, 0)
        total[:, 3 * hidden :] += dot(tri, outs[:halves, i].reshape(halves * padded, hidden), 0, 0)
        return carry

    lax.fori_loop(0, here, body, 0)
    weights[...] = total[...].astype(bf16)


def right_gradient_kernel(slot, lengths, normed, w, own_a, own_b, *refs):
    arrived, (grads, weights, mask, total) = refs[:4], refs[4:]
    here, half, hidden = normed.shape
    short = here // 2
    mask[...] = present_columns(lengths, slot, half)
    total[...] = jnp.zeros_like(total)

    def body(t, carry):
        parts = ((own_a, arrived[:2], t), (own_b, arrived[2:], t + short))
        for own, others, j in parts:
            values = normed[j]
            proj = dot(values, w[...], 1, 0)
            sig_right = jax.nn.sigmoid(proj[:, :hidden])
            val_right = proj[:, hidden:]
            shown = mask[...] * present_row(lengths, slot, first_row(here) + j)
            masked = shown * (own[t] + others[0][t].astype(f32) + others[1][t].astype(f32))
            result = jnp.concatenate(
                [masked * val_right * sig_right * (1.0 - sig_right), masked * sig_right], axis=1
            ).astype(bf16)
            grads[j] = result
            total[...] += dot(values, result, 0, 0)
        return carry

    lax.fori_loop(0, short, body, 0)
    weights[...] = total[...].astype(bf16)


def pair_gradient_kernel(pair, grads, gradient, gain, w, out):
    def body(t, carry):
        for i in (2 * t, 2 * t + 1):
            standard, inverse = standardize(pair[i].astype(f32))
            total = gradient[i] + dot(grads[i], w[...], 1, 1)
            out[i] = layer_norm_backward(total, standard, inverse, gain[...]).astype(bf16)
        return carry

    lax.fori_loop(0, pair.shape[0] // 2, body, 0)


def shards(
    pair,
    cotangent,
    chain_lengths,
    input_norm_gain,
    input_norm_bias,
    w_in,
    output_norm_gain,
    output_norm_bias,
    w_out,
):
    here, half, channels = pair.shape
    hidden = w_out.shape[0]
    row_count = lax.axis_size("row")
    slot = here * row_count // chain_lengths.shape[0]
    order = ring_order(row_count)
    place = jnp.asarray([order.index(r) for r in range(row_count)], jnp.int32)[
        lax.axis_index("row")
    ]
    ring = jnp.asarray(order, jnp.int32)
    col = lax.axis_index("col")
    short = here // 2
    padded = (short + 15) // 16 * 16
    forward = [(order[p], order[(p + 1) % row_count]) for p in range(row_count)]
    backward = [(order[p], order[(p - 1) % row_count]) for p in range(row_count)]
    w_left, w_right = w_in[:, : 2 * hidden], w_in[:, 2 * hidden : 4 * hidden]
    w_early = jnp.concatenate([w_left, w_in[:, 4 * hidden :]], axis=1)
    in_gain, in_bias = input_norm_gain.reshape(1, -1), input_norm_bias.reshape(1, -1)
    out_gain, out_bias = output_norm_gain.reshape(1, -1), output_norm_bias.reshape(1, -1)
    block = (here, half, hidden)
    half_block = (short, half, hidden)
    mask = pltpu.VMEM((half, 128), f32)

    def ahead(x):
        return lax.ppermute(x, "row", forward)

    def behind(x):
        return lax.ppermute(x, "row", backward)

    right_a, right_b, normed = call(
        functools.partial(input_kernel, slot),
        "input_side",
        3.0,
        [chain_lengths, pair, in_gain, in_bias, w_right],
        [SMEM] + [VMEM] * 4,
        [shape_of(half_block, bf16)] * 2 + [shape_of(block, bf16)],
        [mask],
    )

    hops = row_count // 2
    chain1, chain2 = [], []
    a, b, c, d = right_a, right_b, right_b, right_a
    for step in range(hops):
        a, b = ahead(a), behind(b)
        chain1 += [a, b]
        if step < hops - 1:
            c, d = ahead(c), behind(d)
            chain2 += [c, d]

    def half_index(offset, letter):
        return ring[(place + offset + row_count) % row_count] * 2 + letter

    early_hops = hops // 2
    groups = [[right_a, right_b] + chain1[: 2 * early_hops], chain1[2 * early_hops :], chain2]
    index1 = [half_index(sign * s, x) for s in range(1, hops + 1) for sign, x in ((-1, 0), (1, 1))]
    index2 = [half_index(sign * s, x) for s in range(1, hops) for sign, x in ((-1, 1), (1, 0))]
    own = [half_index(0, 0), half_index(0, 1)]
    indices = [own + index1[: 2 * early_hops], index1[2 * early_hops :], index2]
    indices = [jnp.stack(index).astype(jnp.int32) for index in indices]
    presents = [
        jnp.clip(chain_lengths[i * short // slot] - i * short % slot, 0, short) for i in indices
    ]

    left, mine_out = call(
        functools.partial(left_kernel, slot),
        "left_side",
        4.0,
        [chain_lengths, normed, cotangent, w_early],
        [SMEM] + [VMEM] * 3,
        [shape_of(block, f32), shape_of((row_count, here, padded, hidden), bf16)],
        [mask],
    )
    outs = jnp.concatenate([mine_out, swap_col(mine_out)], axis=0)

    norms, grads = [], []
    for rights, index, present in zip(groups, indices, presents):
        partial = triangle(present, left, rights, padded)
        at = ((index // row_count) ^ col) * row_count + index % row_count
        grad, norm = triangle_norm(
            at, partial, swap_col(partial), outs, w_out, out_gain, out_bias
        )
        grads.append(grad)
        norms.append(norm)

    def group1(s):
        at = 2 * (s - 1)
        if s <= early_hops:
            return 0, [at + 2, at + 3]
        at -= 2 * early_hops
        return 1, [at, at + 1]

    def chosen(g, picks):
        return presents[g][picks[0] : picks[1] + 1]

    arrived1, arrived2 = [], []
    for s in range(hops, 0, -1):
        g, picks = group1(s)
        x, y = hop(chosen(g, picks), left, [grads[g]] * 2, picks, arrived1, short)
        arrived1 = [behind(x), ahead(y)]
        if s == hops:
            first_hop = x
    for s in range(hops - 1, 0, -1):
        picks = [2 * s - 2, 2 * s - 1]
        x, y = hop(chosen(2, picks), left, [grads[2]] * 2, picks, arrived2, short)
        arrived2 = [behind(x), ahead(y)]

    own_a, own_b = hop(
        presents[0][:2], left, [grads[0]] * 2, [0, 1], [], short, f32, after=[first_hop]
    )
    before = []
    for g, rights, present in zip(grads, groups, presents):
        before = [left_gradient(present, g, rights, before, after=[first_hop])]
    flat_index = jnp.concatenate(indices)
    wanted = col * row_count + jnp.arange(row_count, dtype=jnp.int32)
    slots = jnp.argmax(flat_index[None, :] == wanted[:, None], axis=1).astype(jnp.int32)
    update, gradient, early = call(
        functools.partial(output_kernel, slot, [len(g) for g in groups]),
        "output_side",
        6.0,
        [chain_lengths, slots, normed, cotangent, before[0], w_early, w_out, outs, *norms],
        [SMEM] * 2 + [VMEM] * 9,
        [
            shape_of(block, bf16),
            shape_of(block, f32),
            shape_of((channels, 4 * hidden), bf16),
        ],
        [
            mask,
            pltpu.VMEM((row_count, here, padded, hidden), bf16),
            pltpu.VMEM((half, hidden), f32),
            pltpu.VMEM((channels, 4 * hidden), f32),
        ],
    )
    summed_early = sum_all(early, row_count).astype(f32)

    late, weights = call(
        functools.partial(right_gradient_kernel, slot),
        "right_gradient",
        3.0,
        [chain_lengths, normed, w_right, own_a, own_b]
        + [arrived1[0], arrived2[1], arrived1[1], arrived2[0]],
        [SMEM] + [VMEM] * 8,
        [
            shape_of((here, half, 2 * hidden), bf16),
            shape_of((channels, 2 * hidden), bf16),
        ],
        [mask, pltpu.VMEM((channels, 2 * hidden), f32)],
    )
    summed_late = sum_all(weights, row_count).astype(f32)
    (pair_gradient,) = call(
        pair_gradient_kernel,
        "pair_gradient",
        3.0,
        [pair, late, gradient, in_gain, w_right],
        [VMEM] * 5,
        [shape_of(block, bf16)],
    )
    grad_w_in = jnp.concatenate(
        [summed_early[:, : 2 * hidden], summed_late, summed_early[:, 2 * hidden : 3 * hidden]],
        axis=1,
    )
    grad_w_out = summed_early[:, 3 * hidden :]
    return (update, pair_gradient, grad_w_in, grad_w_out)


def solution(mesh):
    placed = (
        P(("grp", "row"), "col", None),
        P(("grp", "row"), "col", None),
        P("grp"),
        P(),
        P(),
        P(),
        P(),
        P(),
        P(),
    )
    return jax.shard_map(
        shards,
        mesh=mesh,
        in_specs=placed,
        out_specs=(
            P(("grp", "row"), "col", None),
            P(("grp", "row"), "col", None),
            P("grp", None),
            P("grp", None),
        ),
        check_vma=False,
    )
```

```python
import functools

import jax
import jax.numpy as jnp
from jax import lax
from jax.experimental import pallas as pl
from jax.experimental.pallas import tpu as pltpu
from jax.sharding import PartitionSpec as P

eps = 1e-05
f32 = jnp.float32
bf16 = jnp.bfloat16
VMEM = pl.BlockSpec(memory_space=pltpu.VMEM)
SMEM = pl.BlockSpec(memory_space=pltpu.SMEM)
ANY = pl.BlockSpec(memory_space=pl.ANY)
MIB = 1 << 20


def layer_norm_backward(output_gradient, standardized_input, inverse_deviation, norm_gain):
    scaled_output = output_gradient * norm_gain
    first_operand = jnp.mean(scaled_output, axis=-1, keepdims=True)
    second_operand = jnp.mean(scaled_output * standardized_input, axis=-1, keepdims=True)
    return inverse_deviation * (scaled_output - first_operand - standardized_input * second_operand)


def standardize(values):
    centered = values - jnp.mean(values, axis=-1, keepdims=True)
    inverse = lax.rsqrt(jnp.mean(centered * centered, axis=-1, keepdims=True) + eps)
    return centered * inverse, inverse


def dot(a, b, ca, cb):
    return lax.dot_general(a, b, (((ca,), (cb,)), ((), ())), preferred_element_type=f32)


def ring_order(row_count):
    if row_count == 8:
        return [0, 2, 4, 6, 7, 5, 3, 1]
    return list(range(row_count))


def ring_place(row_count, row):
    if row_count == 8:
        return jnp.where(row % 2 == 0, row // 2, row_count - 1 - row // 2)
    return row


def ring_row(row_count, place):
    if row_count == 8:
        return jnp.where(place < row_count // 2, 2 * place, 2 * (row_count - 1 - place) + 1)
    return place


def half_index(row_count, offset, letter):
    place = ring_place(row_count, lax.axis_index("row"))
    return ring_row(row_count, (place + offset + row_count) % row_count) * 2 + letter


def arrival_slot(row_count, index):
    hops = row_count // 2
    letter = index % 2
    apart = ring_place(row_count, index // 2) - ring_place(row_count, lax.axis_index("row"))
    apart = (apart + row_count) % row_count
    near = jnp.where(letter == 0, row_count - apart, apart)
    first = 2 * near + letter
    second = 2 + 2 * hops + 2 * (row_count - near - 1) + 1 - letter
    return jnp.where(apart == 0, letter, jnp.where(near <= hops, first, second))


def present_count(row_count, lengths, slot, short, where):
    start = half_index(row_count, *where) * short
    return jnp.clip(lengths[start // slot] - start % slot, 0, short)


def swap_col(x):
    return lax.ppermute(x, "col", [(0, 1), (1, 0)])


def sum_all(x, row_count):
    def add(a, b):
        return (a.astype(f32) + b.astype(f32)).astype(bf16)

    x = add(x, swap_col(x))
    step = 1
    while step < row_count:
        x = add(x, lax.ppermute(x, "row", [(r, r ^ step) for r in range(row_count)]))
        step *= 2
    return x


def call(kernel, name, microseconds, args, specs, outs, scratch=(), after=()):
    held = sum(a.size * a.dtype.itemsize for a, s in zip(args, specs) if s is VMEM)
    held += sum(int(o.size) * o.dtype.itemsize for o in outs)
    held += sum(int(s.inner_aval.size) * 4 for s in scratch)

    def body(*refs):
        kernel(*refs[: len(args)], *refs[len(args) + len(after) :])

    return pl.pallas_call(
        body,
        out_shape=list(outs),
        in_specs=list(specs) + [ANY] * len(after),
        out_specs=[VMEM] * len(outs),
        scratch_shapes=list(scratch),
        compiler_params=pltpu.CompilerParams(vmem_limit_bytes=min(56 * MIB, held * 5 // 4 + 6 * MIB)),
        cost_estimate=pl.CostEstimate(
            flops=int(microseconds * 1.1e9), bytes_accessed=MIB, transcendentals=0
        ),
        name=name,
    )(*args, *after)


def shape_of(dims, dtype):
    return jax.ShapeDtypeStruct(dims, dtype)


def present_row(lengths, slot, position):
    return (position % slot < lengths[position // slot]).astype(f32)


def present_columns(lengths, slot, half):
    at = lax.axis_index("col") * half + lax.broadcasted_iota(jnp.int32, (half, 128), 0)
    chain = at // slot
    held = jnp.zeros((half, 128), jnp.int32)
    for c in range(lengths.shape[0]):
        held = jnp.where(chain == c, lengths[c], held)
    return (at - chain * slot < held).astype(f32)


def first_row(here):
    return lax.axis_index("row") * here


def input_kernel(slot, lengths, pair, gain, bias, w, right_a, right_b, normed, mask):
    here, half, hidden = pair.shape
    short = here // 2
    mask[...] = present_columns(lengths, slot, half)

    for out, first in ((right_a, 0), (right_b, short)):
        for t in range(short):
            i = first + t
            standard, _ = standardize(pair[i].astype(f32))
            values = (standard * gain[...] + bias[...]).astype(bf16)
            normed[i] = values
            proj = dot(values, w[:, 2 * hidden : 4 * hidden], 1, 0)
            shown = mask[...] * present_row(lengths, slot, first_row(here) + i)
            gated = jax.nn.sigmoid(proj[:, :hidden]) * proj[:, hidden:]
            out[t] = (shown * gated).astype(bf16)


def by_rows(here, body):
    def step(t, carry):
        for x in range(here // 2):
            body(t * (here // 2) + x)
        return carry

    lax.fori_loop(0, 2, step, 0)


def left_kernel(slot, lengths, normed, cotangent, w, left, outs, mask):
    here, half, hidden = normed.shape
    halves, _, padded, _ = outs.shape
    short = half // halves
    mask[...] = present_columns(lengths, slot, half)

    def body(i):
        proj = dot(normed[i], w[:, : 2 * hidden], 1, 0)
        shown = mask[...] * present_row(lengths, slot, first_row(here) + i)
        gated = shown * jax.nn.sigmoid(proj[:, :hidden]) * proj[:, hidden:]
        left[i] = gated.astype(bf16).astype(f32)
        gate = jax.nn.sigmoid(dot(normed[i], w[:, 4 * hidden :], 1, 0))
        grads = cotangent[i].astype(f32) * gate
        empty = jnp.zeros((padded - short, hidden), f32)
        for m in range(halves):
            part = grads[m * short : (m + 1) * short]
            outs[m, i] = jnp.concatenate([part, empty], axis=0).astype(bf16)

    by_rows(here, body)


def triangle_kernel(row_count, slot, places, lengths, left, *refs):
    count = len(places)
    rights, (out, right, partial, rows) = refs[:count], refs[count:]
    here, half, hidden = left.shape
    short = rights[0].shape[0]
    padded = out.shape[2]
    for s in range(count):
        right[...] = rights[s][...].astype(f32)
        rows[...] = jnp.zeros_like(rows)

        def body(j, carry):
            held = right[j]
            for i in range(here):
                product = (left[i] * held).reshape(half // 8, 8, hidden)
                partial[pl.ds(8 * i, 8), :] = jnp.sum(product, axis=0)
            total = partial[pl.ds(0, here, stride=8), :]
            for sub in range(1, 8):
                total += partial[pl.ds(sub, here, stride=8), :]
            rows[pl.ds(j, here, stride=padded), :] = total
            return carry

        present = present_count(row_count, lengths, slot, short, places[s])
        lax.fori_loop(0, present, body, 0)
        out[s] = rows[...].astype(bf16).reshape(here, padded, hidden)


def triangle(row_count, slot, places, lengths, left, rights, padded, after=()):
    count, (here, half, hidden) = len(rights), left.shape
    return call(
        functools.partial(triangle_kernel, row_count, slot, places),
        "triangle",
        0.7 * count,
        [lengths, left, *rights],
        [SMEM] + [VMEM] * (count + 1),
        [shape_of((count, here, padded, hidden), bf16)],
        [
            pltpu.VMEM(rights[0].shape, f32),
            pltpu.VMEM((here * 8, hidden), f32),
            pltpu.VMEM((here * padded, hidden), f32),
        ],
        after,
    )[0]


def triangle_norm_kernel(row_count, places, mine, other, outs, w_out, gain, bias, grad, normed):
    count, here, padded, hidden = mine.shape
    flat = (here * padded, hidden)

    for s in range(count):
        index = half_index(row_count, *places[s])
        near = ((index // row_count) ^ lax.axis_index("col")) * row_count + index % row_count
        total = (mine[s].astype(f32) + other[s].astype(f32)).reshape(flat)
        standard, inverse = standardize(total)
        normed[s] = (standard * gain[...] + bias[...]).astype(bf16).reshape(here, padded, hidden)
        grad_norm = dot(outs[near].reshape(flat), w_out[...], 1, 1)
        result = layer_norm_backward(grad_norm, standard, inverse, gain[...])
        grad[s] = result.astype(bf16).reshape(here, padded, hidden)


def triangle_norm(row_count, places, mine, other, outs, w_out, gain, bias):
    return call(
        functools.partial(triangle_norm_kernel, row_count, places),
        "triangle_norm",
        0.4 * mine.shape[0],
        [mine, other, outs, w_out, gain, bias],
        [VMEM] * 6,
        [shape_of(mine.shape, bf16)] * 2,
    )


def hop_kernel(row_count, slot, places, picks, carried, lengths, left, *refs):
    count = len(picks)
    grads, refs = refs[:count], refs[count:]
    arrived, refs = refs[: count * carried], refs[count * carried :]
    outs, wide = refs[:count], refs[count]
    here, half, hidden = left.shape
    short = outs[0].shape[0]
    for s in range(count):
        wide[...] = grads[s][picks[s]].astype(f32)
        out = outs[s]

        def body(pair, carry, s=s, out=out):
            at = [jnp.minimum(2 * pair + x, short - 1) for x in range(2)]
            totals = []
            for j in at:
                total = jnp.zeros((half, hidden), f32)
                for more in range(carried):
                    total += arrived[s + more * count][j].astype(f32)
                totals.append(total)
            for i in range(here):
                held = left[i]
                for x in range(2):
                    totals[x] += wide[i, pl.ds(at[x], 1), :] * held
            for x in range(2):
                out[at[x]] = totals[x].astype(out.dtype)
            return carry

        def clear(j, carry, out=out):
            out[j] = jnp.zeros((half, hidden), out.dtype)
            return carry

        present = present_count(row_count, lengths, slot, short, places[s])
        pairs = (present + 1) // 2
        lax.fori_loop(0, pairs, body, 0)
        lax.fori_loop(2 * pairs, short, clear, 0)


def hop(row_count, slot, places, lengths, left, grads, picks, arrived, short, dtype=bf16, after=()):
    here, half, hidden = left.shape
    count = len(grads)
    carried = len(arrived) // count
    return call(
        functools.partial(hop_kernel, row_count, slot, places, picks, carried),
        "scatter_hop",
        0.7 * count,
        [lengths, left, *grads, *arrived],
        [SMEM] + [VMEM] * (1 + count + len(arrived)),
        [shape_of((short, half, hidden), dtype)] * count,
        [pltpu.VMEM(grads[0].shape[1:], f32)],
        after,
    )


def left_gradient_kernel(picks, carried, grads, *refs):
    count = len(picks)
    rights, refs = refs[:count], refs[count:]
    before, (out, right, wide) = refs[:carried], refs[carried:]
    here, half, hidden = out.shape
    short = rights[0].shape[0]
    for s in range(count):
        right[s] = rights[s][...].astype(f32)
        wide[s] = grads[picks[s]].astype(f32)

    def row(i, carry):
        total = before[0][i] if carried else jnp.zeros((half, hidden), f32)
        for s in range(count):
            for j in range(short):
                total += wide[s, i, pl.ds(j, 1), :] * right[s, j]
        out[i] = total
        return carry

    lax.fori_loop(0, here, row, 0)


def left_gradient(grads, picks, rights, before, after=()):
    count, here = len(picks), grads.shape[1]
    short, half, hidden = rights[0].shape
    return call(
        functools.partial(left_gradient_kernel, picks, len(before)),
        "left_gradient",
        0.9 * count,
        [grads, *rights, *before],
        [VMEM] * (1 + count + len(before)),
        [shape_of((here, half, hidden), f32)],
        [
            pltpu.VMEM((count, short, half, hidden), f32),
            pltpu.VMEM((count,) + grads.shape[1:], f32),
        ],
        after,
    )[0]


def output_kernel(
    row_count, slot, counts, lengths, normed, cotangent, grad_left, w, w_out, outs, *refs
):
    norms, (update, gradient, weights, mask, picked, total) = (
        refs[: len(counts)],
        refs[len(counts) :],
    )
    here, half, hidden = normed.shape
    halves, _, padded, _ = picked.shape
    short = half // halves
    mask[...] = present_columns(lengths, slot, half)
    total[...] = jnp.zeros_like(total)
    for m in range(halves):
        low = 0
        stands = arrival_slot(row_count, lax.axis_index("col") * row_count + m)
        for norm, count in zip(norms, counts):

            @pl.when((stands >= low) & (stands < low + count))
            def _(m=m, norm=norm, low=low, stands=stands):
                picked[m] = norm[stands - low]

            low += count

    def body(i):
        values = normed[i]
        proj = dot(values, w[:, : 2 * hidden], 1, 0)
        sig_left = jax.nn.sigmoid(proj[:, :hidden])
        val_left = proj[:, hidden:]
        gate = jax.nn.sigmoid(dot(values, w[:, 4 * hidden :], 1, 0))
        tri = picked[:, i].reshape(halves * padded, hidden)
        product = dot(tri, w_out[...], 1, 0)
        projected = jnp.concatenate(
            [product[m * padded : m * padded + short] for m in range(halves)], axis=0
        )
        update[i] = (gate * projected).astype(bf16)
        grad_gate = (cotangent[i].astype(f32) * projected * gate * (1.0 - gate)).astype(bf16)
        shown = mask[...] * present_row(lengths, slot, first_row(here) + i)
        masked = grad_left[i] * shown
        grads = jnp.concatenate(
            [masked * val_left * sig_left * (1.0 - sig_left), masked * sig_left], axis=1
        ).astype(bf16)
        gradient[i] = dot(grads, w[:, : 2 * hidden], 1, 1) + dot(
            grad_gate, w[:, 4 * hidden :], 1, 1
        )
        total[:, : 2 * hidden] += dot(values, grads, 0, 0)
        total[:, 2 * hidden : 3 * hidden] += dot(values, grad_gate, 0, 0)
        total[:, 3 * hidden :] += dot(tri, outs[:halves, i].reshape(halves * padded, hidden), 0, 0)

    by_rows(here, body)
    weights[...] = total[...].astype(bf16)


def right_gradient_kernel(slot, lengths, normed, w, own_a, own_b, *refs):
    arrived, (grads, weights, mask, total) = refs[:4], refs[4:]
    here, half, hidden = normed.shape
    short = here // 2
    mask[...] = present_columns(lengths, slot, half)
    total[...] = jnp.zeros_like(total)

    for own, others, first in ((own_a, arrived[:2], 0), (own_b, arrived[2:], short)):
        for t in range(short):
            j = first + t
            values = normed[j]
            proj = dot(values, w[:, 2 * hidden : 4 * hidden], 1, 0)
            sig_right = jax.nn.sigmoid(proj[:, :hidden])
            val_right = proj[:, hidden:]
            shown = mask[...] * present_row(lengths, slot, first_row(here) + j)
            masked = shown * (own[t] + others[0][t].astype(f32) + others[1][t].astype(f32))
            result = jnp.concatenate(
                [masked * val_right * sig_right * (1.0 - sig_right), masked * sig_right], axis=1
            ).astype(bf16)
            grads[j] = result
            total[...] += dot(values, result, 0, 0)
    weights[...] = total[...].astype(bf16)


def pair_gradient_kernel(pair, grads, gradient, gain, w, out):
    hidden = pair.shape[2]

    def body(i):
        standard, inverse = standardize(pair[i].astype(f32))
        total = gradient[i] + dot(grads[i], w[:, 2 * hidden : 4 * hidden], 1, 1)
        out[i] = layer_norm_backward(total, standard, inverse, gain[...]).astype(bf16)

    by_rows(pair.shape[0], body)


def shards(
    pair,
    cotangent,
    chain_lengths,
    input_norm_gain,
    input_norm_bias,
    w_in,
    output_norm_gain,
    output_norm_bias,
    w_out,
):
    here, half, channels = pair.shape
    hidden = w_out.shape[0]
    row_count = lax.axis_size("row")
    slot = here * row_count // chain_lengths.shape[0]
    order = ring_order(row_count)
    short = here // 2
    padded = (short + 15) // 16 * 16
    forward = [(order[p], order[(p + 1) % row_count]) for p in range(row_count)]
    backward = [(order[p], order[(p - 1) % row_count]) for p in range(row_count)]
    in_gain, in_bias = input_norm_gain.reshape(1, -1), input_norm_bias.reshape(1, -1)
    out_gain, out_bias = output_norm_gain.reshape(1, -1), output_norm_bias.reshape(1, -1)
    block = (here, half, hidden)
    half_block = (short, half, hidden)
    mask = pltpu.VMEM((half, 128), f32)

    def ahead(x):
        return lax.ppermute(x, "row", forward)

    def behind(x):
        return lax.ppermute(x, "row", backward)

    right_a, right_b, normed = call(
        functools.partial(input_kernel, slot),
        "input_side",
        3.0,
        [chain_lengths, pair, in_gain, in_bias, w_in],
        [SMEM] + [VMEM] * 4,
        [shape_of(half_block, bf16)] * 2 + [shape_of(block, bf16)],
        [mask],
    )

    hops = row_count // 2
    chain1, chain2 = [], []
    a, b, c, d = right_a, right_b, right_b, right_a
    for step in range(hops):
        a, b = ahead(a), behind(b)
        chain1 += [a, b]
        if step < hops - 1:
            c, d = ahead(c), behind(d)
            chain2 += [c, d]

    early_hops = hops // 2
    groups = [[right_a, right_b] + chain1[: 2 * early_hops], chain1[2 * early_hops :], chain2]
    places1 = [p for s in range(1, hops + 1) for p in ((-s, 0), (s, 1))]
    places2 = [p for s in range(1, hops) for p in ((-s, 1), (s, 0))]
    places = [[(0, 0), (0, 1)] + places1[: 2 * early_hops], places1[2 * early_hops :], places2]

    left, mine_out = call(
        functools.partial(left_kernel, slot),
        "left_side",
        4.0,
        [chain_lengths, normed, cotangent, w_in],
        [SMEM] + [VMEM] * 3,
        [shape_of(block, f32), shape_of((row_count, here, padded, hidden), bf16)],
        [mask],
    )
    outs = jnp.concatenate([mine_out, swap_col(mine_out)], axis=0)

    norms, grads = [], []

    def triangle_group(g, after=()):
        partial = triangle(
            row_count, slot, places[g], chain_lengths, left, groups[g], padded, after
        )
        grad, norm = triangle_norm(
            row_count, places[g], partial, swap_col(partial), outs, w_out, out_gain, out_bias
        )
        grads.append(grad)
        norms.append(norm)

    def scatter(g, picks, arrived, dtype=bf16, after=()):
        return hop(
            row_count,
            slot,
            [places[g][pick] for pick in picks],
            chain_lengths,
            left,
            [grads[g]] * 2,
            picks,
            arrived,
            short,
            dtype,
            after,
        )

    def group1(s):
        at = 2 * (s - 1)
        if s <= early_hops:
            return 0, [at + 2, at + 3]
        at -= 2 * early_hops
        return 1, [at, at + 1]

    pieces = []

    def add_left(g, picks, after):
        rights = [groups[g][pick] for pick in picks]
        pieces[:] = [left_gradient(grads[g], picks, rights, pieces[:], after)]

    arrived1, arrived2 = [], []
    triangle_group(0)
    triangle_group(1)
    g, picks = group1(hops)
    x, y = scatter(g, picks, arrived1)
    arrived1 = [behind(x), ahead(y)]
    add_left(0, list(range(len(groups[0]))), [x])
    triangle_group(2, pieces)
    waiting = [
        (g, [at, at + 1]) for g in (1, 2) for at in range(0, len(groups[g]), 2)
    ]
    for s in range(hops - 1, 0, -1):
        x, y = scatter(2, [2 * s - 2, 2 * s - 1], arrived2, after=pieces)
        arrived2 = [behind(x), ahead(y)]
        if waiting:
            add_left(*waiting.pop(0), [x])
        g, picks = group1(s)
        x, y = scatter(g, picks, arrived1, after=pieces)
        arrived1 = [behind(x), ahead(y)]
        if waiting:
            add_left(*waiting.pop(0), [x])
    while waiting:
        add_left(*waiting.pop(0), [x])
    own_a, own_b = scatter(0, [0, 1], [], f32, after=[x])
    update, gradient, early = call(
        functools.partial(output_kernel, row_count, slot, [len(g) for g in groups]),
        "output_side",
        6.0,
        [chain_lengths, normed, cotangent, pieces[0], w_in, w_out, outs, *norms],
        [SMEM] + [VMEM] * 9,
        [
            shape_of(block, bf16),
            shape_of(block, f32),
            shape_of((channels, 4 * hidden), bf16),
        ],
        [
            mask,
            pltpu.VMEM((row_count, here, padded, hidden), bf16),
            pltpu.VMEM((channels, 4 * hidden), f32),
        ],
    )
    summed_early = sum_all(early, row_count).astype(f32)

    late, weights = call(
        functools.partial(right_gradient_kernel, slot),
        "right_gradient",
        3.0,
        [chain_lengths, normed, w_in, own_a, own_b]
        + [arrived1[0], arrived2[1], arrived1[1], arrived2[0]],
        [SMEM] + [VMEM] * 8,
        [
            shape_of((here, half, 2 * hidden), bf16),
            shape_of((channels, 2 * hidden), bf16),
        ],
        [mask, pltpu.VMEM((channels, 2 * hidden), f32)],
    )
    summed_late = sum_all(weights, row_count).astype(f32)
    (pair_gradient,) = call(
        pair_gradient_kernel,
        "pair_gradient",
        3.0,
        [pair, late, gradient, in_gain, w_in],
        [VMEM] * 5,
        [shape_of(block, bf16)],
    )
    grad_w_in = jnp.concatenate(
        [summed_early[:, : 2 * hidden], summed_late, summed_early[:, 2 * hidden : 3 * hidden]],
        axis=1,
    )
    grad_w_out = summed_early[:, 3 * hidden :]
    return (update, pair_gradient, grad_w_in, grad_w_out)


def solution(mesh):
    placed = (
        P(("grp", "row"), "col", None),
        P(("grp", "row"), "col", None),
        P("grp"),
        P(),
        P(),
        P(),
        P(),
        P(),
        P(),
    )
    return jax.shard_map(
        shards,
        mesh=mesh,
        in_specs=placed,
        out_specs=(
            P(("grp", "row"), "col", None),
            P(("grp", "row"), "col", None),
            P("grp", None),
            P("grp", None),
        ),
        check_vma=False,
    )
```

```python
import functools

import jax
import jax.numpy as jnp
from jax import lax
from jax.experimental import pallas as pl
from jax.experimental.pallas import tpu as pltpu
from jax.sharding import PartitionSpec as P

eps = 1e-05
f32 = jnp.float32
bf16 = jnp.bfloat16
VMEM = pl.BlockSpec(memory_space=pltpu.VMEM)
SMEM = pl.BlockSpec(memory_space=pltpu.SMEM)
ANY = pl.BlockSpec(memory_space=pl.ANY)
MIB = 1 << 20


def layer_norm_backward(output_gradient, standardized_input, inverse_deviation, norm_gain):
    scaled_output = output_gradient * norm_gain
    first_operand = jnp.mean(scaled_output, axis=-1, keepdims=True)
    second_operand = jnp.mean(scaled_output * standardized_input, axis=-1, keepdims=True)
    return inverse_deviation * (scaled_output - first_operand - standardized_input * second_operand)


def standardize(values):
    centered = values - jnp.mean(values, axis=-1, keepdims=True)
    inverse = lax.rsqrt(jnp.mean(centered * centered, axis=-1, keepdims=True) + eps)
    return centered * inverse, inverse


def dot(a, b, ca, cb):
    return lax.dot_general(a, b, (((ca,), (cb,)), ((), ())), preferred_element_type=f32)


def ring_order(row_count):
    if row_count == 8:
        return [0, 2, 4, 6, 7, 5, 3, 1]
    return list(range(row_count))


def ring_place(row_count, row):
    if row_count == 8:
        return jnp.where(row % 2 == 0, row // 2, row_count - 1 - row // 2)
    return row


def ring_row(row_count, place):
    if row_count == 8:
        return jnp.where(place < row_count // 2, 2 * place, 2 * (row_count - 1 - place) + 1)
    return place


def half_index(row_count, offset, letter):
    place = ring_place(row_count, lax.axis_index("row"))
    return ring_row(row_count, (place + offset + row_count) % row_count) * 2 + letter


def arrival_slot(row_count, index):
    hops = row_count // 2
    letter = index % 2
    apart = ring_place(row_count, index // 2) - ring_place(row_count, lax.axis_index("row"))
    apart = (apart + row_count) % row_count
    near = jnp.where(letter == 0, row_count - apart, apart)
    first = 4 * near - 2 + letter
    second = 4 * (row_count - near) - 2 + 3 - letter
    return jnp.where(apart == 0, letter, jnp.where(near <= hops, first, second))


def present_count(row_count, lengths, slot, short, where):
    start = half_index(row_count, *where) * short
    return jnp.clip(lengths[start // slot] - start % slot, 0, short)


def swap_col(x):
    return lax.ppermute(x, "col", [(0, 1), (1, 0)])


def add(a, b):
    return (a.astype(f32) + b.astype(f32)).astype(bf16)


def sum_all(x, row_count):
    other = swap_col(x)
    step = 1
    while step < row_count:
        x = add(x, other)
        other = lax.ppermute(x, "row", [(r, r ^ step) for r in range(row_count)])
        step *= 2
    return x, other


def whole_of(x):
    return pl.BlockSpec(x.shape, lambda step: (0,) * x.ndim)


def call(kernel, name, microseconds, args, specs, outs, scratch=(), after=()):
    held = sum(a.size * a.dtype.itemsize for a, s in zip(args, specs) if s is not SMEM)
    after = [x for x in after if x is not None]
    streamed = any(s is not SMEM and s is not VMEM for s in specs)
    held += sum(int(o.size) * o.dtype.itemsize for o in outs)
    held += sum(int(s.inner_aval.size) * 4 for s in scratch)

    def body(*refs):
        kernel(*refs[: len(args)], *refs[len(args) + len(after) :])

    return pl.pallas_call(
        body,
        grid=(1,) if streamed else (),
        out_shape=list(outs),
        in_specs=list(specs) + [ANY] * len(after),
        out_specs=[VMEM] * len(outs),
        scratch_shapes=list(scratch),
        compiler_params=pltpu.CompilerParams(vmem_limit_bytes=min(56 * MIB, held * 5 // 4 + 6 * MIB)),
        cost_estimate=pl.CostEstimate(
            flops=int(microseconds * 1.1e9), bytes_accessed=MIB, transcendentals=0
        ),
        name=name,
    )(*args, *after)


def shape_of(dims, dtype):
    return jax.ShapeDtypeStruct(dims, dtype)


def present_row(lengths, slot, position):
    return (position % slot < lengths[position // slot]).astype(f32)


def present_columns(lengths, slot, half):
    at = lax.axis_index("col") * half + lax.broadcasted_iota(jnp.int32, (half, 128), 0)
    chain = at // slot
    held = jnp.zeros((half, 128), jnp.int32)
    for c in range(lengths.shape[0]):
        held = jnp.where(chain == c, lengths[c], held)
    return (at - chain * slot < held).astype(f32)


def first_row(here):
    return lax.axis_index("row") * here


def input_kernel(slot, lengths, pair, gain, bias, w, right, normed, mask):
    here, half, hidden = pair.shape
    mask[...] = present_columns(lengths, slot, half)

    for i in range(here):
        standard, _ = standardize(pair[i].astype(f32))
        values = (standard * gain[...] + bias[...]).astype(bf16)
        normed[i] = values
        proj = dot(values, w[:, 2 * hidden : 4 * hidden], 1, 0)
        shown = mask[...] * present_row(lengths, slot, first_row(here) + i)
        gated = jax.nn.sigmoid(proj[:, :hidden]) * proj[:, hidden:]
        right[i] = (shown * gated).astype(bf16)


def by_rows(here, body):
    def step(t, carry):
        for x in range(here // 2):
            body(t * (here // 2) + x)
        return carry

    lax.fori_loop(0, 2, step, 0)


def left_kernel(slot, lengths, normed, cotangent, w, left, outs, mask):
    here, half, hidden = normed.shape
    halves, _, padded, _ = outs.shape
    short = half // halves
    mask[...] = present_columns(lengths, slot, half)

    def body(i):
        proj = dot(normed[i], w[:, : 2 * hidden], 1, 0)
        shown = mask[...] * present_row(lengths, slot, first_row(here) + i)
        gated = shown * jax.nn.sigmoid(proj[:, :hidden]) * proj[:, hidden:]
        left[i] = gated.astype(bf16).astype(f32)
        gate = jax.nn.sigmoid(dot(normed[i], w[:, 4 * hidden :], 1, 0))
        grads = cotangent[i].astype(f32) * gate
        empty = jnp.zeros((padded - short, hidden), f32)
        for m in range(halves):
            part = grads[m * short : (m + 1) * short]
            outs[m, i] = jnp.concatenate([part, empty], axis=0).astype(bf16)

    by_rows(here, body)


def triangle_kernel(row_count, slot, halves, arrays, lengths, left, *refs):
    rights, (out, right, partial, rows) = refs[:arrays], refs[arrays:]
    here, half, hidden = left.shape
    padded = out.shape[2]
    short = right.shape[0]
    for s, (array, first, place) in enumerate(halves):
        right[...] = rights[array][pl.ds(first, short)].astype(f32)
        rows[...] = jnp.zeros_like(rows)

        def body(j, carry):
            held = right[j]
            for i in range(here):
                product = (left[i] * held).reshape(half // 8, 8, hidden)
                partial[pl.ds(8 * i, 8), :] = jnp.sum(product, axis=0)
            total = partial[pl.ds(0, here, stride=8), :]
            for sub in range(1, 8):
                total += partial[pl.ds(sub, here, stride=8), :]
            rows[pl.ds(j, here, stride=padded), :] = total
            return carry

        present = present_count(row_count, lengths, slot, short, place)
        lax.fori_loop(0, present, body, 0)
        out[s] = rows[...].astype(bf16).reshape(here, padded, hidden)


def triangle(row_count, slot, halves, lengths, left, rights, padded, after):
    count, (here, half, hidden) = len(halves), left.shape
    return call(
        functools.partial(triangle_kernel, row_count, slot, halves, len(rights)),
        "triangle",
        0.9 * count,
        [lengths, left, *rights],
        [SMEM] + [VMEM] * (len(rights) + 1),
        [shape_of((count, here, padded, hidden), bf16)],
        [
            pltpu.VMEM((here // 2, half, hidden), f32),
            pltpu.VMEM((here * 8, hidden), f32),
            pltpu.VMEM((here * padded, hidden), f32),
        ],
        after,
    )[0]


def triangle_norm_kernel(row_count, places, mine, other, outs, w_out, gain, bias, grad, normed):
    count, here, padded, hidden = mine.shape
    flat = (here * padded, hidden)

    for s in range(count):
        index = half_index(row_count, *places[s])
        near = ((index // row_count) ^ lax.axis_index("col")) * row_count + index % row_count
        total = (mine[s].astype(f32) + other[s].astype(f32)).reshape(flat)
        standard, inverse = standardize(total)
        normed[s] = (standard * gain[...] + bias[...]).astype(bf16).reshape(here, padded, hidden)
        grad_norm = dot(outs[near].reshape(flat), w_out[...], 1, 1)
        result = layer_norm_backward(grad_norm, standard, inverse, gain[...])
        grad[s] = result.astype(bf16).reshape(here, padded, hidden)


def triangle_norm(row_count, places, mine, other, outs, w_out, gain, bias, after):
    return call(
        functools.partial(triangle_norm_kernel, row_count, places),
        "triangle_norm",
        0.4 * mine.shape[0],
        [mine, other, outs, w_out, gain, bias],
        [VMEM] * 6,
        [shape_of(mine.shape, bf16)] * 2,
        (),
        after,
    )


def hop_kernel(row_count, slot, places, picks, carried, lengths, left, *refs):
    count = len(picks)
    grads, refs = refs[:count], refs[count:]
    arrived, refs = refs[: count * carried], refs[count * carried :]
    outs, wide = refs[:count], refs[count]
    here, half, hidden = left.shape
    short = outs[0].shape[0]
    for s in range(count):
        wide[...] = grads[s][picks[s]].astype(f32)
        out = outs[s]

        def body(pair, carry, s=s, out=out):
            at = [jnp.minimum(2 * pair + x, short - 1) for x in range(2)]
            totals = []
            for j in at:
                total = jnp.zeros((half, hidden), f32)
                for more in range(carried):
                    total += arrived[s + more * count][j].astype(f32)
                totals.append(total)
            for i in range(here):
                held = left[i]
                for x in range(2):
                    totals[x] += wide[i, pl.ds(at[x], 1), :] * held
            for x in range(2):
                out[at[x]] = totals[x].astype(out.dtype)
            return carry

        def clear(j, carry, out=out):
            out[j] = jnp.zeros((half, hidden), out.dtype)
            return carry

        present = present_count(row_count, lengths, slot, short, places[s])
        pairs = (present + 1) // 2
        lax.fori_loop(0, pairs, body, 0)
        lax.fori_loop(2 * pairs, short, clear, 0)


def hop(row_count, slot, places, lengths, left, grads, picks, arrived, short, dtype=bf16, after=()):
    here, half, hidden = left.shape
    count = len(grads)
    carried = len(arrived) // count
    return call(
        functools.partial(hop_kernel, row_count, slot, places, picks, carried),
        "scatter_hop",
        0.7 * count,
        [lengths, left, *grads, *arrived],
        [SMEM] + [VMEM] * (1 + count + len(arrived)),
        [shape_of((short, half, hidden), dtype)] * count,
        [pltpu.VMEM(grads[0].shape[1:], f32)],
        after,
    )


def left_gradient_kernel(halves, picks, arrays, carried, grads, *refs):
    count = len(picks)
    rights, refs = refs[:arrays], refs[arrays:]
    before, (out, right, wide) = refs[:carried], refs[carried:]
    here, half, hidden = out.shape
    short = here // 2
    for s, pick in enumerate(picks):
        array, first, _ = halves[pick]
        right[s] = rights[array][pl.ds(first, short)].astype(f32)
        wide[s] = grads[pick].astype(f32)

    def row(i, carry):
        total = before[0][i] if carried else jnp.zeros((half, hidden), f32)
        for s in range(count):
            for j in range(short):
                total += wide[s, i, pl.ds(j, 1), :] * right[s, j]
        out[i] = total
        return carry

    lax.fori_loop(0, here, row, 0)


def left_gradient(halves, picks, grads, rights, before, after):
    count, here = len(picks), grads.shape[1]
    half, hidden = rights[0].shape[1:]
    return call(
        functools.partial(left_gradient_kernel, halves, picks, len(rights), len(before)),
        "left_gradient",
        0.9 * count,
        [grads, *rights, *before],
        [VMEM] * (1 + len(rights) + len(before)),
        [shape_of((here, half, hidden), f32)],
        [
            pltpu.VMEM((count, here // 2, half, hidden), f32),
            pltpu.VMEM((count,) + grads.shape[1:], f32),
        ],
        after,
    )[0]


def output_kernel(
    row_count, slot, counts, lengths, normed, cotangent, grad_left, w, w_out, outs, *refs
):
    norms, (update, gradient, weights, mask, picked, total) = (
        refs[: len(counts)],
        refs[len(counts) :],
    )
    here, half, hidden = normed.shape
    halves, _, padded, _ = picked.shape
    short = half // halves
    mask[...] = present_columns(lengths, slot, half)
    total[...] = jnp.zeros_like(total)
    for m in range(halves):
        low = 0
        stands = arrival_slot(row_count, lax.axis_index("col") * row_count + m)
        for norm, count in zip(norms, counts):

            @pl.when((stands >= low) & (stands < low + count))
            def _(m=m, norm=norm, low=low, stands=stands):
                picked[m] = norm[stands - low]

            low += count

    def body(i):
        values = normed[i]
        proj = dot(values, w[:, : 2 * hidden], 1, 0)
        sig_left = jax.nn.sigmoid(proj[:, :hidden])
        val_left = proj[:, hidden:]
        gate = jax.nn.sigmoid(dot(values, w[:, 4 * hidden :], 1, 0))
        tri = picked[:, i].reshape(halves * padded, hidden)
        product = dot(tri, w_out[...], 1, 0)
        projected = jnp.concatenate(
            [product[m * padded : m * padded + short] for m in range(halves)], axis=0
        )
        update[i] = (gate * projected).astype(bf16)
        grad_gate = (cotangent[i].astype(f32) * projected * gate * (1.0 - gate)).astype(bf16)
        shown = mask[...] * present_row(lengths, slot, first_row(here) + i)
        masked = grad_left[i] * shown
        grads = jnp.concatenate(
            [masked * val_left * sig_left * (1.0 - sig_left), masked * sig_left], axis=1
        ).astype(bf16)
        gradient[i] = dot(grads, w[:, : 2 * hidden], 1, 1) + dot(
            grad_gate, w[:, 4 * hidden :], 1, 1
        )
        total[:, : 2 * hidden] += dot(values, grads, 0, 0)
        total[:, 2 * hidden : 3 * hidden] += dot(values, grad_gate, 0, 0)
        total[:, 3 * hidden :] += dot(tri, outs[:halves, i].reshape(halves * padded, hidden), 0, 0)

    by_rows(here, body)
    weights[...] = total[...].astype(bf16)


def right_gradient_kernel(slot, lengths, normed, w, own_a, own_b, *refs):
    arrived, (grads, weights, mask, total) = refs[:4], refs[4:]
    here, half, hidden = normed.shape
    short = here // 2
    mask[...] = present_columns(lengths, slot, half)
    total[...] = jnp.zeros_like(total)

    for own, others, first in ((own_a, arrived[:2], 0), (own_b, arrived[2:], short)):
        for t in range(short):
            j = first + t
            values = normed[j]
            proj = dot(values, w[:, 2 * hidden : 4 * hidden], 1, 0)
            sig_right = jax.nn.sigmoid(proj[:, :hidden])
            val_right = proj[:, hidden:]
            shown = mask[...] * present_row(lengths, slot, first_row(here) + j)
            masked = shown * (own[t] + others[0][t].astype(f32) + others[1][t].astype(f32))
            result = jnp.concatenate(
                [masked * val_right * sig_right * (1.0 - sig_right), masked * sig_right], axis=1
            ).astype(bf16)
            grads[j] = result
            total[...] += dot(values, result, 0, 0)
    weights[...] = total[...].astype(bf16)


def pair_gradient_kernel(pair, grads, gradient, gain, w, out):
    hidden = pair.shape[2]

    def body(i):
        standard, inverse = standardize(pair[i].astype(f32))
        total = gradient[i] + dot(grads[i], w[:, 2 * hidden : 4 * hidden], 1, 1)
        out[i] = layer_norm_backward(total, standard, inverse, gain[...]).astype(bf16)

    by_rows(pair.shape[0], body)


def weights_kernel(early, mine, other, w_in, w_out):
    hidden = w_out.shape[0]
    w_in[:, : 2 * hidden] = early[:, : 2 * hidden].astype(f32)
    late = mine[...].astype(f32) + other[...].astype(f32)
    w_in[:, 2 * hidden : 4 * hidden] = late.astype(bf16).astype(f32)
    w_in[:, 4 * hidden :] = early[:, 2 * hidden : 3 * hidden].astype(f32)
    w_out[...] = early[:, 3 * hidden :].astype(f32)


def shards(
    pair,
    cotangent,
    chain_lengths,
    input_norm_gain,
    input_norm_bias,
    w_in,
    output_norm_gain,
    output_norm_bias,
    w_out,
):
    here, half, channels = pair.shape
    hidden = w_out.shape[0]
    row_count = lax.axis_size("row")
    slot = here * row_count // chain_lengths.shape[0]
    order = ring_order(row_count)
    short = here // 2
    padded = (short + 15) // 16 * 16
    forward = [(order[p], order[(p + 1) % row_count]) for p in range(row_count)]
    backward = [(order[p], order[(p - 1) % row_count]) for p in range(row_count)]
    in_gain, in_bias = input_norm_gain.reshape(1, -1), input_norm_bias.reshape(1, -1)
    out_gain, out_bias = output_norm_gain.reshape(1, -1), output_norm_bias.reshape(1, -1)
    block = (here, half, hidden)
    mask = pltpu.VMEM((half, 128), f32)

    def ahead(x):
        return lax.ppermute(x, "row", forward)

    def behind(x):
        return lax.ppermute(x, "row", backward)

    right, normed = call(
        functools.partial(input_kernel, slot),
        "input_side",
        3.0,
        [chain_lengths, pair, in_gain, in_bias, w_in],
        [SMEM] + [whole_of(x) for x in (pair, in_gain, in_bias, w_in)],
        [shape_of(block, bf16)] * 2,
        [mask],
    )

    hops = row_count // 2
    groups = [[right]]
    halves = [[(0, 0, (0, 0)), (0, short, (0, 1))]]
    x = y = right
    for s in range(1, hops):
        x, y = ahead(x), behind(y)
        groups.append([x, y])
        halves.append(
            [(0, 0, (-s, 0)), (1, short, (s, 1)), (0, short, (-s, 1)), (1, 0, (s, 0))]
        )
    groups.append([ahead(x[:short]), behind(y[short:])])
    halves.append([(0, 0, (-hops, 0)), (1, 0, (hops, 1))])

    left, mine_out = call(
        functools.partial(left_kernel, slot),
        "left_side",
        4.0,
        [chain_lengths, normed, cotangent, w_in],
        [SMEM] + [VMEM] * 3,
        [shape_of(block, f32), shape_of((row_count, here, padded, hidden), bf16)],
        [mask],
    )
    outs = jnp.concatenate([mine_out, swap_col(mine_out)], axis=0)

    norms, grads, partials, others = [], [], [], []
    last = [left]
    pieces = []

    def triangles(s):
        partials.append(
            triangle(row_count, slot, halves[s], chain_lengths, left, groups[s], padded, last)
        )
        others.append(swap_col(partials[s]))
        last[:] = [partials[s]]

    def normal(s):
        places = [place for _, _, place in halves[s]]
        grad, norm = triangle_norm(
            row_count, places, partials[s], others[s], outs, w_out, out_gain, out_bias, last
        )
        grads.append(grad)
        norms.append(norm)
        last[:] = [grad]

    def add_left(s, picks=None):
        picks = list(range(len(halves[s]))) if picks is None else picks
        pieces[:] = [
            left_gradient(halves[s], picks, grads[s], groups[s], pieces[:], last)
        ]
        last[:] = pieces

    def scatter(s, picks, arrived, dtype=bf16):
        x, y = hop(
            row_count,
            slot,
            [halves[s][pick][2] for pick in picks],
            chain_lengths,
            left,
            [grads[s]] * 2,
            picks,
            arrived,
            short,
            dtype,
            last,
        )
        last[:] = [x]
        return x, y

    arrived = {0: [], 2: []}

    def send(s, chain):
        x, y = scatter(s, [chain, chain + 1], arrived[chain])
        arrived[chain] = [behind(x), ahead(y)]

    def output_side():
        results = call(
            functools.partial(output_kernel, row_count, slot, [len(h) for h in halves]),
            "output_side",
            6.0,
            [chain_lengths, normed, cotangent, pieces[0], w_in, w_out, outs, *norms],
            [SMEM] + [VMEM] * (6 + len(norms)),
            [
                shape_of(block, bf16),
                shape_of(block, f32),
                shape_of((channels, 4 * hidden), bf16),
            ],
            [
                mask,
                pltpu.VMEM((row_count, here, padded, hidden), bf16),
                pltpu.VMEM((channels, 4 * hidden), f32),
            ],
            last,
        )
        last[:] = results[:1]
        return results

    triangles(0)
    for s in range(1, hops):
        triangles(s)
        normal(s - 1)
        add_left(s - 1)
    normal(hops - 1)
    send(hops - 1, 2)
    triangles(hops)
    add_left(hops - 1, [0, 1])
    normal(hops)
    send(hops, 0)
    add_left(hops - 1, [2, 3])
    fillers = [lambda: add_left(hops), None, output_side, lambda: scatter(0, [0, 1], [], f32)]
    results = []
    for s in range(hops - 1, 0, -1):
        if s > 1:
            send(s - 1, 2)
        if fillers:
            results.append(fillers.pop(0)())
        send(s, 0)
        if s == hops - 1:
            fillers.pop(0)
    while fillers:
        results.append(fillers.pop(0)())
    _, (update, gradient, early), (own_a, own_b) = results
    arrived1, arrived2 = arrived[0], [arrived[2][1], arrived[2][0]]
    summed_early = add(*sum_all(early, row_count))

    late, weights = call(
        functools.partial(right_gradient_kernel, slot),
        "right_gradient",
        3.0,
        [chain_lengths, normed, w_in, own_a, own_b]
        + [arrived1[0], arrived2[0], arrived1[1], arrived2[1]],
        [SMEM] + [VMEM] * 8,
        [
            shape_of((here, half, 2 * hidden), bf16),
            shape_of((channels, 2 * hidden), bf16),
        ],
        [mask, pltpu.VMEM((channels, 2 * hidden), f32)],
    )
    terms = sum_all(weights, row_count)
    (pair_gradient,) = call(
        pair_gradient_kernel,
        "pair_gradient",
        3.0,
        [pair, late, gradient, in_gain, w_in],
        [VMEM] * 5,
        [shape_of(block, bf16)],
    )
    grad_w_in, grad_w_out = call(
        weights_kernel,
        "weight_gradients",
        0.5,
        [summed_early, *terms],
        [VMEM] * 3,
        [shape_of(w_in.shape, f32), shape_of(w_out.shape, f32)],
    )
    return (update, pair_gradient, grad_w_in, grad_w_out)


def solution(mesh):
    placed = (
        P(("grp", "row"), "col", None),
        P(("grp", "row"), "col", None),
        P("grp"),
        P(),
        P(),
        P(),
        P(),
        P(),
        P(),
    )
    return jax.shard_map(
        shards,
        mesh=mesh,
        in_specs=placed,
        out_specs=(
            P(("grp", "row"), "col", None),
            P(("grp", "row"), "col", None),
            P("grp", None),
            P("grp", None),
        ),
        check_vma=False,
    )
```

```python
import functools
import math

import jax
import jax.numpy as jnp
from jax import lax
from jax.experimental import pallas as pl
from jax.experimental.pallas import tpu as pltpu
from jax.sharding import PartitionSpec as P

eps = 1e-05
f32 = jnp.float32
bf16 = jnp.bfloat16
VMEM = pl.BlockSpec(memory_space=pltpu.VMEM)
SMEM = pl.BlockSpec(memory_space=pltpu.SMEM)
ANY = pl.BlockSpec(memory_space=pl.ANY)
MIB = 1 << 20


def layer_norm_backward(output_gradient, standardized_input, inverse_deviation, norm_gain):
    scaled_output = output_gradient * norm_gain
    first_operand = jnp.mean(scaled_output, axis=-1, keepdims=True)
    second_operand = jnp.mean(scaled_output * standardized_input, axis=-1, keepdims=True)
    return inverse_deviation * (scaled_output - first_operand - standardized_input * second_operand)


def standardize(values):
    centered = values - jnp.mean(values, axis=-1, keepdims=True)
    inverse = lax.rsqrt(jnp.mean(centered * centered, axis=-1, keepdims=True) + eps)
    return centered * inverse, inverse


def dot(a, b, ca, cb):
    return lax.dot_general(a, b, (((ca,), (cb,)), ((), ())), preferred_element_type=f32)


def ring_order(row_count):
    if row_count == 8:
        return [0, 2, 4, 6, 7, 5, 3, 1]
    return list(range(row_count))


def ring_place(row_count, row):
    if row_count == 8:
        return jnp.where(row % 2 == 0, row // 2, row_count - 1 - row // 2)
    return row


def ring_row(row_count, place):
    if row_count == 8:
        return jnp.where(place < row_count // 2, 2 * place, 2 * (row_count - 1 - place) + 1)
    return place


def half_index(row_count, offset, letter):
    place = ring_place(row_count, lax.axis_index("row"))
    return ring_row(row_count, (place + offset + row_count) % row_count) * 2 + letter


def arrival_slot(row_count, index):
    hops = row_count // 2
    letter = index % 2
    apart = ring_place(row_count, index // 2) - ring_place(row_count, lax.axis_index("row"))
    apart = (apart + row_count) % row_count
    near = jnp.where(letter == 0, row_count - apart, apart)
    first = 4 * near - 2 + letter
    second = 4 * (row_count - near) - 2 + 3 - letter
    return jnp.where(apart == 0, letter, jnp.where(near <= hops, first, second))


def present_count(row_count, lengths, slot, short, where):
    start = half_index(row_count, *where) * short
    return jnp.clip(lengths[start // slot] - start % slot, 0, short)


def swap_col(x):
    return lax.ppermute(x, "col", [(0, 1), (1, 0)])


def add(a, b):
    return (a.astype(f32) + b.astype(f32)).astype(bf16)


def sum_all(x, row_count):
    other = swap_col(x)
    step = 1
    while step < row_count:
        x = add(x, other)
        other = lax.ppermute(x, "row", [(r, r ^ step) for r in range(row_count)])
        step *= 2
    return x, other


def call(kernel, name, microseconds, args, specs, outs, scratch=(), after=()):
    held = sum(a.size * a.dtype.itemsize for a, s in zip(args, specs) if s is VMEM)
    after = [x for x in after if x is not None]
    held += sum(int(o.size) * o.dtype.itemsize for o in outs)
    held += sum(math.prod(s.inner_aval.shape) * 4 for s in scratch)

    def body(*refs):
        kernel(*refs[: len(args)], *refs[len(args) + len(after) :])

    return pl.pallas_call(
        body,
        out_shape=list(outs),
        in_specs=list(specs) + [ANY] * len(after),
        out_specs=[VMEM] * len(outs),
        scratch_shapes=list(scratch),
        compiler_params=pltpu.CompilerParams(vmem_limit_bytes=min(56 * MIB, held * 5 // 4 + 6 * MIB)),
        cost_estimate=pl.CostEstimate(
            flops=int(microseconds * 1e6), bytes_accessed=1024, transcendentals=0
        ),
        name=name,
    )(*args, *after)


def tiles(half):
    return [(k, min(16, half - k)) for k in range(0, half, 16)]


def joined(terms):
    chains = [terms[0::2], terms[1::2]]
    sums = []
    for chain in chains:
        total = chain[0]
        for term in chain[1:]:
            total = total + term
        sums.append(total.astype(f32))
    return sums[0] + sums[1]


def wide_row(ref, *at):
    return jnp.broadcast_to(ref[at], (16, ref.shape[-1])).astype(bf16)


def shape_of(dims, dtype):
    return jax.ShapeDtypeStruct(dims, dtype)


def present_row(lengths, slot, position):
    return (position % slot < lengths[position // slot]).astype(f32)


def present_columns(lengths, slot, half):
    at = lax.axis_index("col") * half + lax.broadcasted_iota(jnp.int32, (half, 128), 0)
    chain = at // slot
    held = jnp.zeros((half, 128), jnp.int32)
    for c in range(lengths.shape[0]):
        held = jnp.where(chain == c, lengths[c], held)
    return (at - chain * slot < held).astype(f32)


def first_row(here):
    return lax.axis_index("row") * here


def input_kernel(slot, *refs):
    given, (right, normed), held, (mask, sems) = refs[:5], refs[5:7], refs[7:12], refs[12:]
    copies = [
        pltpu.make_async_copy(source, target, sems.at[at])
        for at, (source, target) in enumerate(zip(given, held))
    ]
    for copy in copies:
        copy.start()
    for copy in copies:
        copy.wait()
    lengths, pair, gain, bias, w = held
    here, half, hidden = pair.shape
    mask[...] = present_columns(lengths, slot, half)

    for i in range(here):
        standard, _ = standardize(pair[i].astype(f32))
        values = (standard * gain[...] + bias[...]).astype(bf16)
        normed[i] = values
        proj = dot(values, w[:, 2 * hidden : 4 * hidden], 1, 0)
        shown = mask[...] * present_row(lengths, slot, first_row(here) + i)
        gated = jax.nn.sigmoid(proj[:, :hidden]) * proj[:, hidden:]
        right[i] = (shown * gated).astype(bf16)


def by_rows(here, body):
    def step(t, carry):
        for x in range(here // 2):
            body(t * (here // 2) + x)
        return carry

    lax.fori_loop(0, 2, step, 0)


def left_kernel(slot, lengths, normed, cotangent, w, left, outs, mask):
    here, half, hidden = normed.shape
    halves, _, padded, _ = outs.shape
    short = half // halves
    mask[...] = present_columns(lengths, slot, half)

    def body(i):
        proj = dot(normed[i], w[:, : 2 * hidden], 1, 0)
        shown = mask[...] * present_row(lengths, slot, first_row(here) + i)
        gated = shown * jax.nn.sigmoid(proj[:, :hidden]) * proj[:, hidden:]
        left[i] = gated.astype(bf16)
        gate = jax.nn.sigmoid(dot(normed[i], w[:, 4 * hidden :], 1, 0))
        grads = cotangent[i].astype(f32) * gate
        empty = jnp.zeros((padded - short, hidden), f32)
        for m in range(halves):
            part = grads[m * short : (m + 1) * short]
            outs[m, i] = jnp.concatenate([part, empty], axis=0).astype(bf16)

    by_rows(here, body)


def triangle_kernel(row_count, slot, halves, arrays, lengths, left, *refs):
    rights, (out, partial, rows) = refs[:arrays], refs[arrays:]
    here, half, hidden = left.shape
    padded = out.shape[2]
    short = here // 2
    for s, (array, first, place) in enumerate(halves):
        rows[...] = jnp.zeros_like(rows)

        def body(j, carry, right=rights[array], first=first):
            held = [right[first + j, pl.ds(k, size), :] for k, size in tiles(half)]
            for i in range(here):
                products = [
                    left[i, pl.ds(k, size), :] * held[at]
                    for at, (k, size) in enumerate(tiles(half))
                ]
                rest = products.pop() if half % 16 else None
                total = joined(products)
                total = total[:8] + total[8:]
                if rest is not None:
                    total += rest.astype(f32)
                partial[pl.ds(8 * i, 8), :] = total
            total = partial[pl.ds(0, here, stride=8), :]
            for sub in range(1, 8):
                total += partial[pl.ds(sub, here, stride=8), :]
            rows[pl.ds(j, here, stride=padded), :] = total
            return carry

        present = present_count(row_count, lengths, slot, short, place)
        lax.fori_loop(0, present, body, 0)
        out[s] = rows[...].astype(bf16).reshape(here, padded, hidden)


def triangle(row_count, slot, halves, lengths, left, rights, padded, after):
    count, (here, half, hidden) = len(halves), left.shape
    return call(
        functools.partial(triangle_kernel, row_count, slot, halves, len(rights)),
        "triangle",
        0.9 * count,
        [lengths, left, *rights],
        [SMEM] + [VMEM] * (len(rights) + 1),
        [shape_of((count, here, padded, hidden), bf16)],
        [
            pltpu.VMEM((here * 8, hidden), f32),
            pltpu.VMEM((here * padded, hidden), f32),
        ],
        after,
    )[0]


def triangle_norm_kernel(row_count, places, mine, other, outs, w_out, gain, bias, grad, normed):
    count, here, padded, hidden = mine.shape
    flat = (here * padded, hidden)

    for s in range(count):
        index = half_index(row_count, *places[s])
        near = ((index // row_count) ^ lax.axis_index("col")) * row_count + index % row_count
        total = (mine[s].astype(f32) + other[s].astype(f32)).reshape(flat)
        standard, inverse = standardize(total)
        normed[s] = (standard * gain[...] + bias[...]).astype(bf16).reshape(here, padded, hidden)
        grad_norm = dot(outs[near].reshape(flat), w_out[...], 1, 1)
        result = layer_norm_backward(grad_norm, standard, inverse, gain[...])
        grad[s] = result.astype(bf16).reshape(here, padded, hidden)


def triangle_norm(row_count, places, mine, other, outs, w_out, gain, bias, after):
    return call(
        functools.partial(triangle_norm_kernel, row_count, places),
        "triangle_norm",
        0.4 * mine.shape[0],
        [mine, other, outs, w_out, gain, bias],
        [VMEM] * 6,
        [shape_of(mine.shape, bf16)] * 2,
        (),
        after,
    )


def hop_kernel(row_count, slot, places, picks, carried, lengths, left, *refs):
    count = len(picks)
    grads, refs = refs[:count], refs[count:]
    arrived, refs = refs[: count * carried], refs[count * carried :]
    outs, wide = refs[:count], refs[count]
    here, half, hidden = left.shape
    short = outs[0].shape[0]
    for s in range(count):
        wide[...] = grads[s][picks[s]].astype(f32)
        out = outs[s]

        def body(pair, carry, s=s, out=out):
            at = [jnp.minimum(2 * pair + x, short - 1) for x in range(2)]
            totals = [[] for _ in at]
            for j, total in zip(at, totals):
                for k, size in tiles(half):
                    start = jnp.zeros((size, hidden), f32)
                    for more in range(carried):
                        start += arrived[s + more * count][j, pl.ds(k, size), :].astype(f32)
                    total.append(start)
            for low in range(0, here, short):
                chosen = range(low, min(low + short, here))
                weights = [[wide_row(wide, i, pl.ds(j, 1)) for i in chosen] for j in at]
                for t, (k, size) in enumerate(tiles(half)):
                    held = [left[i, pl.ds(k, size), :] for i in chosen]
                    for x in range(2):
                        totals[x][t] += joined([w[:size] * h for w, h in zip(weights[x], held)])
            for j, total in zip(at, totals):
                for t, (k, size) in enumerate(tiles(half)):
                    out[j, pl.ds(k, size), :] = total[t].astype(out.dtype)
            return carry

        def clear(j, carry, out=out):
            out[j] = jnp.zeros((half, hidden), out.dtype)
            return carry

        present = present_count(row_count, lengths, slot, short, places[s])
        pairs = (present + 1) // 2
        lax.fori_loop(0, pairs, body, 0)
        lax.fori_loop(2 * pairs, short, clear, 0)


def hop(row_count, slot, places, lengths, left, grads, picks, arrived, short, dtype=bf16, after=()):
    here, half, hidden = left.shape
    count = len(grads)
    carried = len(arrived) // count
    return call(
        functools.partial(hop_kernel, row_count, slot, places, picks, carried),
        "scatter_hop",
        0.7 * count,
        [lengths, left, *grads, *arrived],
        [SMEM] + [VMEM] * (1 + count + len(arrived)),
        [shape_of((short, half, hidden), dtype)] * count,
        [pltpu.VMEM(grads[0].shape[1:], f32)],
        after,
    )


def left_gradient_kernel(halves, picks, arrays, carried, grads, *refs):
    count = len(picks)
    rights, refs = refs[:arrays], refs[arrays:]
    before, (out, wide) = refs[:carried], refs[carried:]
    here, half, hidden = out.shape
    short = here // 2
    for s, pick in enumerate(picks):
        wide[s] = grads[pick].astype(f32)

    def row(pair, carry):
        rows = (2 * pair, 2 * pair + 1)
        for s, pick in enumerate(picks):
            array, first, _ = halves[pick]
            weights = [[wide_row(wide, s, i, pl.ds(j, 1)) for j in range(short)] for i in rows]
            for k, size in tiles(half):
                held = [rights[array][first + j, pl.ds(k, size), :] for j in range(short)]
                for i, weight in zip(rows, weights):
                    total = joined([w[:size] * h for w, h in zip(weight, held)])
                    if s:
                        total += out[i, pl.ds(k, size), :]
                    elif carried:
                        total += before[0][i, pl.ds(k, size), :]
                    out[i, pl.ds(k, size), :] = total
        return carry

    lax.fori_loop(0, here // 2, row, 0)


def left_gradient(halves, picks, grads, rights, before, after):
    count, here = len(picks), grads.shape[1]
    half, hidden = rights[0].shape[1:]
    return call(
        functools.partial(left_gradient_kernel, halves, picks, len(rights), len(before)),
        "left_gradient",
        0.9 * count,
        [grads, *rights, *before],
        [VMEM] * (1 + len(rights) + len(before)),
        [shape_of((here, half, hidden), f32)],
        [pltpu.VMEM((count,) + grads.shape[1:], f32)],
        after,
    )[0]


def output_kernel(
    row_count, slot, counts, lengths, normed, cotangent, grad_left, w, w_out, outs, *refs
):
    norms, (update, gradient, weights, mask, picked, total) = (
        refs[: len(counts)],
        refs[len(counts) :],
    )
    here, half, hidden = normed.shape
    halves, _, padded, _ = picked.shape
    short = half // halves
    mask[...] = present_columns(lengths, slot, half)
    total[...] = jnp.zeros_like(total)
    for m in range(halves):
        low = 0
        stands = arrival_slot(row_count, lax.axis_index("col") * row_count + m)
        for norm, count in zip(norms, counts):

            @pl.when((stands >= low) & (stands < low + count))
            def _(m=m, norm=norm, low=low, stands=stands):
                picked[m] = norm[stands - low]

            low += count

    def body(i):
        values = normed[i]
        proj = dot(values, w[:, : 2 * hidden], 1, 0)
        sig_left = jax.nn.sigmoid(proj[:, :hidden])
        val_left = proj[:, hidden:]
        gate = jax.nn.sigmoid(dot(values, w[:, 4 * hidden :], 1, 0))
        tri = picked[:, i].reshape(halves * padded, hidden)
        product = dot(tri, w_out[...], 1, 0)
        projected = jnp.concatenate(
            [product[m * padded : m * padded + short] for m in range(halves)], axis=0
        )
        update[i] = (gate * projected).astype(bf16)
        grad_gate = (cotangent[i].astype(f32) * projected * gate * (1.0 - gate)).astype(bf16)
        shown = mask[...] * present_row(lengths, slot, first_row(here) + i)
        masked = grad_left[i] * shown
        grads = jnp.concatenate(
            [masked * val_left * sig_left * (1.0 - sig_left), masked * sig_left], axis=1
        ).astype(bf16)
        gradient[i] = dot(grads, w[:, : 2 * hidden], 1, 1) + dot(
            grad_gate, w[:, 4 * hidden :], 1, 1
        )
        total[:, : 2 * hidden] += dot(values, grads, 0, 0)
        total[:, 2 * hidden : 3 * hidden] += dot(values, grad_gate, 0, 0)
        total[:, 3 * hidden :] += dot(tri, outs[:halves, i].reshape(halves * padded, hidden), 0, 0)

    by_rows(here, body)
    weights[...] = total[...].astype(bf16)


def right_gradient_kernel(slot, lengths, normed, w, own_a, own_b, *refs):
    arrived, (grads, weights, mask, total) = refs[:4], refs[4:]
    here, half, hidden = normed.shape
    short = here // 2
    mask[...] = present_columns(lengths, slot, half)
    total[...] = jnp.zeros_like(total)

    for own, others, first in ((own_a, arrived[:2], 0), (own_b, arrived[2:], short)):
        for t in range(short):
            j = first + t
            values = normed[j]
            proj = dot(values, w[:, 2 * hidden : 4 * hidden], 1, 0)
            sig_right = jax.nn.sigmoid(proj[:, :hidden])
            val_right = proj[:, hidden:]
            shown = mask[...] * present_row(lengths, slot, first_row(here) + j)
            masked = shown * (own[t] + others[0][t].astype(f32) + others[1][t].astype(f32))
            result = jnp.concatenate(
                [masked * val_right * sig_right * (1.0 - sig_right), masked * sig_right], axis=1
            ).astype(bf16)
            grads[j] = result
            total[...] += dot(values, result, 0, 0)
    weights[...] = total[...].astype(bf16)


def pair_gradient_kernel(pair, grads, gradient, gain, w, out):
    hidden = pair.shape[2]

    def body(i):
        standard, inverse = standardize(pair[i].astype(f32))
        total = gradient[i] + dot(grads[i], w[:, 2 * hidden : 4 * hidden], 1, 1)
        out[i] = layer_norm_backward(total, standard, inverse, gain[...]).astype(bf16)

    by_rows(pair.shape[0], body)


def weights_kernel(early, mine, other, w_in, w_out):
    hidden = w_out.shape[0]
    w_in[:, : 2 * hidden] = early[:, : 2 * hidden].astype(f32)
    late = mine[...].astype(f32) + other[...].astype(f32)
    w_in[:, 2 * hidden : 4 * hidden] = late.astype(bf16).astype(f32)
    w_in[:, 4 * hidden :] = early[:, 2 * hidden : 3 * hidden].astype(f32)
    w_out[...] = early[:, 3 * hidden :].astype(f32)


def shards(
    pair,
    cotangent,
    chain_lengths,
    input_norm_gain,
    input_norm_bias,
    w_in,
    output_norm_gain,
    output_norm_bias,
    w_out,
):
    here, half, channels = pair.shape
    hidden = w_out.shape[0]
    row_count = lax.axis_size("row")
    slot = here * row_count // chain_lengths.shape[0]
    order = ring_order(row_count)
    short = here // 2
    padded = (short + 15) // 16 * 16
    forward = [(order[p], order[(p + 1) % row_count]) for p in range(row_count)]
    backward = [(order[p], order[(p - 1) % row_count]) for p in range(row_count)]
    in_gain, in_bias = input_norm_gain.reshape(1, -1), input_norm_bias.reshape(1, -1)
    out_gain, out_bias = output_norm_gain.reshape(1, -1), output_norm_bias.reshape(1, -1)
    block = (here, half, hidden)
    mask = pltpu.VMEM((half, 128), f32)

    def ahead(x):
        return lax.ppermute(x, "row", forward)

    def behind(x):
        return lax.ppermute(x, "row", backward)

    right, normed = call(
        functools.partial(input_kernel, slot),
        "input_side",
        3.0,
        [chain_lengths, pair, in_gain, in_bias, w_in],
        [pl.BlockSpec(memory_space=pltpu.HBM)] * 5,
        [shape_of(block, bf16)] * 2,
        [
            pltpu.SMEM(chain_lengths.shape, jnp.int32),
            pltpu.VMEM(block, bf16),
            pltpu.VMEM(in_gain.shape, f32),
            pltpu.VMEM(in_bias.shape, f32),
            pltpu.VMEM(w_in.shape, bf16),
            mask,
            pltpu.SemaphoreType.DMA((5,)),
        ],
    )

    hops = row_count // 2
    groups = [[right]]
    halves = [[(0, 0, (0, 0)), (0, short, (0, 1))]]
    for s in range(1, hops):
        halves.append(
            [(0, 0, (-s, 0)), (1, short, (s, 1)), (0, short, (-s, 1)), (1, 0, (s, 0))]
        )
    halves.append([(0, 0, (-hops, 0)), (1, 0, (hops, 1))])

    def gather(s, x, y):
        if s == hops:
            x, y = x[:short], y[short:]
        groups.append([ahead(x), behind(y)])

    gather(1, right, right)
    left, mine_out = call(
        functools.partial(left_kernel, slot),
        "left_side",
        4.0,
        [chain_lengths, normed, cotangent, w_in],
        [SMEM] + [VMEM] * 3,
        [shape_of(block, bf16), shape_of((row_count, here, padded, hidden), bf16)],
        [mask],
    )
    outs = jnp.concatenate([mine_out, swap_col(mine_out)], axis=0)

    norms, grads, partials, others = [], [], [], []
    last = [left]
    pieces = []

    def triangles(s):
        partials.append(
            triangle(row_count, slot, halves[s], chain_lengths, left, groups[s], padded, last)
        )
        others.append(swap_col(partials[s]))
        last[:] = [partials[s]]

    def normal(s):
        places = [place for _, _, place in halves[s]]
        grad, norm = triangle_norm(
            row_count, places, partials[s], others[s], outs, w_out, out_gain, out_bias, last
        )
        grads.append(grad)
        norms.append(norm)
        last[:] = [grad]

    def add_left(s, picks=None):
        picks = list(range(len(halves[s]))) if picks is None else picks
        pieces[:] = [
            left_gradient(halves[s], picks, grads[s], groups[s], pieces[:], last)
        ]
        last[:] = pieces

    def scatter(s, picks, arrived, dtype=bf16):
        x, y = hop(
            row_count,
            slot,
            [halves[s][pick][2] for pick in picks],
            chain_lengths,
            left,
            [grads[s]] * 2,
            picks,
            arrived,
            short,
            dtype,
            last,
        )
        last[:] = [x]
        return x, y

    arrived = {0: [], 2: []}

    def send(s, chain):
        x, y = scatter(s, [chain, chain + 1], arrived[chain])
        arrived[chain] = [behind(x), ahead(y)]

    def output_side():
        results = call(
            functools.partial(output_kernel, row_count, slot, [len(h) for h in halves]),
            "output_side",
            6.0,
            [chain_lengths, normed, cotangent, pieces[0], w_in, w_out, outs, *norms],
            [SMEM] + [VMEM] * (6 + len(norms)),
            [
                shape_of(block, bf16),
                shape_of(block, f32),
                shape_of((channels, 4 * hidden), bf16),
            ],
            [
                mask,
                pltpu.VMEM((row_count, here, padded, hidden), bf16),
                pltpu.VMEM((channels, 4 * hidden), f32),
            ],
            last,
        )
        last[:] = results[:1]
        return results

    for s in range(hops):
        triangles(s)
        normal(s)
        if s == hops - 1:
            send(s, 2)
            add_left(s, [0, 1])
        else:
            add_left(s)
            x, y, _ = lax.optimization_barrier((*groups[s + 1], pieces[0]))
            gather(s + 2, x, y)
    triangles(hops)
    normal(hops)
    send(hops, 0)
    add_left(hops - 1, [2, 3])
    fillers = [lambda: add_left(hops), None, output_side, lambda: scatter(0, [0, 1], [], f32)]
    results = []
    for s in range(hops - 1, 0, -1):
        if s > 1:
            send(s - 1, 2)
        if fillers:
            results.append(fillers.pop(0)())
        send(s, 0)
        if s == hops - 1:
            fillers.pop(0)
    while fillers:
        results.append(fillers.pop(0)())
    _, (update, gradient, early), (own_a, own_b) = results
    arrived1, arrived2 = arrived[0], [arrived[2][1], arrived[2][0]]
    summed_early = add(*sum_all(early, row_count))

    late, weights = call(
        functools.partial(right_gradient_kernel, slot),
        "right_gradient",
        3.0,
        [chain_lengths, normed, w_in, own_a, own_b]
        + [arrived1[0], arrived2[0], arrived1[1], arrived2[1]],
        [SMEM] + [VMEM] * 8,
        [
            shape_of((here, half, 2 * hidden), bf16),
            shape_of((channels, 2 * hidden), bf16),
        ],
        [mask, pltpu.VMEM((channels, 2 * hidden), f32)],
    )
    terms = sum_all(weights, row_count)
    (pair_gradient,) = call(
        pair_gradient_kernel,
        "pair_gradient",
        3.0,
        [pair, late, gradient, in_gain, w_in],
        [VMEM] * 5,
        [shape_of(block, bf16)],
    )
    grad_w_in, grad_w_out = call(
        weights_kernel,
        "weight_gradients",
        0.5,
        [summed_early, *terms],
        [VMEM] * 3,
        [shape_of(w_in.shape, f32), shape_of(w_out.shape, f32)],
    )
    return (update, pair_gradient, grad_w_in, grad_w_out)


def solution(mesh):
    placed = (
        P(("grp", "row"), "col", None),
        P(("grp", "row"), "col", None),
        P("grp"),
        P(),
        P(),
        P(),
        P(),
        P(),
        P(),
    )
    return jax.shard_map(
        shards,
        mesh=mesh,
        in_specs=placed,
        out_specs=(
            P(("grp", "row"), "col", None),
            P(("grp", "row"), "col", None),
            P("grp", None),
            P("grp", None),
        ),
        check_vma=False,
    )
```

```python
import functools
import math

import jax
import jax.numpy as jnp
from jax import lax
from jax.experimental import pallas as pl
from jax.experimental.pallas import tpu as pltpu
from jax.sharding import PartitionSpec as P

eps = 1e-05
f32 = jnp.float32
bf16 = jnp.bfloat16
VMEM = pl.BlockSpec(memory_space=pltpu.VMEM)
SMEM = pl.BlockSpec(memory_space=pltpu.SMEM)
ANY = pl.BlockSpec(memory_space=pl.ANY)
MIB = 1 << 20


def layer_norm_backward(output_gradient, standardized_input, inverse_deviation, norm_gain):
    scaled_output = output_gradient * norm_gain
    first_operand = jnp.mean(scaled_output, axis=-1, keepdims=True)
    second_operand = jnp.mean(scaled_output * standardized_input, axis=-1, keepdims=True)
    return inverse_deviation * (scaled_output - first_operand - standardized_input * second_operand)


def standardize(values):
    centered = values - jnp.mean(values, axis=-1, keepdims=True)
    inverse = lax.rsqrt(jnp.mean(centered * centered, axis=-1, keepdims=True) + eps)
    return centered * inverse, inverse


def dot(a, b, ca, cb):
    return lax.dot_general(a, b, (((ca,), (cb,)), ((), ())), preferred_element_type=f32)


def ring_order(row_count):
    if row_count == 8:
        return [0, 2, 4, 6, 7, 5, 3, 1]
    return list(range(row_count))


def ring_place(row_count, row):
    if row_count == 8:
        return jnp.where(row % 2 == 0, row // 2, row_count - 1 - row // 2)
    return row


def ring_row(row_count, place):
    if row_count == 8:
        return jnp.where(place < row_count // 2, 2 * place, 2 * (row_count - 1 - place) + 1)
    return place


def half_index(row_count, offset, letter):
    place = ring_place(row_count, lax.axis_index("row"))
    return ring_row(row_count, (place + offset + row_count) % row_count) * 2 + letter


def arrival_slot(row_count, index):
    hops = row_count // 2
    letter = index % 2
    apart = ring_place(row_count, index // 2) - ring_place(row_count, lax.axis_index("row"))
    apart = (apart + row_count) % row_count
    near = jnp.where(letter == 0, row_count - apart, apart)
    first = 4 * near - 2 + letter
    second = 4 * (row_count - near) + 1 - letter
    return jnp.where(apart == 0, letter, jnp.where(near <= hops, first, second))


def present_count(row_count, lengths, slot, short, where):
    start = half_index(row_count, *where) * short
    return jnp.clip(lengths[start // slot] - start % slot, 0, short)


def swap_col(x):
    return lax.ppermute(x, "col", [(0, 1), (1, 0)])


def add(a, b):
    return (a.astype(f32) + b.astype(f32)).astype(bf16)


def exchanges(x, row_count):
    other = swap_col(x)
    yield x, other
    step = 1
    while step < row_count:
        x = add(x, other)
        other = lax.ppermute(x, "row", [(r, r ^ step) for r in range(row_count)])
        yield x, other
        step *= 2


def call(kernel, name, args, specs, outs, scratch=(), after=(), microseconds=0, limit=0):
    held = sum(a.size * a.dtype.itemsize for a, s in zip(args, specs) if s is VMEM)
    after = [x for x in after if x is not None]
    held += sum(int(o.size) * o.dtype.itemsize for o in outs)
    held += sum(math.prod(s.inner_aval.shape) * 4 for s in scratch)

    def body(*refs):
        kernel(*refs[: len(args)], *refs[len(args) + len(after) :])

    return pl.pallas_call(
        body,
        out_shape=list(outs),
        in_specs=list(specs) + [ANY] * len(after),
        out_specs=[VMEM] * len(outs),
        scratch_shapes=list(scratch),
        compiler_params=pltpu.CompilerParams(vmem_limit_bytes=limit or min(56 * MIB, held * 5 // 4 + 6 * MIB)),
        cost_estimate=pl.CostEstimate(
            flops=int(microseconds * 1.1e9) + 1024, bytes_accessed=1024, transcendentals=0
        ),
        name=name,
    )(*args, *after)


def tiles(half):
    return [(k, min(16, half - k)) for k in range(0, half, 16)]


def parts(short):
    return [(0, (short + 1) // 2), ((short + 1) // 2, short)]


def joined(terms):
    chains = [terms[0::2], terms[1::2]]
    sums = []
    for chain in chains:
        total = chain[0]
        for term in chain[1:]:
            total = total + term
        sums.append(total.astype(f32))
    return sums[0] + sums[1]


def wide_row(ref, *at):
    return jnp.broadcast_to(ref[at], (16, ref.shape[-1])).astype(bf16)


def shape_of(dims, dtype):
    return jax.ShapeDtypeStruct(dims, dtype)


def present_row(lengths, slot, position):
    return (position % slot < lengths[position // slot]).astype(f32)


def present_columns(lengths, slot, half):
    at = lax.axis_index("col") * half + lax.broadcasted_iota(jnp.int32, (half, 128), 0)
    chain = at // slot
    held = jnp.zeros((half, 128), jnp.int32)
    for c in range(lengths.shape[0]):
        held = jnp.where(chain == c, lengths[c], held)
    return (at - chain * slot < held).astype(f32)


def first_row(here):
    return lax.axis_index("row") * here


def input_kernel(slot, *refs):
    given, (right_a, right_b, normed), held, (mask, sems) = (
        refs[:5],
        refs[5:8],
        refs[8:13],
        refs[13:],
    )
    copies = [
        pltpu.make_async_copy(source, target, sems.at[at])
        for at, (source, target) in enumerate(zip(given, held))
    ]
    for copy in copies:
        copy.start()
    for copy in copies:
        copy.wait()
    lengths, pair, gain, bias, w = held
    here, half, hidden = pair.shape
    mask[...] = present_columns(lengths, slot, half)

    for i in range(here):
        standard, _ = standardize(pair[i].astype(f32))
        values = (standard * gain[...] + bias[...]).astype(bf16)
        normed[i] = values
        proj = dot(values, w[:, 2 * hidden : 4 * hidden], 1, 0)
        shown = mask[...] * present_row(lengths, slot, first_row(here) + i)
        gated = jax.nn.sigmoid(proj[:, :hidden]) * proj[:, hidden:]
        out, at = (right_a, i) if i < here // 2 else (right_b, i - here // 2)
        out[at] = (shown * gated).astype(bf16)


def by_rows(here, body):
    def step(t, carry):
        for x in range(here // 2):
            body(t * (here // 2) + x)
        return carry

    lax.fori_loop(0, 2, step, 0)


def left_kernel(slot, lengths, normed, cotangent, w, left, outs, mask):
    here, half, hidden = normed.shape
    halves, _, padded, _ = outs.shape
    short = half // halves
    mask[...] = present_columns(lengths, slot, half)

    def body(i):
        proj = dot(normed[i], w[:, : 2 * hidden], 1, 0)
        shown = mask[...] * present_row(lengths, slot, first_row(here) + i)
        gated = shown * jax.nn.sigmoid(proj[:, :hidden]) * proj[:, hidden:]
        left[i] = gated.astype(bf16)
        gate = jax.nn.sigmoid(dot(normed[i], w[:, 4 * hidden :], 1, 0))
        grads = cotangent[i].astype(f32) * gate
        empty = jnp.zeros((padded - short, hidden), f32)
        for m in range(halves):
            part = grads[m * short : (m + 1) * short]
            outs[m, i] = jnp.concatenate([part, empty], axis=0).astype(bf16)

    by_rows(here, body)


def triangle_kernel(row_count, slot, halves, arrays, lengths, left, *refs):
    rights, (out, partial, rows) = refs[:arrays], refs[arrays:]
    here, half, hidden = left.shape
    padded = out.shape[2]
    short = here // 2
    for s, (array, first, place) in enumerate(halves):
        rows[...] = jnp.zeros_like(rows)
        right = rights[array]

        def column(j, right=right, first=first):
            buffer = j % partial.shape[0]
            held = [right[first + j, pl.ds(k, size), :] for k, size in tiles(half)]
            for i in range(here):
                products = [
                    left[i, pl.ds(k, size), :] * held[at]
                    for at, (k, size) in enumerate(tiles(half))
                ]
                rest = products.pop() if half % 16 else None
                total = joined(products)
                total = total[:8] + total[8:]
                if rest is not None:
                    total += rest.astype(f32)
                partial[buffer, pl.ds(8 * i, 8), :] = total
            total = partial[buffer, pl.ds(0, here, stride=8), :]
            for sub in range(1, 8):
                total += partial[buffer, pl.ds(sub, here, stride=8), :]
            rows[pl.ds(j, here, stride=padded), :] = total

        present = present_count(row_count, lengths, slot, short, place)
        for low, high in parts(short):

            @pl.when(present > low)
            def _(low=low, high=high, column=column):
                for j in range(low, high):
                    column(j)

        out[s] = rows[...].astype(bf16).reshape(here, padded, hidden)


def triangle(row_count, slot, halves, lengths, left, rights, padded, after):
    count, (here, half, hidden) = len(halves), left.shape
    return call(
        functools.partial(triangle_kernel, row_count, slot, halves, len(rights)),
        "triangle",
        [lengths, left, *rights],
        [SMEM] + [VMEM] * (len(rights) + 1),
        [shape_of((count, here, padded, hidden), bf16)],
        [
            pltpu.VMEM((3, here * 8, hidden), f32),
            pltpu.VMEM((here * padded, hidden), f32),
        ],
        after,
        microseconds=5,
    )[0]


def triangle_norm_kernel(
    row_count, places, mine, other, mine_out, other_out, w_out, gain, bias, grad, normed
):
    count, here, padded, hidden = mine.shape
    flat = (here * padded, hidden)

    for s in range(count):
        index = half_index(row_count, *places[s])
        outs = jnp.where(
            index // row_count == lax.axis_index("col"),
            mine_out[index % row_count],
            other_out[index % row_count],
        )
        total = (mine[s].astype(f32) + other[s].astype(f32)).reshape(flat)
        standard, inverse = standardize(total)
        normed[s] = (standard * gain[...] + bias[...]).astype(bf16).reshape(here, padded, hidden)
        grad_norm = dot(outs.reshape(flat), w_out[...], 1, 1)
        result = layer_norm_backward(grad_norm, standard, inverse, gain[...])
        grad[s] = result.astype(bf16).reshape(here, padded, hidden)


def triangle_norm(row_count, places, mine, other, outs, w_out, gain, bias, after):
    return call(
        functools.partial(triangle_norm_kernel, row_count, places),
        "triangle_norm",
        [mine, other, *outs, w_out, gain, bias],
        [VMEM] * 7,
        [shape_of(mine.shape, bf16)] * 2,
        (),
        after,
    )


def hop_kernel(row_count, slot, places, picks, carried, lengths, left, *refs):
    count = len(picks)
    grads, refs = refs[:count], refs[count:]
    arrived, refs = refs[: count * carried], refs[count * carried :]
    outs, wide = refs[:count], refs[count]
    here, half, hidden = left.shape
    short = outs[0].shape[0]
    for s in range(count):
        wide[...] = grads[s][picks[s]].astype(f32)
        out = outs[s]

        def columns(at, s=s, out=out):
            totals = []
            for j in at:
                total = []
                for k, size in tiles(half):
                    start = jnp.zeros((size, hidden), f32)
                    for more in range(carried):
                        start += arrived[s + more * count][j, pl.ds(k, size), :].astype(f32)
                    total.append(start)
                totals.append(total)
            for low in range(0, here, short):
                chosen = range(low, min(low + short, here))
                weights = [[wide_row(wide, i, pl.ds(j, 1)) for i in chosen] for j in at]
                for t, (k, size) in enumerate(tiles(half)):
                    held = [left[i, pl.ds(k, size), :] for i in chosen]
                    for total, weight in zip(totals, weights):
                        total[t] += joined([w[:size] * h for w, h in zip(weight, held)])
            for j, total in zip(at, totals):
                for t, (k, size) in enumerate(tiles(half)):
                    out[j, pl.ds(k, size), :] = total[t].astype(out.dtype)

        present = present_count(row_count, lengths, slot, short, places[s])
        for low, high in parts(short):

            @pl.when(present > low)
            def _(low=low, high=high, columns=columns):
                for j in range(low, high, 2):
                    columns(range(j, min(j + 2, high)))

            @pl.when(present <= low)
            def _(low=low, high=high, out=out):
                out[pl.ds(low, high - low)] = jnp.zeros((high - low, half, hidden), out.dtype)


def hop(row_count, slot, places, lengths, left, grads, picks, arrived, short, dtype=bf16, after=()):
    here, half, hidden = left.shape
    count = len(grads)
    carried = len(arrived) // count
    return call(
        functools.partial(hop_kernel, row_count, slot, places, picks, carried),
        "scatter_hop",
        [lengths, left, *grads, *arrived],
        [SMEM] + [VMEM] * (1 + count + len(arrived)),
        [shape_of((short, half, hidden), dtype)] * count,
        [pltpu.VMEM(grads[0].shape[1:], f32)],
        after,
    )


def left_gradient_kernel(halves, picks, arrays, carried, grads, *refs):
    count = len(picks)
    rights, refs = refs[:arrays], refs[arrays:]
    before, (out, wide) = refs[:carried], refs[carried:]
    here, half, hidden = out.shape
    short = here // 2
    for s, pick in enumerate(picks):
        wide[s] = grads[pick].astype(f32)

    def row(pair, carry):
        rows = (2 * pair, 2 * pair + 1)
        for s, pick in enumerate(picks):
            array, first, _ = halves[pick]
            weights = [[wide_row(wide, s, i, pl.ds(j, 1)) for j in range(short)] for i in rows]
            for k, size in tiles(half):
                held = [rights[array][first + j, pl.ds(k, size), :] for j in range(short)]
                for i, weight in zip(rows, weights):
                    total = joined([w[:size] * h for w, h in zip(weight, held)])
                    if s:
                        total += out[i, pl.ds(k, size), :]
                    elif carried:
                        total += before[0][i, pl.ds(k, size), :]
                    out[i, pl.ds(k, size), :] = total
        return carry

    lax.fori_loop(0, here // 2, row, 0)


def left_gradient(halves, picks, grads, rights, before, after):
    count, here = len(picks), grads.shape[1]
    half, hidden = rights[0].shape[1:]
    return call(
        functools.partial(left_gradient_kernel, halves, picks, len(rights), len(before)),
        "left_gradient",
        [grads, *rights, *before],
        [VMEM] * (1 + len(rights) + len(before)),
        [shape_of((here, half, hidden), f32)],
        [pltpu.VMEM((count,) + grads.shape[1:], f32)],
        after,
    )[0]


def output_kernel(
    row_count, slot, counts, rows, before, lengths, normed, cotangent, grad_left, w, w_out, *refs
):
    outs, norms, refs = refs[0], refs[1 : 1 + len(counts)], refs[1 + len(counts) :]
    earlier, (update, gradient, weights, mask, picked, total) = refs[:before], refs[before:]
    here, half, hidden = normed.shape
    halves, _, padded, _ = picked.shape
    short = half // halves
    mask[...] = present_columns(lengths, slot, half)
    total[...] = earlier[0][...] if before else jnp.zeros_like(total)
    for m in range(halves):
        low = 0
        stands = arrival_slot(row_count, lax.axis_index("col") * row_count + m)
        for norm, count in zip(norms, counts):

            @pl.when((stands >= low) & (stands < low + count))
            def _(m=m, norm=norm, low=low, stands=stands):
                picked[m] = norm[stands - low, pl.ds(rows[0], len(rows))]

            low += count

    for at, i in enumerate(rows):
        values = normed[i]
        proj = dot(values, w[:, : 2 * hidden], 1, 0)
        sig_left = jax.nn.sigmoid(proj[:, :hidden])
        val_left = proj[:, hidden:]
        gate = jax.nn.sigmoid(dot(values, w[:, 4 * hidden :], 1, 0))
        tri = picked[:, at].reshape(halves * padded, hidden)
        product = dot(tri, w_out[...], 1, 0)
        projected = jnp.concatenate(
            [product[m * padded : m * padded + short] for m in range(halves)], axis=0
        )
        update[at] = (gate * projected).astype(bf16)
        grad_gate = (cotangent[i].astype(f32) * projected * gate * (1.0 - gate)).astype(bf16)
        shown = mask[...] * present_row(lengths, slot, first_row(here) + i)
        masked = grad_left[i] * shown
        grads = jnp.concatenate(
            [masked * val_left * sig_left * (1.0 - sig_left), masked * sig_left], axis=1
        ).astype(bf16)
        gradient[at] = dot(grads, w[:, : 2 * hidden], 1, 1) + dot(
            grad_gate, w[:, 4 * hidden :], 1, 1
        )
        total[:, : 2 * hidden] += dot(values, grads, 0, 0)
        total[:, 2 * hidden : 3 * hidden] += dot(values, grad_gate, 0, 0)
        total[:, 3 * hidden :] += dot(tri, outs[:, i].reshape(halves * padded, hidden), 0, 0)

    weights[...] = total[...].astype(weights.dtype)


def right_gradient_kernel(slot, lengths, normed, w, own_a, own_b, *refs):
    arrived, (grads, weights, mask, total) = refs[:4], refs[4:]
    here, half, hidden = normed.shape
    short = here // 2
    mask[...] = present_columns(lengths, slot, half)
    total[...] = jnp.zeros_like(total)

    for own, others, first in ((own_a, arrived[:2], 0), (own_b, arrived[2:], short)):
        for t in range(short):
            j = first + t
            values = normed[j]
            proj = dot(values, w[:, 2 * hidden : 4 * hidden], 1, 0)
            sig_right = jax.nn.sigmoid(proj[:, :hidden])
            val_right = proj[:, hidden:]
            shown = mask[...] * present_row(lengths, slot, first_row(here) + j)
            masked = shown * (own[t] + others[0][t].astype(f32) + others[1][t].astype(f32))
            result = jnp.concatenate(
                [masked * val_right * sig_right * (1.0 - sig_right), masked * sig_right], axis=1
            ).astype(bf16)
            grads[j] = result
            total[...] += dot(values, result, 0, 0)
    weights[...] = total[...].astype(bf16)


def pair_gradient_kernel(pair, grads, gain, w, *refs):
    gradients, out = refs[:-1], refs[-1]
    hidden = pair.shape[2]

    i = 0
    for gradient in gradients:
        for at in range(gradient.shape[0]):
            standard, inverse = standardize(pair[i].astype(f32))
            total = gradient[at] + dot(grads[i], w[:, 2 * hidden : 4 * hidden], 1, 1)
            out[i] = layer_norm_backward(total, standard, inverse, gain[...]).astype(bf16)
            i += 1


def weights_kernel(early, mine, other, w_in, w_out):
    hidden = w_out.shape[0]
    w_in[:, : 2 * hidden] = early[:, : 2 * hidden].astype(f32)
    late = mine[...].astype(f32) + other[...].astype(f32)
    w_in[:, 2 * hidden : 4 * hidden] = late.astype(bf16).astype(f32)
    w_in[:, 4 * hidden :] = early[:, 2 * hidden : 3 * hidden].astype(f32)
    w_out[...] = early[:, 3 * hidden :].astype(f32)


def shards(
    pair,
    cotangent,
    chain_lengths,
    input_norm_gain,
    input_norm_bias,
    w_in,
    output_norm_gain,
    output_norm_bias,
    w_out,
):
    here, half, channels = pair.shape
    hidden = w_out.shape[0]
    row_count = lax.axis_size("row")
    slot = here * row_count // chain_lengths.shape[0]
    order = ring_order(row_count)
    short = here // 2
    padded = (short + 15) // 16 * 16
    forward = [(order[p], order[(p + 1) % row_count]) for p in range(row_count)]
    backward = [(order[p], order[(p - 1) % row_count]) for p in range(row_count)]
    in_gain, in_bias = input_norm_gain.reshape(1, -1), input_norm_bias.reshape(1, -1)
    out_gain, out_bias = output_norm_gain.reshape(1, -1), output_norm_bias.reshape(1, -1)
    block = (here, half, hidden)
    mask = pltpu.VMEM((half, 128), f32)

    def ahead(x):
        return lax.ppermute(x, "row", forward)

    def behind(x):
        return lax.ppermute(x, "row", backward)

    right_a, right_b, normed = call(
        functools.partial(input_kernel, slot),
        "input_side",
        [chain_lengths, pair, in_gain, in_bias, w_in],
        [pl.BlockSpec(memory_space=pltpu.HBM)] * 5,
        [shape_of((short, half, hidden), bf16)] * 2 + [shape_of(block, bf16)],
        [
            pltpu.SMEM(chain_lengths.shape, jnp.int32),
            pltpu.VMEM(block, bf16),
            pltpu.VMEM(in_gain.shape, f32),
            pltpu.VMEM(in_bias.shape, f32),
            pltpu.VMEM(w_in.shape, bf16),
            mask,
            pltpu.SemaphoreType.DMA((5,)),
        ],
        limit=60 * MIB,
    )

    hops = row_count // 2
    groups = [[right_a, right_b]]
    halves = [[(0, 0, (0, 0)), (1, 0, (0, 1))]]
    steps = 2 * hops
    for s in range(1, hops + 1):
        halves.append([(0, 0, (-s, 0)), (1, 0, (s, 1))])
        if s < hops:
            halves.append([(0, 0, (-s, 1)), (1, 0, (s, 0))])

    def gather(x, y):
        groups.append([ahead(x), behind(y)])

    gather(right_a, right_b)
    gather(right_b, right_a)
    left, mine_out = call(
        functools.partial(left_kernel, slot),
        "left_side",
        [chain_lengths, normed, cotangent, w_in],
        [SMEM] + [VMEM] * 3,
        [shape_of(block, bf16), shape_of((row_count, here, padded, hidden), bf16)],
        [mask],
        microseconds=4,
    )
    other_out = swap_col(mine_out)

    norms, grads, partials, others = [], [], [], []
    last = [left]
    pieces = []

    def triangles(s):
        partials.append(
            triangle(row_count, slot, halves[s], chain_lengths, left, groups[s], padded, last)
        )
        others.append(swap_col(partials[s]))
        last[:] = [partials[s]]

    def normal(s):
        places = [place for _, _, place in halves[s]]
        grad, norm = triangle_norm(
            row_count, places, partials[s], others[s], [mine_out, other_out], w_out, out_gain, out_bias, last
        )
        grads.append(grad)
        norms.append(norm)
        last[:] = [grad]

    def add_left(s, picks=(0, 1)):
        pieces[:] = [
            left_gradient(halves[s], picks, grads[s], groups[s], pieces[:], last)
        ]
        last[:] = pieces

    def scatter(s, picks, arrived, dtype=bf16):
        x, y = hop(
            row_count,
            slot,
            [halves[s][pick][2] for pick in picks],
            chain_lengths,
            left,
            [grads[s]] * 2,
            picks,
            arrived,
            short,
            dtype,
            last,
        )
        last[:] = [x]
        return x, y

    arrived = {0: [], 1: []}

    def send(s, chain):
        group = 2 * s - 1 + chain
        x, y = scatter(group, [0, 1], arrived[chain])
        arrived[chain] = [behind(x), ahead(y)]

    updates, gradients, totals = [], [], []
    cuts = [here * at // 4 for at in range(5)]

    def output_piece(at):
        rows = range(cuts[at], cuts[at + 1])
        results = call(
            functools.partial(
                output_kernel, row_count, slot, [len(h) for h in halves], rows, len(totals[-1:])
            ),
            "output_side",
            [chain_lengths, normed, cotangent, pieces[0], w_in, w_out, mine_out]
            + norms
            + totals[-1:],
            [SMEM] + [VMEM] * (6 + len(norms) + len(totals[-1:])),
            [
                shape_of((len(rows), half, hidden), bf16),
                shape_of((len(rows), half, hidden), f32),
                shape_of((channels, 4 * hidden), bf16 if at == 3 else f32),
            ],
            [
                mask,
                pltpu.VMEM((row_count, len(rows), padded, hidden), bf16),
                pltpu.VMEM((channels, 4 * hidden), f32),
            ],
            last,
        )
        for kept, result in zip((updates, gradients, totals), results):
            kept.append(result)
        last[:] = results[:1]

    for s in range(steps):
        if s:
            if s + 2 < steps:
                x, y, _ = lax.optimization_barrier((*groups[s], last[0]))
                gather(x, y)
            triangles(s)
            add_left(s - 1)
        else:
            triangles(s)
        normal(s)
        if s == steps - 2:
            send(hops - 1, 1)
    send(hops, 0)
    add_left(steps - 1)
    output_piece(0)
    send(hops - 2, 1)
    output_piece(1)
    sums = None
    for s in range(hops - 1, 0, -1):
        if s == 1:
            own_a, own_b = scatter(0, [0, 1], [], f32)
        send(s, 0)
        if sums is None:
            output_piece(2)
            output_piece(3)
            sums = exchanges(totals[-1], row_count)
            terms = next(sums)
        for chain in (1, 0):
            if chain and s > 2:
                last.append(terms[1])
                terms = next(sums, terms)
                send(s - 2, 1)
        last.append(terms[1])
        terms = next(sums, terms)
    update = jnp.concatenate(updates, axis=0)
    summed_early = add(*terms)
    arrived1, arrived2 = arrived[0], [arrived[1][1], arrived[1][0]]

    late, weights = call(
        functools.partial(right_gradient_kernel, slot),
        "right_gradient",
        [chain_lengths, normed, w_in, own_a, own_b]
        + [arrived1[0], arrived2[0], arrived1[1], arrived2[1]],
        [SMEM] + [VMEM] * 8,
        [
            shape_of((here, half, 2 * hidden), bf16),
            shape_of((channels, 2 * hidden), bf16),
        ],
        [mask, pltpu.VMEM((channels, 2 * hidden), f32)],
        last,
    )
    *_, terms = exchanges(weights, row_count)
    (pair_gradient,) = call(
        pair_gradient_kernel,
        "pair_gradient",
        [pair, late, in_gain, w_in, *gradients],
        [VMEM] * (4 + len(gradients)),
        [shape_of(block, bf16)],
        microseconds=3,
    )
    grad_w_in, grad_w_out = call(
        weights_kernel,
        "weight_gradients",
        [summed_early, *terms],
        [VMEM] * 3,
        [shape_of(w_in.shape, f32), shape_of(w_out.shape, f32)],
    )
    return (update, pair_gradient, grad_w_in, grad_w_out)


def solution(mesh):
    placed = (
        P(("grp", "row"), "col", None),
        P(("grp", "row"), "col", None),
        P("grp"),
        P(),
        P(),
        P(),
        P(),
        P(),
        P(),
    )
    return jax.shard_map(
        shards,
        mesh=mesh,
        in_specs=placed,
        out_specs=(
            P(("grp", "row"), "col", None),
            P(("grp", "row"), "col", None),
            P("grp", None),
            P("grp", None),
        ),
        check_vma=False,
    )
```

```python
import functools
import math

import jax
import jax.numpy as jnp
from jax import lax
from jax.experimental import pallas as pl
from jax.experimental.pallas import tpu as pltpu
from jax.sharding import PartitionSpec as P

eps = 1e-05
f32 = jnp.float32
bf16 = jnp.bfloat16
VMEM = pl.BlockSpec(memory_space=pltpu.VMEM)
SMEM = pl.BlockSpec(memory_space=pltpu.SMEM)
ANY = pl.BlockSpec(memory_space=pl.ANY)
MIB = 1 << 20


def layer_norm_backward(output_gradient, standardized_input, inverse_deviation, norm_gain):
    scaled_output = output_gradient * norm_gain
    first_operand = jnp.mean(scaled_output, axis=-1, keepdims=True)
    second_operand = jnp.mean(scaled_output * standardized_input, axis=-1, keepdims=True)
    return inverse_deviation * (scaled_output - first_operand - standardized_input * second_operand)


def standardize(values):
    centered = values - jnp.mean(values, axis=-1, keepdims=True)
    inverse = lax.rsqrt(jnp.mean(centered * centered, axis=-1, keepdims=True) + eps)
    return centered * inverse, inverse


def dot(a, b, ca, cb):
    return lax.dot_general(a, b, (((ca,), (cb,)), ((), ())), preferred_element_type=f32)


def ring_order(row_count):
    if row_count == 8:
        return [0, 2, 4, 6, 7, 5, 3, 1]
    return list(range(row_count))


def ring_place(row_count, row):
    if row_count == 8:
        return jnp.where(row % 2 == 0, row // 2, row_count - 1 - row // 2)
    return row


def ring_row(row_count, place):
    if row_count == 8:
        return jnp.where(place < row_count // 2, 2 * place, 2 * (row_count - 1 - place) + 1)
    return place


def half_index(row_count, offset, letter):
    place = ring_place(row_count, lax.axis_index("row"))
    return ring_row(row_count, (place + offset + row_count) % row_count) * 2 + letter


def arrival_slot(row_count, index):
    hops = row_count // 2
    letter = index % 2
    apart = ring_place(row_count, index // 2) - ring_place(row_count, lax.axis_index("row"))
    apart = (apart + row_count) % row_count
    near = jnp.where(letter == 0, row_count - apart, apart)
    first = 4 * near - 2 + letter
    second = 4 * (row_count - near) - 2 + 3 - letter
    return jnp.where(apart == 0, letter, jnp.where(near <= hops, first, second))


def present_count(row_count, lengths, slot, short, where):
    start = half_index(row_count, *where) * short
    return jnp.clip(lengths[start // slot] - start % slot, 0, short)


def swap_col(x):
    return lax.ppermute(x, "col", [(0, 1), (1, 0)])


def add(a, b):
    return (a.astype(f32) + b.astype(f32)).astype(bf16)


def call(kernel, name, args, specs, outs, scratch=(), after=(), microseconds=0, limit=0):
    held = sum(a.size * a.dtype.itemsize for a, s in zip(args, specs) if s is VMEM)
    after = [x for x in after if x is not None]
    held += sum(int(o.size) * o.dtype.itemsize for o in outs)
    held += sum(math.prod(s.inner_aval.shape) * 4 for s in scratch)

    def body(*refs):
        kernel(*refs[: len(args)], *refs[len(args) + len(after) :])

    return pl.pallas_call(
        body,
        out_shape=list(outs),
        in_specs=list(specs) + [ANY] * len(after),
        out_specs=[VMEM] * len(outs),
        scratch_shapes=list(scratch),
        compiler_params=pltpu.CompilerParams(vmem_limit_bytes=limit or min(56 * MIB, held * 5 // 4 + 6 * MIB)),
        cost_estimate=pl.CostEstimate(
            flops=int(microseconds * 1.1e9) + 1024, bytes_accessed=1024, transcendentals=0
        ),
        name=name,
    )(*args, *after)


def tiles(half):
    return [(k, min(16, half - k)) for k in range(0, half, 16)]


def parts(short):
    return [(0, (short + 1) // 2), ((short + 1) // 2, short)]


def joined(terms):
    chains = [terms[0::2], terms[1::2]]
    sums = []
    for chain in chains:
        total = chain[0]
        for term in chain[1:]:
            total = total + term
        sums.append(total.astype(f32))
    return sums[0] + sums[1]


def wide_row(ref, *at):
    return jnp.broadcast_to(ref[at], (16, ref.shape[-1])).astype(bf16)


def shape_of(dims, dtype):
    return jax.ShapeDtypeStruct(dims, dtype)


def present_row(lengths, slot, position):
    return (position % slot < lengths[position // slot]).astype(f32)


def present_columns(lengths, slot, half):
    at = lax.axis_index("col") * half + lax.broadcasted_iota(jnp.int32, (half, 128), 0)
    chain = at // slot
    held = jnp.zeros((half, 128), jnp.int32)
    for c in range(lengths.shape[0]):
        held = jnp.where(chain == c, lengths[c], held)
    return (at - chain * slot < held).astype(f32)


def first_row(here):
    return lax.axis_index("row") * here


def input_kernel(slot, lengths, pair, gain, bias, w, right, normed, mask):
    here, half, hidden = pair.shape
    mask[...] = present_columns(lengths, slot, half)

    for i in range(here):
        standard, _ = standardize(pair[i].astype(f32))
        values = (standard * gain[...] + bias[...]).astype(bf16)
        normed[i] = values
        proj = dot(values, w[:, 2 * hidden : 4 * hidden], 1, 0)
        shown = mask[...] * present_row(lengths, slot, first_row(here) + i)
        gated = jax.nn.sigmoid(proj[:, :hidden]) * proj[:, hidden:]
        right[i] = (shown * gated).astype(bf16)


def by_rows(here, body):
    def step(t, carry):
        for x in range(here // 2):
            body(t * (here // 2) + x)
        return carry

    lax.fori_loop(0, 2, step, 0)


def left_kernel(slot, lengths, normed, cotangent, w, left, outs, mask):
    here, half, hidden = normed.shape
    halves, _, padded, _ = outs.shape
    short = half // halves
    mask[...] = present_columns(lengths, slot, half)

    def body(i):
        proj = dot(normed[i], w[:, : 2 * hidden], 1, 0)
        shown = mask[...] * present_row(lengths, slot, first_row(here) + i)
        gated = shown * jax.nn.sigmoid(proj[:, :hidden]) * proj[:, hidden:]
        left[i, pl.ds(0, half), :] = gated.astype(bf16)
        if left.shape[1] > half:
            left[i, pl.ds(half, left.shape[1] - half), :] = jnp.zeros(
                (left.shape[1] - half, hidden), bf16
            )
        gate = jax.nn.sigmoid(dot(normed[i], w[:, 4 * hidden :], 1, 0))
        grads = cotangent[i].astype(f32) * gate
        empty = jnp.zeros((padded - short, hidden), f32)
        for m in range(halves):
            part = grads[m * short : (m + 1) * short]
            outs[m, i] = jnp.concatenate([part, empty], axis=0).astype(bf16)

    by_rows(here, body)


def triangle_kernel(row_count, slot, halves, arrays, lengths, left, *refs):
    rights, (out, rows, which) = refs[:arrays], refs[arrays:]
    here, deep, hidden = left.shape
    half = rights[0].shape[1]
    padded = out.shape[2]
    short = here // 2
    row = lax.broadcasted_iota(jnp.int32, which.shape, 0)
    lane = lax.broadcasted_iota(jnp.int32, which.shape, 1)
    which[...] = ((lane >= row * deep) & (lane < (row + 1) * deep)).astype(f32).astype(bf16)
    for s, (array, first, place) in enumerate(halves):
        rows[...] = jnp.zeros_like(rows)

        def column(j, carry, right=rights[array], first=first):
            held = right[first + j]
            if deep > half:
                held = jnp.concatenate([held, jnp.zeros((deep - half, hidden), bf16)], axis=0)
            products = jnp.concatenate([left[i] * held for i in range(here)], axis=0)
            total = dot(which[...], products, 1, 0)
            rows[pl.ds(j, here, stride=padded), :] = total[:here]
            return carry

        present = present_count(row_count, lengths, slot, short, place)
        lax.fori_loop(0, present, column, 0)
        out[s] = rows[...].astype(bf16).reshape(here, padded, hidden)


def triangle(row_count, slot, halves, lengths, left, rights, padded, after):
    count, (here, deep, hidden) = len(halves), left.shape
    return call(
        functools.partial(triangle_kernel, row_count, slot, halves, len(rights)),
        "triangle",
        [lengths, left, *rights],
        [SMEM] + [VMEM] * (len(rights) + 1),
        [shape_of((count, here, padded, hidden), bf16)],
        [
            pltpu.VMEM((here * padded, hidden), f32),
            pltpu.VMEM(((here + 15) // 16 * 16, here * deep), bf16),
        ],
        after,
    )[0]


def triangle_norm_kernel(
    row_count, places, mine, other, mine_out, other_out, w_out, gain, bias, grad, normed
):
    count, here, padded, hidden = mine.shape
    flat = (here * padded, hidden)

    for s in range(count):
        index = half_index(row_count, *places[s])
        outs = jnp.where(
            index // row_count == lax.axis_index("col"),
            mine_out[index % row_count],
            other_out[index % row_count],
        )
        total = (mine[s].astype(f32) + other[s].astype(f32)).reshape(flat)
        standard, inverse = standardize(total)
        normed[s] = (standard * gain[...] + bias[...]).astype(bf16).reshape(here, padded, hidden)
        grad_norm = dot(outs.reshape(flat), w_out[...], 1, 1)
        result = layer_norm_backward(grad_norm, standard, inverse, gain[...])
        grad[s] = result.astype(bf16).reshape(here, padded, hidden)


def triangle_norm(row_count, places, mine, other, outs, w_out, gain, bias, after):
    return call(
        functools.partial(triangle_norm_kernel, row_count, places),
        "triangle_norm",
        [mine, other, *outs, w_out, gain, bias],
        [VMEM] * 7,
        [shape_of(mine.shape, bf16)] * 2,
        (),
        after,
    )


def hop_kernel(row_count, slot, places, picks, carried, lengths, left, *refs):
    count = len(picks)
    grads, refs = refs[:count], refs[count:]
    arrived, refs = refs[: count * carried], refs[count * carried :]
    outs, wide = refs[:count], refs[count]
    here = left.shape[0]
    short, half, hidden = outs[0].shape
    for s in range(count):
        wide[...] = grads[s][picks[s]].astype(f32)
        out = outs[s]

        def columns(at, s=s, out=out):
            totals = []
            for j in at:
                total = []
                for k, size in tiles(half):
                    start = jnp.zeros((size, hidden), f32)
                    for more in range(carried):
                        start += arrived[s + more * count][j, pl.ds(k, size), :].astype(f32)
                    total.append(start)
                totals.append(total)
            for low in range(0, here, short):
                chosen = range(low, min(low + short, here))
                weights = [[wide_row(wide, i, pl.ds(j, 1)) for i in chosen] for j in at]
                for t, (k, size) in enumerate(tiles(half)):
                    held = [left[i, pl.ds(k, size), :] for i in chosen]
                    for total, weight in zip(totals, weights):
                        total[t] += joined([w[:size] * h for w, h in zip(weight, held)])
            for j, total in zip(at, totals):
                for t, (k, size) in enumerate(tiles(half)):
                    out[j, pl.ds(k, size), :] = total[t].astype(out.dtype)

        present = present_count(row_count, lengths, slot, short, places[s])
        for low, high in parts(short):

            @pl.when(present > low)
            def _(low=low, high=high, columns=columns):
                for j in range(low, high, 2):
                    columns(range(j, min(j + 2, high)))

            @pl.when(present <= low)
            def _(low=low, high=high, out=out):
                out[pl.ds(low, high - low)] = jnp.zeros((high - low, half, hidden), out.dtype)


def hop(row_count, slot, places, lengths, left, grads, picks, arrived, out, dtype, after):
    count = len(grads)
    carried = len(arrived) // count
    return call(
        functools.partial(hop_kernel, row_count, slot, places, picks, carried),
        "scatter_hop",
        [lengths, left, *grads, *arrived],
        [SMEM] + [VMEM] * (1 + count + len(arrived)),
        [shape_of(out, dtype)] * count,
        [pltpu.VMEM(grads[0].shape[1:], f32)],
        after,
    )


def left_gradient_kernel(halves, picks, arrays, carried, grads, *refs):
    count = len(picks)
    rights, refs = refs[:arrays], refs[arrays:]
    before, (out, wide) = refs[:carried], refs[carried:]
    here, half, hidden = out.shape
    short = here // 2
    for s, pick in enumerate(picks):
        wide[s] = grads[pick].astype(f32)

    def row(pair, carry):
        rows = (2 * pair, 2 * pair + 1)
        for s, pick in enumerate(picks):
            array, first, _ = halves[pick]
            weights = [[wide_row(wide, s, i, pl.ds(j, 1)) for j in range(short)] for i in rows]
            for k, size in tiles(half):
                held = [rights[array][first + j, pl.ds(k, size), :] for j in range(short)]
                for i, weight in zip(rows, weights):
                    total = joined([w[:size] * h for w, h in zip(weight, held)])
                    if s:
                        total += out[i, pl.ds(k, size), :]
                    elif carried:
                        total += before[0][i, pl.ds(k, size), :]
                    out[i, pl.ds(k, size), :] = total
        return carry

    lax.fori_loop(0, here // 2, row, 0)


def left_gradient(halves, picks, grads, rights, before, after):
    count, here = len(picks), grads.shape[1]
    half, hidden = rights[0].shape[1:]
    return call(
        functools.partial(left_gradient_kernel, halves, picks, len(rights), len(before)),
        "left_gradient",
        [grads, *rights, *before],
        [VMEM] * (1 + len(rights) + len(before)),
        [shape_of((here, half, hidden), f32)],
        [pltpu.VMEM((count,) + grads.shape[1:], f32)],
        after,
    )[0]


def output_kernel(
    row_count, slot, counts, lengths, normed, cotangent, grad_left, w, w_out, outs, *refs
):
    norms, (update, gradient, total, mask, picked) = refs[: len(counts)], refs[len(counts) :]
    here, half, hidden = normed.shape
    halves, _, padded, _ = picked.shape
    short = half // halves
    mask[...] = present_columns(lengths, slot, half)
    total[...] = jnp.zeros_like(total)
    for m in range(halves):
        low = 0
        stands = arrival_slot(row_count, lax.axis_index("col") * row_count + m)
        for norm, count in zip(norms, counts):

            @pl.when((stands >= low) & (stands < low + count))
            def _(m=m, norm=norm, low=low, stands=stands):
                picked[m] = norm[stands - low]

            low += count

    def body(i):
        values = normed[i]
        proj = dot(values, w[:, : 2 * hidden], 1, 0)
        sig_left = jax.nn.sigmoid(proj[:, :hidden])
        val_left = proj[:, hidden:]
        gate = jax.nn.sigmoid(dot(values, w[:, 4 * hidden :], 1, 0))
        tri = picked[:, i].reshape(halves * padded, hidden)
        product = dot(tri, w_out[...], 1, 0)
        projected = jnp.concatenate(
            [product[m * padded : m * padded + short] for m in range(halves)], axis=0
        )
        update[i] = (gate * projected).astype(bf16)
        grad_gate = (cotangent[i].astype(f32) * projected * gate * (1.0 - gate)).astype(bf16)
        shown = mask[...] * present_row(lengths, slot, first_row(here) + i)
        masked = grad_left[i] * shown
        grads = jnp.concatenate(
            [masked * val_left * sig_left * (1.0 - sig_left), masked * sig_left], axis=1
        ).astype(bf16)
        gradient[i] = dot(grads, w[:, : 2 * hidden], 1, 1) + dot(
            grad_gate, w[:, 4 * hidden :], 1, 1
        )
        total[:, : 2 * hidden] += dot(values, grads, 0, 0)
        total[:, 2 * hidden : 3 * hidden] += dot(values, grad_gate, 0, 0)
        total[:, 3 * hidden :] += dot(tri, outs[:, i].reshape(halves * padded, hidden), 0, 0)

    by_rows(here, body)


def right_gradient_kernel(slot, lengths, normed, w, early, own_a, own_b, *refs):
    arrived, (grads, keep, give, mask, total) = refs[:4], refs[4:]
    here, half, hidden = normed.shape
    short = here // 2
    mask[...] = present_columns(lengths, slot, half)
    total[...] = jnp.zeros_like(total)

    for own, others, first in ((own_a, arrived[:2], 0), (own_b, arrived[2:], short)):
        for t in range(short):
            j = first + t
            values = normed[j]
            proj = dot(values, w[:, 2 * hidden : 4 * hidden], 1, 0)
            sig_right = jax.nn.sigmoid(proj[:, :hidden])
            val_right = proj[:, hidden:]
            shown = mask[...] * present_row(lengths, slot, first_row(here) + j)
            masked = shown * (own[t] + others[0][t].astype(f32) + others[1][t].astype(f32))
            result = jnp.concatenate(
                [masked * val_right * sig_right * (1.0 - sig_right), masked * sig_right], axis=1
            ).astype(bf16)
            grads[j] = result
            total[...] += dot(values, result, 0, 0)
    rows, wide = keep.shape[0], early.shape[1]
    col = lax.axis_index("col")
    for out, start in ((keep, col * rows), (give, (1 - col) * rows)):
        chosen = pl.ds(pl.multiple_of(start, rows), rows)
        out[:, :wide] = early[chosen, :].astype(bf16)
        out[:, wide:] = total[chosen, :].astype(bf16)


def pair_gradient_kernel(pair, grads, gain, w, *refs):
    gradients, out = refs[:-1], refs[-1]
    hidden = pair.shape[2]

    i = 0
    for gradient in gradients:
        for at in range(gradient.shape[0]):
            standard, inverse = standardize(pair[i].astype(f32))
            total = gradient[at] + dot(grads[i], w[:, 2 * hidden : 4 * hidden], 1, 1)
            out[i] = layer_norm_backward(total, standard, inverse, gain[...]).astype(bf16)
            i += 1


def weights_kernel(mine, other, w_in, w_out):
    rows, hidden = mine.shape[0], w_out.shape[0]
    col = lax.axis_index("col")
    for part, start in ((mine, col * rows), (other, (1 - col) * rows)):
        chosen = pl.ds(pl.multiple_of(start, rows), rows)
        w_in[chosen, : 2 * hidden] = part[:, : 2 * hidden].astype(f32)
        w_in[chosen, 2 * hidden : 4 * hidden] = part[:, 4 * hidden :].astype(f32)
        w_in[chosen, 4 * hidden :] = part[:, 2 * hidden : 3 * hidden].astype(f32)
        w_out[chosen, :] = part[:, 3 * hidden : 4 * hidden].astype(f32)


def shards(
    pair,
    cotangent,
    chain_lengths,
    input_norm_gain,
    input_norm_bias,
    w_in,
    output_norm_gain,
    output_norm_bias,
    w_out,
):
    here, half, channels = pair.shape
    hidden = w_out.shape[0]
    row_count = lax.axis_size("row")
    slot = here * row_count // chain_lengths.shape[0]
    order = ring_order(row_count)
    short = here // 2
    padded = (short + 15) // 16 * 16
    forward = [(order[p], order[(p + 1) % row_count]) for p in range(row_count)]
    backward = [(order[p], order[(p - 1) % row_count]) for p in range(row_count)]
    in_gain, in_bias = input_norm_gain.reshape(1, -1), input_norm_bias.reshape(1, -1)
    out_gain, out_bias = output_norm_gain.reshape(1, -1), output_norm_bias.reshape(1, -1)
    block = (here, half, hidden)
    mask = pltpu.VMEM((half, 128), f32)

    def ahead(x):
        return lax.ppermute(x, "row", forward)

    def behind(x):
        return lax.ppermute(x, "row", backward)

    right, normed = call(
        functools.partial(input_kernel, slot),
        "input_side",
        [chain_lengths, pair, in_gain, in_bias, w_in],
        [SMEM] + [VMEM] * 4,
        [shape_of(block, bf16)] * 2,
        [mask],
    )

    hops = row_count // 2
    groups = [[right]]
    halves = [[(0, 0, (0, 0)), (0, short, (0, 1))]]
    for s in range(1, hops):
        halves.append(
            [(0, 0, (-s, 0)), (1, short, (s, 1)), (0, short, (-s, 1)), (1, 0, (s, 0))]
        )
    halves.append([(0, 0, (-hops, 0)), (1, 0, (hops, 1))])

    def gather(s, x, y):
        if s == hops:
            x, y = x[:short], y[short:]
        groups.append([ahead(x), behind(y)])

    gather(1, right, right)
    left, mine_out = call(
        functools.partial(left_kernel, slot),
        "left_side",
        [chain_lengths, normed, cotangent, w_in],
        [SMEM] + [VMEM] * 3,
        [
            shape_of((here, (half + 15) // 16 * 16, hidden), bf16),
            shape_of((row_count, here, padded, hidden), bf16),
        ],
        [mask],
        microseconds=4,
    )
    other_out = swap_col(mine_out)

    norms, grads, partials, others = [], [], [], []
    last = [left]
    pieces = []

    def triangles(s):
        partials.append(
            triangle(row_count, slot, halves[s], chain_lengths, left, groups[s], padded, last)
        )
        others.append(swap_col(partials[s]))
        last[:] = [partials[s]]

    def normal(s):
        places = [place for _, _, place in halves[s]]
        grad, norm = triangle_norm(
            row_count, places, partials[s], others[s], [mine_out, other_out], w_out, out_gain, out_bias, last
        )
        grads.append(grad)
        norms.append(norm)
        last[:] = [grad]

    def add_left(s):
        picks = range(len(halves[s]))
        pieces[:] = [
            left_gradient(halves[s], picks, grads[s], groups[s], pieces[:], last)
        ]
        last[:] = pieces

    def scatter(s, picks, arrived, dtype=bf16):
        x, y = hop(
            row_count,
            slot,
            [halves[s][pick][2] for pick in picks],
            chain_lengths,
            left,
            [grads[s]] * 2,
            picks,
            arrived,
            (short, half, hidden),
            dtype,
            last,
        )
        last[:] = [x]
        return x, y

    arrived = {0: [], 1: []}

    def send(s, chain):
        x, y = scatter(s, [2 * chain, 2 * chain + 1], arrived[chain])
        arrived[chain] = [behind(x), ahead(y)]

    def output_side():
        return call(
            functools.partial(output_kernel, row_count, slot, [len(h) for h in halves]),
            "output_side",
            [chain_lengths, normed, cotangent, pieces[0], w_in, w_out, mine_out, *norms],
            [SMEM] + [VMEM] * (6 + len(norms)),
            [
                shape_of(block, bf16),
                shape_of(block, f32),
                shape_of((channels, 4 * hidden), f32),
            ],
            [
                mask,
                pltpu.VMEM((row_count, here, padded, hidden), bf16),
            ],
            last,
            microseconds=6,
        )

    for s in range(hops + 1):
        triangles(s)
        if s:
            add_left(s - 1)
        normal(s)
        if s == hops - 1:
            send(s, 1)
        elif s < hops:
            x, y, _ = lax.optimization_barrier((*groups[s + 1], last[0]))
            gather(s + 2, x, y)
    send(hops, 0)
    add_left(hops)
    send(hops - 2, 1)
    for s in range(hops - 1, 0, -1):
        if s == 1:
            own_a, own_b = scatter(0, [0, 1], [], f32)
        send(s, 0)
        if s > 2:
            send(s - 2, 1)
    update, gradient, early = output_side()
    arrived1, arrived2 = arrived[0], [arrived[1][1], arrived[1][0]]

    late, keep, give = call(
        functools.partial(right_gradient_kernel, slot),
        "right_gradient",
        [chain_lengths, normed, w_in, early, own_a, own_b]
        + [arrived1[0], arrived2[0], arrived1[1], arrived2[1]],
        [SMEM] + [VMEM] * 9,
        [shape_of((here, half, 2 * hidden), bf16)]
        + [shape_of((channels // 2, 6 * hidden), bf16)] * 2,
        [mask, pltpu.VMEM((channels, 2 * hidden), f32)],
    )
    mine = add(keep, swap_col(give))
    step = 1
    while step < row_count:
        mine = add(
            mine, lax.ppermute(mine, "row", [(r, r ^ step) for r in range(row_count)])
        )
        step *= 2
    (pair_gradient,) = call(
        pair_gradient_kernel,
        "pair_gradient",
        [pair, late, in_gain, w_in, gradient],
        [VMEM] * 5,
        [shape_of(block, bf16)],
        microseconds=3,
    )
    mine, pair_gradient = lax.optimization_barrier((mine, pair_gradient))
    grad_w_in, grad_w_out = call(
        weights_kernel,
        "weight_gradients",
        [mine, swap_col(mine)],
        [VMEM] * 2,
        [shape_of(w_in.shape, f32), shape_of(w_out.shape, f32)],
    )
    return (update, pair_gradient, grad_w_in, grad_w_out)


def solution(mesh):
    placed = (
        P(("grp", "row"), "col", None),
        P(("grp", "row"), "col", None),
        P("grp"),
        P(),
        P(),
        P(),
        P(),
        P(),
        P(),
    )
    return jax.shard_map(
        shards,
        mesh=mesh,
        in_specs=placed,
        out_specs=(
            P(("grp", "row"), "col", None),
            P(("grp", "row"), "col", None),
            P("grp", None),
            P("grp", None),
        ),
        check_vma=False,
    )
```

```python
import functools
import math

import jax
import jax.numpy as jnp
from jax import lax
from jax.experimental import pallas as pl
from jax.experimental.pallas import tpu as pltpu
from jax.sharding import PartitionSpec as P

eps = 1e-05
f32 = jnp.float32
bf16 = jnp.bfloat16
VMEM = pl.BlockSpec(memory_space=pltpu.VMEM)
SMEM = pl.BlockSpec(memory_space=pltpu.SMEM)
ANY = pl.BlockSpec(memory_space=pl.ANY)
MIB = 1 << 20


def layer_norm_backward(output_gradient, standardized_input, inverse_deviation, norm_gain):
    scaled_output = output_gradient * norm_gain
    first_operand = jnp.mean(scaled_output, axis=-1, keepdims=True)
    second_operand = jnp.mean(scaled_output * standardized_input, axis=-1, keepdims=True)
    return inverse_deviation * (scaled_output - first_operand - standardized_input * second_operand)


def standardize(values):
    centered = values - jnp.mean(values, axis=-1, keepdims=True)
    inverse = lax.rsqrt(jnp.mean(centered * centered, axis=-1, keepdims=True) + eps)
    return centered * inverse, inverse


def dot(a, b, ca, cb):
    return lax.dot_general(a, b, (((ca,), (cb,)), ((), ())), preferred_element_type=f32)


def ring_order(row_count):
    if row_count == 8:
        return [0, 2, 4, 6, 7, 5, 3, 1]
    return list(range(row_count))


def ring_place(row_count, row):
    if row_count == 8:
        return jnp.where(row % 2 == 0, row // 2, row_count - 1 - row // 2)
    return row


def ring_row(row_count, place):
    if row_count == 8:
        return jnp.where(place < row_count // 2, 2 * place, 2 * (row_count - 1 - place) + 1)
    return place


def half_index(row_count, offset, letter):
    place = ring_place(row_count, lax.axis_index("row"))
    return ring_row(row_count, (place + offset + row_count) % row_count) * 2 + letter


def arrival_slot(row_count, index):
    hops = row_count // 2
    letter = index % 2
    apart = ring_place(row_count, index // 2) - ring_place(row_count, lax.axis_index("row"))
    apart = (apart + row_count) % row_count
    near = jnp.where(letter == 0, row_count - apart, apart)
    first = 4 * near - 2 + letter
    second = 4 * (row_count - near) - 2 + 3 - letter
    return jnp.where(apart == 0, letter, jnp.where(near <= hops, first, second))


def present_count(row_count, lengths, slot, short, where):
    start = half_index(row_count, *where) * short
    return jnp.clip(lengths[start // slot] - start % slot, 0, short)


def swap_col(x):
    return lax.ppermute(x, "col", [(0, 1), (1, 0)])


def add(a, b):
    return (a.astype(f32) + b.astype(f32)).astype(bf16)


def call(kernel, name, args, specs, outs, scratch=(), after=(), microseconds=0, limit=0):
    held = sum(a.size * a.dtype.itemsize for a, s in zip(args, specs) if s is VMEM)
    after = [x for x in after if x is not None]
    held += sum(int(o.size) * o.dtype.itemsize for o in outs)
    held += sum(math.prod(s.inner_aval.shape) * 4 for s in scratch)

    def body(*refs):
        kernel(*refs[: len(args)], *refs[len(args) + len(after) :])

    return pl.pallas_call(
        body,
        out_shape=list(outs),
        in_specs=list(specs) + [ANY] * len(after),
        out_specs=[VMEM] * len(outs),
        scratch_shapes=list(scratch),
        compiler_params=pltpu.CompilerParams(vmem_limit_bytes=limit or min(56 * MIB, held * 5 // 4 + 6 * MIB)),
        cost_estimate=pl.CostEstimate(
            flops=int(microseconds * 1.1e9) + 1024, bytes_accessed=1024, transcendentals=0
        ),
        name=name,
    )(*args, *after)


def tiles(half):
    return [(k, min(16, half - k)) for k in range(0, half, 16)]


def parts(short):
    return [(0, (short + 1) // 2), ((short + 1) // 2, short)]


def joined(terms):
    chains = [terms[0::2], terms[1::2]]
    sums = []
    for chain in chains:
        total = chain[0]
        for term in chain[1:]:
            total = total + term
        sums.append(total.astype(f32))
    return sums[0] + sums[1]


def wide_row(ref, *at):
    return jnp.broadcast_to(ref[at], (16, ref.shape[-1])).astype(bf16)


def shape_of(dims, dtype):
    return jax.ShapeDtypeStruct(dims, dtype)


def present_row(lengths, slot, position):
    return (position % slot < lengths[position // slot]).astype(f32)


def present_columns(lengths, slot, half):
    at = lax.axis_index("col") * half + lax.broadcasted_iota(jnp.int32, (half, 128), 0)
    chain = at // slot
    held = jnp.zeros((half, 128), jnp.int32)
    for c in range(lengths.shape[0]):
        held = jnp.where(chain == c, lengths[c], held)
    return (at - chain * slot < held).astype(f32)


def first_row(here):
    return lax.axis_index("row") * here


def input_kernel(slot, lengths, pair, gain, bias, w, right, normed, mask):
    here, half, hidden = pair.shape
    mask[...] = present_columns(lengths, slot, half)

    for i in range(here):
        standard, _ = standardize(pair[i].astype(f32))
        values = (standard * gain[...] + bias[...]).astype(bf16)
        normed[i] = values
        proj = dot(values, w[:, 2 * hidden : 4 * hidden], 1, 0)
        shown = mask[...] * present_row(lengths, slot, first_row(here) + i)
        gated = jax.nn.sigmoid(proj[:, :hidden]) * proj[:, hidden:]
        right[i] = (shown * gated).astype(bf16)


def by_rows(here, body):
    def step(t, carry):
        for x in range(here // 2):
            body(t * (here // 2) + x)
        return carry

    lax.fori_loop(0, 2, step, 0)


def left_kernel(slot, lengths, normed, cotangent, w, left, outs, mask):
    here, half, hidden = normed.shape
    halves, _, padded, _ = outs.shape
    short = half // halves
    mask[...] = present_columns(lengths, slot, half)

    def body(i):
        proj = dot(normed[i], w[:, : 2 * hidden], 1, 0)
        shown = mask[...] * present_row(lengths, slot, first_row(here) + i)
        gated = shown * jax.nn.sigmoid(proj[:, :hidden]) * proj[:, hidden:]
        left[i] = gated.astype(bf16)
        gate = jax.nn.sigmoid(dot(normed[i], w[:, 4 * hidden :], 1, 0))
        grads = cotangent[i].astype(f32) * gate
        empty = jnp.zeros((padded - short, hidden), f32)
        for m in range(halves):
            part = grads[m * short : (m + 1) * short]
            outs[m, i] = jnp.concatenate([part, empty], axis=0).astype(bf16)

    by_rows(here, body)


def triangle_kernel(row_count, slot, halves, arrays, lengths, left, *refs):
    rights, (out, partial, rows) = refs[:arrays], refs[arrays:]
    here, half, hidden = left.shape
    padded = out.shape[2]
    short = here // 2
    cuts = tiles(half)
    for s, (array, first, place) in enumerate(halves):
        rows[...] = jnp.zeros_like(rows)

        def columns(pair, carry, right=rights[array], first=first):
            at = [jnp.minimum(2 * pair + x, short - 1) for x in range(2)]
            held = [[right[first + j, pl.ds(k, size), :] for k, size in cuts] for j in at]
            for i in range(here):
                given = [left[i, pl.ds(k, size), :] for k, size in cuts]
                for x in range(2):
                    products = [a * b for a, b in zip(given, held[x])]
                    rest = products.pop() if half % 16 else None
                    total = products[0]
                    for product in products[1:]:
                        total = total + product
                    total = total.astype(f32)
                    total = total[:8] + total[8:]
                    if rest is not None:
                        total += rest.astype(f32)
                    partial[x, pl.ds(8 * i, 8), :] = total
            for x in range(2):
                total = partial[x, pl.ds(0, here, stride=8), :]
                for sub in range(1, 8):
                    total += partial[x, pl.ds(sub, here, stride=8), :]
                rows[pl.ds(at[x], here, stride=padded), :] = total
            return carry

        present = present_count(row_count, lengths, slot, short, place)
        lax.fori_loop(0, (present + 1) // 2, columns, 0)
        out[s] = rows[...].astype(bf16).reshape(here, padded, hidden)


def triangle(row_count, slot, halves, lengths, left, rights, padded, after):
    count, (here, half, hidden) = len(halves), left.shape
    return call(
        functools.partial(triangle_kernel, row_count, slot, halves, len(rights)),
        "triangle",
        [lengths, left, *rights],
        [SMEM] + [VMEM] * (len(rights) + 1),
        [shape_of((count, here, padded, hidden), bf16)],
        [
            pltpu.VMEM((2, here * 8, hidden), f32),
            pltpu.VMEM((here * padded, hidden), f32),
        ],
        after,
    )[0]


def triangle_norm_kernel(
    row_count, places, mine, other, mine_out, other_out, w_out, gain, bias, grad, normed
):
    count, here, padded, hidden = mine.shape
    flat = (here * padded, hidden)

    for s in range(count):
        index = half_index(row_count, *places[s])
        outs = jnp.where(
            index // row_count == lax.axis_index("col"),
            mine_out[index % row_count],
            other_out[index % row_count],
        )
        total = (mine[s].astype(f32) + other[s].astype(f32)).reshape(flat)
        standard, inverse = standardize(total)
        normed[s] = (standard * gain[...] + bias[...]).astype(bf16).reshape(here, padded, hidden)
        grad_norm = dot(outs.reshape(flat), w_out[...], 1, 1)
        result = layer_norm_backward(grad_norm, standard, inverse, gain[...])
        grad[s] = result.astype(bf16).reshape(here, padded, hidden)


def triangle_norm(row_count, places, mine, other, outs, w_out, gain, bias, after):
    return call(
        functools.partial(triangle_norm_kernel, row_count, places),
        "triangle_norm",
        [mine, other, *outs, w_out, gain, bias],
        [VMEM] * 7,
        [shape_of(mine.shape, bf16)] * 2,
        (),
        after,
    )


def hop_kernel(row_count, slot, places, picks, carried, lengths, left, *refs):
    count = len(picks)
    grads, refs = refs[:count], refs[count:]
    arrived, refs = refs[: count * carried], refs[count * carried :]
    outs, wide = refs[:count], refs[count]
    here = left.shape[0]
    short, half, hidden = outs[0].shape
    for s in range(count):
        wide[...] = grads[s][picks[s]].astype(f32)
        out = outs[s]

        def columns(at, s=s, out=out):
            totals = []
            for j in at:
                total = []
                for k, size in tiles(half):
                    start = jnp.zeros((size, hidden), f32)
                    for more in range(carried):
                        start += arrived[s + more * count][j, pl.ds(k, size), :].astype(f32)
                    total.append(start)
                totals.append(total)
            for low in range(0, here, short):
                chosen = range(low, min(low + short, here))
                weights = [[wide_row(wide, i, pl.ds(j, 1)) for i in chosen] for j in at]
                for t, (k, size) in enumerate(tiles(half)):
                    held = [left[i, pl.ds(k, size), :] for i in chosen]
                    for total, weight in zip(totals, weights):
                        total[t] += joined([w[:size] * h for w, h in zip(weight, held)])
            for j, total in zip(at, totals):
                for t, (k, size) in enumerate(tiles(half)):
                    out[j, pl.ds(k, size), :] = total[t].astype(out.dtype)

        present = present_count(row_count, lengths, slot, short, places[s])
        for low, high in parts(short):

            @pl.when(present > low)
            def _(low=low, high=high, columns=columns):
                for j in range(low, high, 2):
                    columns(range(j, min(j + 2, high)))

            @pl.when(present <= low)
            def _(low=low, high=high, out=out):
                out[pl.ds(low, high - low)] = jnp.zeros((high - low, half, hidden), out.dtype)


def hop(row_count, slot, places, lengths, left, grads, picks, arrived, out, dtype, after):
    count = len(grads)
    carried = len(arrived) // count
    return call(
        functools.partial(hop_kernel, row_count, slot, places, picks, carried),
        "scatter_hop",
        [lengths, left, *grads, *arrived],
        [SMEM] + [VMEM] * (1 + count + len(arrived)),
        [shape_of(out, dtype)] * count,
        [pltpu.VMEM(grads[0].shape[1:], f32)],
        after,
    )


def add_kernel(one, two, first, second, out_one, out_two):
    out_one[...] = (one[...] + first[...].astype(f32)).astype(bf16)
    out_two[...] = (two[...] + second[...].astype(f32)).astype(bf16)


def left_gradient_kernel(halves, picks, arrays, carried, grads, *refs):
    count = len(picks)
    rights, refs = refs[:arrays], refs[arrays:]
    before, (out, wide) = refs[:carried], refs[carried:]
    here, half, hidden = out.shape
    short = here // 2
    for s, pick in enumerate(picks):
        wide[s] = grads[pick].astype(f32)

    def row(pair, carry):
        rows = (2 * pair, 2 * pair + 1)
        for s, pick in enumerate(picks):
            array, first, _ = halves[pick]
            weights = [[wide_row(wide, s, i, pl.ds(j, 1)) for j in range(short)] for i in rows]
            for k, size in tiles(half):
                held = [rights[array][first + j, pl.ds(k, size), :] for j in range(short)]
                for i, weight in zip(rows, weights):
                    total = joined([w[:size] * h for w, h in zip(weight, held)])
                    if s:
                        total += out[i, pl.ds(k, size), :]
                    elif carried:
                        total += before[0][i, pl.ds(k, size), :]
                    out[i, pl.ds(k, size), :] = total
        return carry

    lax.fori_loop(0, here // 2, row, 0)


def left_gradient(halves, picks, grads, rights, before, after):
    count, here = len(picks), grads.shape[1]
    half, hidden = rights[0].shape[1:]
    return call(
        functools.partial(left_gradient_kernel, halves, picks, len(rights), len(before)),
        "left_gradient",
        [grads, *rights, *before],
        [VMEM] * (1 + len(rights) + len(before)),
        [shape_of((here, half, hidden), f32)],
        [pltpu.VMEM((count,) + grads.shape[1:], f32)],
        after,
    )[0]


def output_kernel(
    row_count, slot, counts, lengths, normed, cotangent, grad_left, w, w_out, outs, *refs
):
    norms, (update, gradient, total, mask, picked) = refs[: len(counts)], refs[len(counts) :]
    here, half, hidden = normed.shape
    halves, _, padded, _ = picked.shape
    short = half // halves
    mask[...] = present_columns(lengths, slot, half)
    total[...] = jnp.zeros_like(total)
    for m in range(halves):
        low = 0
        stands = arrival_slot(row_count, lax.axis_index("col") * row_count + m)
        for norm, count in zip(norms, counts):

            @pl.when((stands >= low) & (stands < low + count))
            def _(m=m, norm=norm, low=low, stands=stands):
                picked[m] = norm[stands - low]

            low += count

    def body(i):
        values = normed[i]
        proj = dot(values, w[:, : 2 * hidden], 1, 0)
        sig_left = jax.nn.sigmoid(proj[:, :hidden])
        val_left = proj[:, hidden:]
        gate = jax.nn.sigmoid(dot(values, w[:, 4 * hidden :], 1, 0))
        tri = picked[:, i].reshape(halves * padded, hidden)
        product = dot(tri, w_out[...], 1, 0)
        projected = jnp.concatenate(
            [product[m * padded : m * padded + short] for m in range(halves)], axis=0
        )
        update[i] = (gate * projected).astype(bf16)
        grad_gate = (cotangent[i].astype(f32) * projected * gate * (1.0 - gate)).astype(bf16)
        shown = mask[...] * present_row(lengths, slot, first_row(here) + i)
        masked = grad_left[i] * shown
        grads = jnp.concatenate(
            [masked * val_left * sig_left * (1.0 - sig_left), masked * sig_left], axis=1
        ).astype(bf16)
        gradient[i] = dot(grads, w[:, : 2 * hidden], 1, 1) + dot(
            grad_gate, w[:, 4 * hidden :], 1, 1
        )
        total[:, : 2 * hidden] += dot(values, grads, 0, 0)
        total[:, 2 * hidden : 3 * hidden] += dot(values, grad_gate, 0, 0)
        total[:, 3 * hidden :] += dot(tri, outs[:, i].reshape(halves * padded, hidden), 0, 0)

    by_rows(here, body)


def right_gradient_kernel(slot, lengths, normed, w, early, own_a, own_b, *refs):
    arrived, (grads, keep, give, mask, total) = refs[:4], refs[4:]
    here, half, hidden = normed.shape
    short = here // 2
    mask[...] = present_columns(lengths, slot, half)
    total[...] = jnp.zeros_like(total)

    for own, others, first in ((own_a, arrived[:2], 0), (own_b, arrived[2:], short)):
        for t in range(short):
            j = first + t
            values = normed[j]
            proj = dot(values, w[:, 2 * hidden : 4 * hidden], 1, 0)
            sig_right = jax.nn.sigmoid(proj[:, :hidden])
            val_right = proj[:, hidden:]
            shown = mask[...] * present_row(lengths, slot, first_row(here) + j)
            masked = shown * (own[t] + others[0][t].astype(f32) + others[1][t].astype(f32))
            result = jnp.concatenate(
                [masked * val_right * sig_right * (1.0 - sig_right), masked * sig_right], axis=1
            ).astype(bf16)
            grads[j] = result
            total[...] += dot(values, result, 0, 0)
    rows, wide = keep.shape[0], early.shape[1]
    col = lax.axis_index("col")
    for out, start in ((keep, col * rows), (give, (1 - col) * rows)):
        chosen = pl.ds(pl.multiple_of(start, rows), rows)
        out[:, :wide] = early[chosen, :].astype(bf16)
        out[:, wide:] = total[chosen, :].astype(bf16)


def pair_gradient_kernel(pair, grads, gain, w, *refs):
    gradients, out = refs[:-1], refs[-1]
    hidden = pair.shape[2]

    i = 0
    for gradient in gradients:
        for at in range(gradient.shape[0]):
            standard, inverse = standardize(pair[i].astype(f32))
            total = gradient[at] + dot(grads[i], w[:, 2 * hidden : 4 * hidden], 1, 1)
            out[i] = layer_norm_backward(total, standard, inverse, gain[...]).astype(bf16)
            i += 1


def weights_kernel(mine, other, w_in, w_out):
    rows, hidden = mine.shape[0], w_out.shape[0]
    col = lax.axis_index("col")
    for part, start in ((mine, col * rows), (other, (1 - col) * rows)):
        chosen = pl.ds(pl.multiple_of(start, rows), rows)
        w_in[chosen, : 2 * hidden] = part[:, : 2 * hidden].astype(f32)
        w_in[chosen, 2 * hidden : 4 * hidden] = part[:, 4 * hidden :].astype(f32)
        w_in[chosen, 4 * hidden :] = part[:, 2 * hidden : 3 * hidden].astype(f32)
        w_out[chosen, :] = part[:, 3 * hidden : 4 * hidden].astype(f32)


def shards(
    pair,
    cotangent,
    chain_lengths,
    input_norm_gain,
    input_norm_bias,
    w_in,
    output_norm_gain,
    output_norm_bias,
    w_out,
):
    here, half, channels = pair.shape
    hidden = w_out.shape[0]
    row_count = lax.axis_size("row")
    slot = here * row_count // chain_lengths.shape[0]
    order = ring_order(row_count)
    short = here // 2
    padded = (short + 15) // 16 * 16
    forward = [(order[p], order[(p + 1) % row_count]) for p in range(row_count)]
    backward = [(order[p], order[(p - 1) % row_count]) for p in range(row_count)]
    in_gain, in_bias = input_norm_gain.reshape(1, -1), input_norm_bias.reshape(1, -1)
    out_gain, out_bias = output_norm_gain.reshape(1, -1), output_norm_bias.reshape(1, -1)
    block = (here, half, hidden)
    mask = pltpu.VMEM((half, 128), f32)

    def ahead(x):
        return lax.ppermute(x, "row", forward)

    def behind(x):
        return lax.ppermute(x, "row", backward)

    right, normed = call(
        functools.partial(input_kernel, slot),
        "input_side",
        [chain_lengths, pair, in_gain, in_bias, w_in],
        [SMEM] + [VMEM] * 4,
        [shape_of(block, bf16)] * 2,
        [mask],
    )

    hops = row_count // 2
    groups = [[right]]
    halves = [[(0, 0, (0, 0)), (0, short, (0, 1))]]
    for s in range(1, hops):
        halves.append(
            [(0, 0, (-s, 0)), (1, short, (s, 1)), (0, short, (-s, 1)), (1, 0, (s, 0))]
        )
    halves.append([(0, 0, (-hops, 0)), (1, 0, (hops, 1))])

    def gather(s, x, y):
        if s == hops:
            x, y = x[:short], y[short:]
        groups.append([ahead(x), behind(y)])

    gather(1, right, right)
    left, mine_out = call(
        functools.partial(left_kernel, slot),
        "left_side",
        [chain_lengths, normed, cotangent, w_in],
        [SMEM] + [VMEM] * 3,
        [shape_of(block, bf16), shape_of((row_count, here, padded, hidden), bf16)],
        [mask],
        microseconds=4,
    )
    other_out = swap_col(mine_out)

    norms, grads, partials, others = [], [], [], []
    last = [left]
    pieces = []

    def triangles(s):
        partials.append(
            triangle(row_count, slot, halves[s], chain_lengths, left, groups[s], padded, last)
        )
        others.append(swap_col(partials[s]))
        last[:] = [partials[s]]

    def normal(s):
        places = [place for _, _, place in halves[s]]
        grad, norm = triangle_norm(
            row_count, places, partials[s], others[s], [mine_out, other_out], w_out, out_gain, out_bias, last
        )
        grads.append(grad)
        norms.append(norm)
        last[:] = [grad]

    def add_left(s):
        picks = range(len(halves[s]))
        pieces[:] = [
            left_gradient(halves[s], picks, grads[s], groups[s], pieces[:], last)
        ]
        last[:] = pieces

    def scatter(s, picks, arrived, dtype=bf16):
        x, y = hop(
            row_count,
            slot,
            [halves[s][pick][2] for pick in picks],
            chain_lengths,
            left,
            [grads[s]] * 2,
            picks,
            arrived,
            (short, half, hidden),
            dtype,
            last,
        )
        last[:] = [x]
        return x, y

    arrived = {0: [], 1: []}

    def send(s, chain, after=()):
        picks = [2 * chain, 2 * chain + 1]
        if arrived[chain]:
            terms = scatter(s, picks, [], f32)
            x, y = call(
                add_kernel,
                "scatter_add",
                [*terms, *arrived[chain]],
                [VMEM] * 4,
                [shape_of((short, half, hidden), bf16)] * 2,
                (),
                [*last, *after],
            )
            last[:] = [x]
        else:
            x, y = scatter(s, picks, [])
        arrived[chain] = [behind(x), ahead(y)]

    def output_side():
        return call(
            functools.partial(output_kernel, row_count, slot, [len(h) for h in halves]),
            "output_side",
            [chain_lengths, normed, cotangent, pieces[0], w_in, w_out, mine_out, *norms],
            [SMEM] + [VMEM] * (6 + len(norms)),
            [
                shape_of(block, bf16),
                shape_of(block, f32),
                shape_of((channels, 4 * hidden), f32),
            ],
            [
                mask,
                pltpu.VMEM((row_count, here, padded, hidden), bf16),
            ],
            last,
            microseconds=6,
        )

    for s in range(hops + 1):
        triangles(s)
        if s:
            add_left(s - 1)
        normal(s)
        if s == hops - 1:
            send(s, 1)
        elif s < hops:
            x, y, _ = lax.optimization_barrier((*groups[s + 1], last[0]))
            gather(s + 2, x, y)
    send(hops, 0)
    add_left(hops)
    send(hops - 2, 1)
    for s in range(hops - 1, 0, -1):
        if s == 1:
            own_a, own_b = scatter(0, [0, 1], [], f32)
        send(s, 0, arrived[1] if s == 1 else ())
        if s > 2:
            send(s - 2, 1)
    update, gradient, early = output_side()
    arrived1, arrived2 = arrived[0], [arrived[1][1], arrived[1][0]]

    late, keep, give = call(
        functools.partial(right_gradient_kernel, slot),
        "right_gradient",
        [chain_lengths, normed, w_in, early, own_a, own_b]
        + [arrived1[0], arrived2[0], arrived1[1], arrived2[1]],
        [SMEM] + [VMEM] * 9,
        [shape_of((here, half, 2 * hidden), bf16)]
        + [shape_of((channels // 2, 6 * hidden), bf16)] * 2,
        [mask, pltpu.VMEM((channels, 2 * hidden), f32)],
    )
    mine = add(keep, swap_col(give))
    step = 1
    while step < row_count:
        mine = add(
            mine, lax.ppermute(mine, "row", [(r, r ^ step) for r in range(row_count)])
        )
        step *= 2
    (pair_gradient,) = call(
        pair_gradient_kernel,
        "pair_gradient",
        [pair, late, in_gain, w_in, gradient],
        [VMEM] * 5,
        [shape_of(block, bf16)],
        microseconds=3,
    )
    mine, pair_gradient = lax.optimization_barrier((mine, pair_gradient))
    grad_w_in, grad_w_out = call(
        weights_kernel,
        "weight_gradients",
        [mine, swap_col(mine)],
        [VMEM] * 2,
        [shape_of(w_in.shape, f32), shape_of(w_out.shape, f32)],
    )
    return (update, pair_gradient, grad_w_in, grad_w_out)


def solution(mesh):
    placed = (
        P(("grp", "row"), "col", None),
        P(("grp", "row"), "col", None),
        P("grp"),
        P(),
        P(),
        P(),
        P(),
        P(),
        P(),
    )
    return jax.shard_map(
        shards,
        mesh=mesh,
        in_specs=placed,
        out_specs=(
            P(("grp", "row"), "col", None),
            P(("grp", "row"), "col", None),
            P("grp", None),
            P("grp", None),
        ),
        check_vma=False,
    )
```

```python
import functools
import math

import jax
import jax.numpy as jnp
from jax import lax
from jax.experimental import pallas as pl
from jax.experimental.pallas import tpu as pltpu
from jax.sharding import PartitionSpec as P

eps = 1e-05
f32 = jnp.float32
bf16 = jnp.bfloat16
VMEM = pl.BlockSpec(memory_space=pltpu.VMEM)
SMEM = pl.BlockSpec(memory_space=pltpu.SMEM)
ANY = pl.BlockSpec(memory_space=pl.ANY)
MIB = 1 << 20


def layer_norm_backward(output_gradient, standardized_input, inverse_deviation, norm_gain):
    scaled_output = output_gradient * norm_gain
    first_operand = jnp.mean(scaled_output, axis=-1, keepdims=True)
    second_operand = jnp.mean(scaled_output * standardized_input, axis=-1, keepdims=True)
    return inverse_deviation * (scaled_output - first_operand - standardized_input * second_operand)


def standardize(values):
    centered = values - jnp.mean(values, axis=-1, keepdims=True)
    inverse = lax.rsqrt(jnp.mean(centered * centered, axis=-1, keepdims=True) + eps)
    return centered * inverse, inverse


def dot(a, b, ca, cb):
    return lax.dot_general(a, b, (((ca,), (cb,)), ((), ())), preferred_element_type=f32)


def ring_order(row_count):
    if row_count == 8:
        return [0, 2, 4, 6, 7, 5, 3, 1]
    return list(range(row_count))


def ring_place(row_count, row):
    if row_count == 8:
        return jnp.where(row % 2 == 0, row // 2, row_count - 1 - row // 2)
    return row


def ring_row(row_count, place):
    if row_count == 8:
        return jnp.where(place < row_count // 2, 2 * place, 2 * (row_count - 1 - place) + 1)
    return place


def half_index(row_count, offset, letter):
    place = ring_place(row_count, lax.axis_index("row"))
    return ring_row(row_count, (place + offset + row_count) % row_count) * 2 + letter


def arrival_slot(row_count, index):
    hops = row_count // 2
    letter = index % 2
    apart = ring_place(row_count, index // 2) - ring_place(row_count, lax.axis_index("row"))
    apart = (apart + row_count) % row_count
    near = jnp.where(letter == 0, row_count - apart, apart)
    first = 4 * near - 2 + letter
    second = 4 * (row_count - near) + 1 - letter
    return jnp.where(apart == 0, letter, jnp.where(near <= hops, first, second))


def present_count(row_count, lengths, slot, short, where):
    start = half_index(row_count, *where) * short
    return jnp.clip(lengths[start // slot] - start % slot, 0, short)


def swap_col(x):
    return lax.ppermute(x, "col", [(0, 1), (1, 0)])


def add(a, b):
    return (a.astype(f32) + b.astype(f32)).astype(bf16)


def call(kernel, name, args, specs, outs, scratch=(), after=(), microseconds=0, limit=0):
    held = sum(a.size * a.dtype.itemsize for a, s in zip(args, specs) if s is VMEM)
    after = [x for x in after if x is not None]
    held += sum(int(o.size) * o.dtype.itemsize for o in outs)
    held += sum(math.prod(s.inner_aval.shape) * 4 for s in scratch)

    def body(*refs):
        kernel(*refs[: len(args)], *refs[len(args) + len(after) :])

    return pl.pallas_call(
        body,
        out_shape=list(outs),
        in_specs=list(specs) + [ANY] * len(after),
        out_specs=[VMEM] * len(outs),
        scratch_shapes=list(scratch),
        compiler_params=pltpu.CompilerParams(vmem_limit_bytes=limit or min(56 * MIB, held * 5 // 4 + 6 * MIB)),
        cost_estimate=pl.CostEstimate(
            flops=int(microseconds * 1.1e9) + 1024, bytes_accessed=1024, transcendentals=0
        ),
        name=name,
    )(*args, *after)


def tiles(half):
    return [(k, min(16, half - k)) for k in range(0, half, 16)]


def parts(short):
    return [(0, (short + 1) // 2), ((short + 1) // 2, short)]


def joined(terms):
    chains = [terms[0::2], terms[1::2]]
    sums = []
    for chain in chains:
        total = chain[0]
        for term in chain[1:]:
            total = total + term
        sums.append(total.astype(f32))
    return sums[0] + sums[1]


def wide_row(ref, *at):
    return jnp.broadcast_to(ref[at], (16, ref.shape[-1])).astype(bf16)


def shape_of(dims, dtype):
    return jax.ShapeDtypeStruct(dims, dtype)


def present_row(lengths, slot, position):
    return (position % slot < lengths[position // slot]).astype(f32)


def present_columns(lengths, slot, half):
    at = lax.axis_index("col") * half + lax.broadcasted_iota(jnp.int32, (half, 128), 0)
    chain = at // slot
    held = jnp.zeros((half, 128), jnp.int32)
    for c in range(lengths.shape[0]):
        held = jnp.where(chain == c, lengths[c], held)
    return (at - chain * slot < held).astype(f32)


def first_row(here):
    return lax.axis_index("row") * here


def input_kernel(slot, lengths, pair, gain, bias, w, right_a, right_b, normed, mask):
    here, half, hidden = pair.shape
    mask[...] = present_columns(lengths, slot, half)

    for i in range(here):
        standard, _ = standardize(pair[i].astype(f32))
        values = (standard * gain[...] + bias[...]).astype(bf16)
        normed[i] = values
        proj = dot(values, w[:, 2 * hidden : 4 * hidden], 1, 0)
        shown = mask[...] * present_row(lengths, slot, first_row(here) + i)
        gated = jax.nn.sigmoid(proj[:, :hidden]) * proj[:, hidden:]
        out, at = (right_a, i) if i < here // 2 else (right_b, i - here // 2)
        out[at] = (shown * gated).astype(bf16)


def by_rows(here, body):
    def step(t, carry):
        for x in range(here // 2):
            body(t * (here // 2) + x)
        return carry

    lax.fori_loop(0, 2, step, 0)


def left_kernel(slot, lengths, normed, cotangent, w, left, outs, mask):
    here, half, hidden = normed.shape
    halves, _, padded, _ = outs.shape
    short = half // halves
    mask[...] = present_columns(lengths, slot, half)

    def body(i):
        proj = dot(normed[i], w[:, : 2 * hidden], 1, 0)
        shown = mask[...] * present_row(lengths, slot, first_row(here) + i)
        gated = shown * jax.nn.sigmoid(proj[:, :hidden]) * proj[:, hidden:]
        left[i] = gated.astype(bf16)
        gate = jax.nn.sigmoid(dot(normed[i], w[:, 4 * hidden :], 1, 0))
        grads = cotangent[i].astype(f32) * gate
        empty = jnp.zeros((padded - short, hidden), f32)
        for m in range(halves):
            part = grads[m * short : (m + 1) * short]
            outs[m, i] = jnp.concatenate([part, empty], axis=0).astype(bf16)

    by_rows(here, body)


def triangle_kernel(row_count, slot, halves, arrays, lengths, left, *refs):
    rights, (out, partial, rows) = refs[:arrays], refs[arrays:]
    here, half, hidden = left.shape
    padded = out.shape[2]
    short = here // 2
    cuts = tiles(half)
    for s, (array, first, place) in enumerate(halves):
        rows[...] = jnp.zeros_like(rows)

        def columns(pair, carry, right=rights[array], first=first):
            at = [jnp.minimum(2 * pair + x, short - 1) for x in range(2)]
            held = [[right[first + j, pl.ds(k, size), :] for k, size in cuts] for j in at]
            for i in range(here):
                given = [left[i, pl.ds(k, size), :] for k, size in cuts]
                for x in range(2):
                    products = [a * b for a, b in zip(given, held[x])]
                    rest = products.pop() if half % 16 else None
                    total = products[0]
                    for product in products[1:]:
                        total = total + product
                    total = total.astype(f32)
                    total = total[:8] + total[8:]
                    if rest is not None:
                        total += rest.astype(f32)
                    partial[x, pl.ds(8 * i, 8), :] = total
            for x in range(2):
                total = partial[x, pl.ds(0, here, stride=8), :]
                for sub in range(1, 8):
                    total += partial[x, pl.ds(sub, here, stride=8), :]
                rows[pl.ds(at[x], here, stride=padded), :] = total
            return carry

        present = present_count(row_count, lengths, slot, short, place)
        lax.fori_loop(0, (present + 1) // 2, columns, 0)
        out[s] = rows[...].astype(bf16).reshape(here, padded, hidden)


def triangle(row_count, slot, halves, lengths, left, rights, padded, after):
    count, (here, half, hidden) = len(halves), left.shape
    return call(
        functools.partial(triangle_kernel, row_count, slot, halves, len(rights)),
        "triangle",
        [lengths, left, *rights],
        [SMEM] + [VMEM] * (len(rights) + 1),
        [shape_of((count, here, padded, hidden), bf16)],
        [
            pltpu.VMEM((2, here * 8, hidden), f32),
            pltpu.VMEM((here * padded, hidden), f32),
        ],
        after,
    )[0]


def triangle_norm_kernel(
    row_count, places, mine, other, mine_out, other_out, w_out, gain, bias, grad, normed
):
    count, here, padded, hidden = mine.shape
    flat = (here * padded, hidden)

    for s in range(count):
        index = half_index(row_count, *places[s])
        outs = jnp.where(
            index // row_count == lax.axis_index("col"),
            mine_out[index % row_count],
            other_out[index % row_count],
        )
        total = (mine[s].astype(f32) + other[s].astype(f32)).reshape(flat)
        standard, inverse = standardize(total)
        normed[s] = (standard * gain[...] + bias[...]).astype(bf16).reshape(here, padded, hidden)
        grad_norm = dot(outs.reshape(flat), w_out[...], 1, 1)
        result = layer_norm_backward(grad_norm, standard, inverse, gain[...])
        grad[s] = result.astype(bf16).reshape(here, padded, hidden)


def triangle_norm(row_count, places, mine, other, outs, w_out, gain, bias, after):
    return call(
        functools.partial(triangle_norm_kernel, row_count, places),
        "triangle_norm",
        [mine, other, *outs, w_out, gain, bias],
        [VMEM] * 7,
        [shape_of(mine.shape, bf16)] * 2,
        (),
        after,
    )


def hop_kernel(row_count, slot, places, picks, carried, lengths, left, *refs):
    count = len(picks)
    grads, refs = refs[:count], refs[count:]
    arrived, refs = refs[: count * carried], refs[count * carried :]
    outs, wide = refs[:count], refs[count]
    here = left.shape[0]
    short, half, hidden = outs[0].shape
    for s in range(count):
        wide[...] = grads[s][picks[s]].astype(f32)
        out = outs[s]

        def columns(at, s=s, out=out):
            totals = []
            for j in at:
                total = []
                for k, size in tiles(half):
                    start = jnp.zeros((size, hidden), f32)
                    for more in range(carried):
                        start += arrived[s + more * count][j, pl.ds(k, size), :].astype(f32)
                    total.append(start)
                totals.append(total)
            for low in range(0, here, short):
                chosen = range(low, min(low + short, here))
                weights = [[wide_row(wide, i, pl.ds(j, 1)) for i in chosen] for j in at]
                for t, (k, size) in enumerate(tiles(half)):
                    held = [left[i, pl.ds(k, size), :] for i in chosen]
                    for total, weight in zip(totals, weights):
                        total[t] += joined([w[:size] * h for w, h in zip(weight, held)])
            for j, total in zip(at, totals):
                for t, (k, size) in enumerate(tiles(half)):
                    out[j, pl.ds(k, size), :] = total[t].astype(out.dtype)

        present = present_count(row_count, lengths, slot, short, places[s])
        for low, high in parts(short):

            @pl.when(present > low)
            def _(low=low, high=high, columns=columns):
                for j in range(low, high, 2):
                    columns(range(j, min(j + 2, high)))

            @pl.when(present <= low)
            def _(low=low, high=high, out=out):
                out[pl.ds(low, high - low)] = jnp.zeros((high - low, half, hidden), out.dtype)


def hop(row_count, slot, places, lengths, left, grads, picks, arrived, out, dtype, after):
    count = len(grads)
    carried = len(arrived) // count
    return call(
        functools.partial(hop_kernel, row_count, slot, places, picks, carried),
        "scatter_hop",
        [lengths, left, *grads, *arrived],
        [SMEM] + [VMEM] * (1 + count + len(arrived)),
        [shape_of(out, dtype)] * count,
        [pltpu.VMEM(grads[0].shape[1:], f32)],
        after,
    )


def add_kernel(one, two, first, second, out_one, out_two):
    out_one[...] = (one[...] + first[...].astype(f32)).astype(bf16)
    out_two[...] = (two[...] + second[...].astype(f32)).astype(bf16)


def left_gradient_kernel(halves, picks, arrays, carried, grads, *refs):
    count = len(picks)
    rights, refs = refs[:arrays], refs[arrays:]
    before, (out, wide) = refs[:carried], refs[carried:]
    here, half, hidden = out.shape
    short = here // 2
    for s, pick in enumerate(picks):
        wide[s] = grads[pick].astype(f32)

    def row(pair, carry):
        rows = (2 * pair, 2 * pair + 1)
        for s, pick in enumerate(picks):
            array, first, _ = halves[pick]
            weights = [[wide_row(wide, s, i, pl.ds(j, 1)) for j in range(short)] for i in rows]
            for k, size in tiles(half):
                held = [rights[array][first + j, pl.ds(k, size), :] for j in range(short)]
                for i, weight in zip(rows, weights):
                    total = joined([w[:size] * h for w, h in zip(weight, held)])
                    if s:
                        total += out[i, pl.ds(k, size), :]
                    elif carried:
                        total += before[0][i, pl.ds(k, size), :]
                    out[i, pl.ds(k, size), :] = total
        return carry

    lax.fori_loop(0, here // 2, row, 0)


def left_gradient(halves, picks, grads, rights, before, after):
    count, here = len(picks), grads.shape[1]
    half, hidden = rights[0].shape[1:]
    return call(
        functools.partial(left_gradient_kernel, halves, picks, len(rights), len(before)),
        "left_gradient",
        [grads, *rights, *before],
        [VMEM] * (1 + len(rights) + len(before)),
        [shape_of((here, half, hidden), f32)],
        [pltpu.VMEM((count,) + grads.shape[1:], f32)],
        after,
    )[0]


def output_kernel(
    row_count, slot, counts, lengths, normed, cotangent, grad_left, w, w_out, outs, *refs
):
    norms, (update, gradient, total, mask, picked) = refs[: len(counts)], refs[len(counts) :]
    here, half, hidden = normed.shape
    halves, _, padded, _ = picked.shape
    short = half // halves
    mask[...] = present_columns(lengths, slot, half)
    total[...] = jnp.zeros_like(total)
    for m in range(halves):
        low = 0
        stands = arrival_slot(row_count, lax.axis_index("col") * row_count + m)
        for norm, count in zip(norms, counts):

            @pl.when((stands >= low) & (stands < low + count))
            def _(m=m, norm=norm, low=low, stands=stands):
                picked[m] = norm[stands - low]

            low += count

    def body(i):
        values = normed[i]
        proj = dot(values, w[:, : 2 * hidden], 1, 0)
        sig_left = jax.nn.sigmoid(proj[:, :hidden])
        val_left = proj[:, hidden:]
        gate = jax.nn.sigmoid(dot(values, w[:, 4 * hidden :], 1, 0))
        tri = picked[:, i].reshape(halves * padded, hidden)
        product = dot(tri, w_out[...], 1, 0)
        projected = jnp.concatenate(
            [product[m * padded : m * padded + short] for m in range(halves)], axis=0
        )
        update[i] = (gate * projected).astype(bf16)
        grad_gate = (cotangent[i].astype(f32) * projected * gate * (1.0 - gate)).astype(bf16)
        shown = mask[...] * present_row(lengths, slot, first_row(here) + i)
        masked = grad_left[i] * shown
        grads = jnp.concatenate(
            [masked * val_left * sig_left * (1.0 - sig_left), masked * sig_left], axis=1
        ).astype(bf16)
        gradient[i] = dot(grads, w[:, : 2 * hidden], 1, 1) + dot(
            grad_gate, w[:, 4 * hidden :], 1, 1
        )
        total[:, : 2 * hidden] += dot(values, grads, 0, 0)
        total[:, 2 * hidden : 3 * hidden] += dot(values, grad_gate, 0, 0)
        total[:, 3 * hidden :] += dot(tri, outs[:, i].reshape(halves * padded, hidden), 0, 0)

    by_rows(here, body)


def right_gradient_kernel(slot, lengths, normed, w, early, own_a, own_b, *refs):
    arrived, (grads, keep, give, mask, total) = refs[:4], refs[4:]
    here, half, hidden = normed.shape
    short = here // 2
    mask[...] = present_columns(lengths, slot, half)
    total[...] = jnp.zeros_like(total)

    for own, others, first in ((own_a, arrived[:2], 0), (own_b, arrived[2:], short)):
        for t in range(short):
            j = first + t
            values = normed[j]
            proj = dot(values, w[:, 2 * hidden : 4 * hidden], 1, 0)
            sig_right = jax.nn.sigmoid(proj[:, :hidden])
            val_right = proj[:, hidden:]
            shown = mask[...] * present_row(lengths, slot, first_row(here) + j)
            masked = shown * (own[t] + others[0][t].astype(f32) + others[1][t].astype(f32))
            result = jnp.concatenate(
                [masked * val_right * sig_right * (1.0 - sig_right), masked * sig_right], axis=1
            ).astype(bf16)
            grads[j] = result
            total[...] += dot(values, result, 0, 0)
    rows, wide = keep.shape[0], early.shape[1]
    col = lax.axis_index("col")
    for out, start in ((keep, col * rows), (give, (1 - col) * rows)):
        chosen = pl.ds(pl.multiple_of(start, rows), rows)
        out[:, :wide] = early[chosen, :].astype(bf16)
        out[:, wide:] = total[chosen, :].astype(bf16)


def pair_gradient_kernel(pair, grads, gain, w, *refs):
    gradients, out = refs[:-1], refs[-1]
    hidden = pair.shape[2]

    i = 0
    for gradient in gradients:
        for at in range(gradient.shape[0]):
            standard, inverse = standardize(pair[i].astype(f32))
            total = gradient[at] + dot(grads[i], w[:, 2 * hidden : 4 * hidden], 1, 1)
            out[i] = layer_norm_backward(total, standard, inverse, gain[...]).astype(bf16)
            i += 1


def weights_kernel(mine, other, w_in, w_out):
    rows, hidden = mine.shape[0], w_out.shape[0]
    col = lax.axis_index("col")
    for part, start in ((mine, col * rows), (other, (1 - col) * rows)):
        chosen = pl.ds(pl.multiple_of(start, rows), rows)
        w_in[chosen, : 2 * hidden] = part[:, : 2 * hidden].astype(f32)
        w_in[chosen, 2 * hidden : 4 * hidden] = part[:, 4 * hidden :].astype(f32)
        w_in[chosen, 4 * hidden :] = part[:, 2 * hidden : 3 * hidden].astype(f32)
        w_out[chosen, :] = part[:, 3 * hidden : 4 * hidden].astype(f32)


def shards(
    pair,
    cotangent,
    chain_lengths,
    input_norm_gain,
    input_norm_bias,
    w_in,
    output_norm_gain,
    output_norm_bias,
    w_out,
):
    here, half, channels = pair.shape
    hidden = w_out.shape[0]
    row_count = lax.axis_size("row")
    slot = here * row_count // chain_lengths.shape[0]
    order = ring_order(row_count)
    short = here // 2
    padded = (short + 15) // 16 * 16
    forward = [(order[p], order[(p + 1) % row_count]) for p in range(row_count)]
    backward = [(order[p], order[(p - 1) % row_count]) for p in range(row_count)]
    in_gain, in_bias = input_norm_gain.reshape(1, -1), input_norm_bias.reshape(1, -1)
    out_gain, out_bias = output_norm_gain.reshape(1, -1), output_norm_bias.reshape(1, -1)
    block = (here, half, hidden)
    mask = pltpu.VMEM((half, 128), f32)

    def ahead(x):
        return lax.ppermute(x, "row", forward)

    def behind(x):
        return lax.ppermute(x, "row", backward)

    right_a, right_b, normed = call(
        functools.partial(input_kernel, slot),
        "input_side",
        [chain_lengths, pair, in_gain, in_bias, w_in],
        [SMEM] + [VMEM] * 4,
        [shape_of((short, half, hidden), bf16)] * 2 + [shape_of(block, bf16)],
        [mask],
    )

    hops = row_count // 2
    steps = 2 * hops
    groups = [[right_a, right_b]]
    halves = [[(0, 0, (0, 0)), (1, 0, (0, 1))]]
    for s in range(1, hops + 1):
        halves.append([(0, 0, (-s, 0)), (1, 0, (s, 1))])
        if s < hops:
            halves.append([(0, 0, (-s, 1)), (1, 0, (s, 0))])

    def gather(x, y):
        groups.append([ahead(x), behind(y)])

    gather(right_a, right_b)
    gather(right_b, right_a)
    left, mine_out = call(
        functools.partial(left_kernel, slot),
        "left_side",
        [chain_lengths, normed, cotangent, w_in],
        [SMEM] + [VMEM] * 3,
        [shape_of(block, bf16), shape_of((row_count, here, padded, hidden), bf16)],
        [mask],
        microseconds=4,
    )
    other_out = swap_col(mine_out)

    norms, grads, partials, others = [], [], [], []
    last = [left]
    pieces = []

    def triangles(s):
        partials.append(
            triangle(row_count, slot, halves[s], chain_lengths, left, groups[s], padded, last)
        )
        others.append(swap_col(partials[s]))
        last[:] = [partials[s]]

    def normal(s):
        places = [place for _, _, place in halves[s]]
        grad, norm = triangle_norm(
            row_count, places, partials[s], others[s], [mine_out, other_out], w_out, out_gain, out_bias, last
        )
        grads.append(grad)
        norms.append(norm)
        last[:] = [grad]

    def add_left(s):
        picks = range(len(halves[s]))
        pieces[:] = [
            left_gradient(halves[s], picks, grads[s], groups[s], pieces[:], last)
        ]
        last[:] = pieces

    def scatter(s, picks, arrived, dtype=bf16):
        x, y = hop(
            row_count,
            slot,
            [halves[s][pick][2] for pick in picks],
            chain_lengths,
            left,
            [grads[s]] * 2,
            picks,
            arrived,
            (short, half, hidden),
            dtype,
            last,
        )
        last[:] = [x]
        return x, y

    arrived = {0: [], 1: []}

    def send(s, chain, after=()):
        group, picks = 2 * s - 1 + chain, [0, 1]
        if arrived[chain]:
            terms = scatter(group, picks, [], f32)
            x, y = call(
                add_kernel,
                "scatter_add",
                [*terms, *arrived[chain]],
                [VMEM] * 4,
                [shape_of((short, half, hidden), bf16)] * 2,
                (),
                [*last, *after],
            )
            last[:] = [x]
        else:
            x, y = scatter(group, picks, [])
        arrived[chain] = [behind(x), ahead(y)]

    def output_side():
        return call(
            functools.partial(output_kernel, row_count, slot, [len(h) for h in halves]),
            "output_side",
            [chain_lengths, normed, cotangent, pieces[0], w_in, w_out, mine_out, *norms],
            [SMEM] + [VMEM] * (6 + len(norms)),
            [
                shape_of(block, bf16),
                shape_of(block, f32),
                shape_of((channels, 4 * hidden), f32),
            ],
            [
                mask,
                pltpu.VMEM((row_count, here, padded, hidden), bf16),
            ],
            last,
            microseconds=6,
        )

    for s in range(steps):
        if s and s + 2 < steps:
            x, y, _ = lax.optimization_barrier((*groups[s], last[0]))
            gather(x, y)
        if s == steps - 1:
            normal(s - 1)
            send(hops - 1, 1)
        triangles(s)
        if 0 < s < steps - 1:
            normal(s - 1)
    waiting = list(range(steps))

    def add_lefts(count):
        for _ in range(min(count, len(waiting))):
            add_left(waiting.pop(0))

    add_lefts(1)
    normal(steps - 1)
    send(hops, 0)
    add_lefts(1)
    send(hops - 2, 1)
    for s in range(hops - 1, 0, -1):
        add_lefts(1)
        if s == 1:
            own_a, own_b = scatter(0, [0, 1], [], f32)
            add_lefts(2)
        send(s, 0, arrived[1] if s == 1 else ())
        if s > 2:
            add_lefts(1)
            send(s - 2, 1)
    add_lefts(steps)
    update, gradient, early = output_side()
    arrived1, arrived2 = arrived[0], [arrived[1][1], arrived[1][0]]

    late, keep, give = call(
        functools.partial(right_gradient_kernel, slot),
        "right_gradient",
        [chain_lengths, normed, w_in, early, own_a, own_b]
        + [arrived1[0], arrived2[0], arrived1[1], arrived2[1]],
        [SMEM] + [VMEM] * 9,
        [shape_of((here, half, 2 * hidden), bf16)]
        + [shape_of((channels // 2, 6 * hidden), bf16)] * 2,
        [mask, pltpu.VMEM((channels, 2 * hidden), f32)],
    )
    mine = add(keep, swap_col(give))

    def from_row(apart):
        return lax.ppermute(mine, "row", [(r, r ^ apart) for r in range(row_count)])

    step = 1
    if row_count % 4 == 0:
        one, two, three = [from_row(apart).astype(f32) for apart in (1, 2, 3)]
        mine = ((mine.astype(f32) + one) + (two + three)).astype(bf16)
        step = 4
    while step < row_count:
        mine = add(mine, from_row(step))
        step *= 2
    (pair_gradient,) = call(
        pair_gradient_kernel,
        "pair_gradient",
        [pair, late, in_gain, w_in, gradient],
        [VMEM] * 5,
        [shape_of(block, bf16)],
        microseconds=3,
    )
    mine, pair_gradient = lax.optimization_barrier((mine, pair_gradient))
    grad_w_in, grad_w_out = call(
        weights_kernel,
        "weight_gradients",
        [mine, swap_col(mine)],
        [VMEM] * 2,
        [shape_of(w_in.shape, f32), shape_of(w_out.shape, f32)],
    )
    return (update, pair_gradient, grad_w_in, grad_w_out)


def solution(mesh):
    placed = (
        P(("grp", "row"), "col", None),
        P(("grp", "row"), "col", None),
        P("grp"),
        P(),
        P(),
        P(),
        P(),
        P(),
        P(),
    )
    return jax.shard_map(
        shards,
        mesh=mesh,
        in_specs=placed,
        out_specs=(
            P(("grp", "row"), "col", None),
            P(("grp", "row"), "col", None),
            P("grp", None),
            P("grp", None),
        ),
        check_vma=False,
    )
```

```python
import functools
import math

import jax
import jax.numpy as jnp
from jax import lax
from jax.experimental import pallas as pl
from jax.experimental.pallas import tpu as pltpu
from jax.sharding import PartitionSpec as P

eps = 1e-05
f32 = jnp.float32
bf16 = jnp.bfloat16
VMEM = pl.BlockSpec(memory_space=pltpu.VMEM)
SMEM = pl.BlockSpec(memory_space=pltpu.SMEM)
ANY = pl.BlockSpec(memory_space=pl.ANY)
MIB = 1 << 20


def layer_norm_backward(output_gradient, standardized_input, inverse_deviation, norm_gain):
    scaled_output = output_gradient * norm_gain
    first_operand = jnp.mean(scaled_output, axis=-1, keepdims=True)
    second_operand = jnp.mean(scaled_output * standardized_input, axis=-1, keepdims=True)
    return inverse_deviation * (scaled_output - first_operand - standardized_input * second_operand)


def standardize(values):
    centered = values - jnp.mean(values, axis=-1, keepdims=True)
    inverse = lax.rsqrt(jnp.mean(centered * centered, axis=-1, keepdims=True) + eps)
    return centered * inverse, inverse


def dot(a, b, ca, cb):
    return lax.dot_general(a, b, (((ca,), (cb,)), ((), ())), preferred_element_type=f32)


def ring_order(row_count):
    if row_count == 8:
        return [0, 2, 4, 6, 7, 5, 3, 1]
    return list(range(row_count))


def ring_place(row_count, row):
    if row_count == 8:
        return jnp.where(row % 2 == 0, row // 2, row_count - 1 - row // 2)
    return row


def ring_row(row_count, place):
    if row_count == 8:
        return jnp.where(place < row_count // 2, 2 * place, 2 * (row_count - 1 - place) + 1)
    return place


def half_index(row_count, offset, letter):
    place = ring_place(row_count, lax.axis_index("row"))
    return ring_row(row_count, (place + offset + row_count) % row_count) * 2 + letter


def arrival_slot(row_count, index):
    hops = row_count // 2
    letter = index % 2
    apart = ring_place(row_count, index // 2) - ring_place(row_count, lax.axis_index("row"))
    apart = (apart + row_count) % row_count
    near = jnp.where(letter == 0, row_count - apart, apart)
    first = 4 * near - 2 + letter
    second = 4 * (row_count - near) + 1 - letter
    return jnp.where(apart == 0, letter, jnp.where(near <= hops, first, second))


def present_count(row_count, lengths, slot, short, where):
    start = half_index(row_count, *where) * short
    return jnp.clip(lengths[start // slot] - start % slot, 0, short)


def swap_col(x):
    return lax.ppermute(x, "col", [(0, 1), (1, 0)])


def add(a, b):
    return (a.astype(f32) + b.astype(f32)).astype(bf16)


def call(kernel, name, args, specs, outs, scratch=(), after=(), microseconds=0, limit=0):
    held = sum(a.size * a.dtype.itemsize for a, s in zip(args, specs) if s is VMEM)
    after = [x for x in after if x is not None]
    held += sum(int(o.size) * o.dtype.itemsize for o in outs)
    held += sum(math.prod(s.inner_aval.shape) * 4 for s in scratch)

    def body(*refs):
        kernel(*refs[: len(args)], *refs[len(args) + len(after) :])

    return pl.pallas_call(
        body,
        out_shape=list(outs),
        in_specs=list(specs) + [ANY] * len(after),
        out_specs=[VMEM] * len(outs),
        scratch_shapes=list(scratch),
        compiler_params=pltpu.CompilerParams(vmem_limit_bytes=limit or min(56 * MIB, held * 5 // 4 + 6 * MIB)),
        cost_estimate=pl.CostEstimate(
            flops=int(microseconds * 1.1e9) + 1024, bytes_accessed=1024, transcendentals=0
        ),
        name=name,
    )(*args, *after)


def tiles(half):
    return [(k, min(16, half - k)) for k in range(0, half, 16)]


def parts(short):
    return [(0, (short + 1) // 2), ((short + 1) // 2, short)]


def joined(terms):
    chains = [terms[0::2], terms[1::2]]
    sums = []
    for chain in chains:
        total = chain[0]
        for term in chain[1:]:
            total = total + term
        sums.append(total.astype(f32))
    return sums[0] + sums[1]


def wide_row(ref, *at):
    return jnp.broadcast_to(ref[at], (16, ref.shape[-1])).astype(bf16)


def shape_of(dims, dtype):
    return jax.ShapeDtypeStruct(dims, dtype)


def present_row(lengths, slot, position):
    return (position % slot < lengths[position // slot]).astype(f32)


def present_columns(lengths, slot, half):
    at = lax.axis_index("col") * half + lax.broadcasted_iota(jnp.int32, (half, 128), 0)
    chain = at // slot
    held = jnp.zeros((half, 128), jnp.int32)
    for c in range(lengths.shape[0]):
        held = jnp.where(chain == c, lengths[c], held)
    return (at - chain * slot < held).astype(f32)


def first_row(here):
    return lax.axis_index("row") * here


def input_kernel(slot, lengths, pair, gain, bias, w, right_a, right_b, normed, mask):
    here, half, hidden = pair.shape
    mask[...] = present_columns(lengths, slot, half)

    for i in range(here):
        standard, _ = standardize(pair[i].astype(f32))
        values = (standard * gain[...] + bias[...]).astype(bf16)
        normed[i] = values
        proj = dot(values, w[:, 2 * hidden : 4 * hidden], 1, 0)
        shown = mask[...] * present_row(lengths, slot, first_row(here) + i)
        gated = jax.nn.sigmoid(proj[:, :hidden]) * proj[:, hidden:]
        out, at = (right_a, i) if i < here // 2 else (right_b, i - here // 2)
        out[at] = (shown * gated).astype(bf16)


def by_rows(here, body):
    def step(t, carry):
        for x in range(here // 2):
            body(t * (here // 2) + x)
        return carry

    lax.fori_loop(0, 2, step, 0)


def left_kernel(slot, lengths, normed, cotangent, w, left, outs, mask):
    here, half, hidden = normed.shape
    halves, _, padded, _ = outs.shape
    short = half // halves
    mask[...] = present_columns(lengths, slot, half)

    def body(i):
        proj = dot(normed[i], w[:, : 2 * hidden], 1, 0)
        shown = mask[...] * present_row(lengths, slot, first_row(here) + i)
        gated = shown * jax.nn.sigmoid(proj[:, :hidden]) * proj[:, hidden:]
        left[i] = gated.astype(bf16)
        gate = jax.nn.sigmoid(dot(normed[i], w[:, 4 * hidden :], 1, 0))
        grads = cotangent[i].astype(f32) * gate
        empty = jnp.zeros((padded - short, hidden), f32)
        for m in range(halves):
            part = grads[m * short : (m + 1) * short]
            outs[m, i] = jnp.concatenate([part, empty], axis=0).astype(bf16)

    by_rows(here, body)


def triangle_kernel(row_count, slot, halves, arrays, lengths, left, *refs):
    rights, (out, partial, rows) = refs[:arrays], refs[arrays:]
    here, half, hidden = left.shape
    padded = out.shape[2]
    short = here // 2
    cuts = tiles(half)
    for s, (array, first, place) in enumerate(halves):
        rows[...] = jnp.zeros_like(rows)

        def columns(pair, carry, right=rights[array], first=first):
            at = [jnp.minimum(2 * pair + x, short - 1) for x in range(2)]
            held = [[right[first + j, pl.ds(k, size), :] for k, size in cuts] for j in at]
            for i in range(here):
                given = [left[i, pl.ds(k, size), :] for k, size in cuts]
                for x in range(2):
                    products = [a * b for a, b in zip(given, held[x])]
                    rest = products.pop() if half % 16 else None
                    total = products[0]
                    for product in products[1:]:
                        total = total + product
                    total = total.astype(f32)
                    total = total[:8] + total[8:]
                    if rest is not None:
                        total += rest.astype(f32)
                    partial[x, pl.ds(8 * i, 8), :] = total
            for x in range(2):
                total = partial[x, pl.ds(0, here, stride=8), :]
                for sub in range(1, 8):
                    total += partial[x, pl.ds(sub, here, stride=8), :]
                rows[pl.ds(at[x], here, stride=padded), :] = total
            return carry

        present = present_count(row_count, lengths, slot, short, place)
        lax.fori_loop(0, (present + 1) // 2, columns, 0)
        out[s] = rows[...].astype(bf16).reshape(here, padded, hidden)


def triangle(row_count, slot, halves, lengths, left, rights, padded, after):
    count, (here, half, hidden) = len(halves), left.shape
    return call(
        functools.partial(triangle_kernel, row_count, slot, halves, len(rights)),
        "triangle",
        [lengths, left, *rights],
        [SMEM] + [VMEM] * (len(rights) + 1),
        [shape_of((count, here, padded, hidden), bf16)],
        [
            pltpu.VMEM((2, here * 8, hidden), f32),
            pltpu.VMEM((here * padded, hidden), f32),
        ],
        after,
    )[0]


def triangle_norm_kernel(
    row_count, places, mine, other, mine_out, other_out, w_out, gain, bias, grad, normed
):
    count, here, padded, hidden = mine.shape
    flat = (here * padded, hidden)

    for s in range(count):
        index = half_index(row_count, *places[s])
        outs = jnp.where(
            index // row_count == lax.axis_index("col"),
            mine_out[index % row_count],
            other_out[index % row_count],
        )
        total = (mine[s].astype(f32) + other[s].astype(f32)).reshape(flat)
        standard, inverse = standardize(total)
        normed[s] = (standard * gain[...] + bias[...]).astype(bf16).reshape(here, padded, hidden)
        grad_norm = dot(outs.reshape(flat), w_out[...], 1, 1)
        result = layer_norm_backward(grad_norm, standard, inverse, gain[...])
        grad[s] = result.astype(bf16).reshape(here, padded, hidden)


def triangle_norm(row_count, places, mine, other, outs, w_out, gain, bias, after):
    return call(
        functools.partial(triangle_norm_kernel, row_count, places),
        "triangle_norm",
        [mine, other, *outs, w_out, gain, bias],
        [VMEM] * 7,
        [shape_of(mine.shape, bf16)] * 2,
        (),
        after,
    )


def hop_kernel(row_count, slot, places, picks, carried, lengths, left, *refs):
    count = len(picks)
    grads, refs = refs[:count], refs[count:]
    arrived, refs = refs[: count * carried], refs[count * carried :]
    outs, wide = refs[:count], refs[count]
    here = left.shape[0]
    short, half, hidden = outs[0].shape
    for s in range(count):
        wide[...] = grads[s][picks[s]].astype(f32)
        out = outs[s]

        def columns(at, s=s, out=out):
            totals = []
            for j in at:
                total = []
                for k, size in tiles(half):
                    start = jnp.zeros((size, hidden), f32)
                    for more in range(carried):
                        start += arrived[s + more * count][j, pl.ds(k, size), :].astype(f32)
                    total.append(start)
                totals.append(total)
            for low in range(0, here, short):
                chosen = range(low, min(low + short, here))
                weights = [[wide_row(wide, i, pl.ds(j, 1)) for i in chosen] for j in at]
                for t, (k, size) in enumerate(tiles(half)):
                    held = [left[i, pl.ds(k, size), :] for i in chosen]
                    for total, weight in zip(totals, weights):
                        total[t] += joined([w[:size] * h for w, h in zip(weight, held)])
            for j, total in zip(at, totals):
                for t, (k, size) in enumerate(tiles(half)):
                    out[j, pl.ds(k, size), :] = total[t].astype(out.dtype)

        present = present_count(row_count, lengths, slot, short, places[s])
        for low, high in parts(short):

            @pl.when(present > low)
            def _(low=low, high=high, columns=columns):
                for j in range(low, high, 2):
                    columns(range(j, min(j + 2, high)))

            @pl.when(present <= low)
            def _(low=low, high=high, out=out):
                out[pl.ds(low, high - low)] = jnp.zeros((high - low, half, hidden), out.dtype)


def hop(row_count, slot, places, lengths, left, grads, picks, arrived, out, dtype, after):
    count = len(grads)
    carried = len(arrived) // count
    return call(
        functools.partial(hop_kernel, row_count, slot, places, picks, carried),
        "scatter_hop",
        [lengths, left, *grads, *arrived],
        [SMEM] + [VMEM] * (1 + count + len(arrived)),
        [shape_of(out, dtype)] * count,
        [pltpu.VMEM(grads[0].shape[1:], f32)],
        after,
    )


def add_kernel(one, two, first, second, out_one, out_two):
    out_one[...] = (one[...] + first[...].astype(f32)).astype(bf16)
    out_two[...] = (two[...] + second[...].astype(f32)).astype(bf16)


def left_gradient_kernel(halves, picks, arrays, carried, grads, *refs):
    count = len(picks)
    rights, refs = refs[:arrays], refs[arrays:]
    before, (out, wide) = refs[:carried], refs[carried:]
    here, half, hidden = out.shape
    short = here // 2
    for s, pick in enumerate(picks):
        wide[s] = grads[pick].astype(f32)

    def row(pair, carry):
        rows = (2 * pair, 2 * pair + 1)
        for s, pick in enumerate(picks):
            array, first, _ = halves[pick]
            weights = [[wide_row(wide, s, i, pl.ds(j, 1)) for j in range(short)] for i in rows]
            for k, size in tiles(half):
                held = [rights[array][first + j, pl.ds(k, size), :] for j in range(short)]
                for i, weight in zip(rows, weights):
                    total = joined([w[:size] * h for w, h in zip(weight, held)])
                    if s:
                        total += out[i, pl.ds(k, size), :]
                    elif carried:
                        total += before[0][i, pl.ds(k, size), :]
                    out[i, pl.ds(k, size), :] = total
        return carry

    lax.fori_loop(0, here // 2, row, 0)


def left_gradient(halves, picks, grads, rights, before, after):
    count, here = len(picks), grads.shape[1]
    half, hidden = rights[0].shape[1:]
    return call(
        functools.partial(left_gradient_kernel, halves, picks, len(rights), len(before)),
        "left_gradient",
        [grads, *rights, *before],
        [VMEM] * (1 + len(rights) + len(before)),
        [shape_of((here, half, hidden), f32)],
        [pltpu.VMEM((count,) + grads.shape[1:], f32)],
        after,
    )[0]


def output_kernel(
    row_count, slot, counts, lengths, normed, cotangent, grad_left, w, w_out, outs, *refs
):
    norms, (update, gradient, total, mask, picked) = refs[: len(counts)], refs[len(counts) :]
    here, half, hidden = normed.shape
    halves, _, padded, _ = picked.shape
    short = half // halves
    mask[...] = present_columns(lengths, slot, half)
    total[...] = jnp.zeros_like(total)
    for m in range(halves):
        low = 0
        stands = arrival_slot(row_count, lax.axis_index("col") * row_count + m)
        for norm, count in zip(norms, counts):

            @pl.when((stands >= low) & (stands < low + count))
            def _(m=m, norm=norm, low=low, stands=stands):
                picked[m] = norm[stands - low]

            low += count

    def body(i):
        values = normed[i]
        proj = dot(values, w[:, : 2 * hidden], 1, 0)
        sig_left = jax.nn.sigmoid(proj[:, :hidden])
        val_left = proj[:, hidden:]
        gate = jax.nn.sigmoid(dot(values, w[:, 4 * hidden :], 1, 0))
        tri = picked[:, i].reshape(halves * padded, hidden)
        product = dot(tri, w_out[...], 1, 0)
        projected = jnp.concatenate(
            [product[m * padded : m * padded + short] for m in range(halves)], axis=0
        )
        update[i] = (gate * projected).astype(bf16)
        grad_gate = (cotangent[i].astype(f32) * projected * gate * (1.0 - gate)).astype(bf16)
        shown = mask[...] * present_row(lengths, slot, first_row(here) + i)
        masked = grad_left[i] * shown
        grads = jnp.concatenate(
            [masked * val_left * sig_left * (1.0 - sig_left), masked * sig_left], axis=1
        ).astype(bf16)
        gradient[i] = dot(grads, w[:, : 2 * hidden], 1, 1) + dot(
            grad_gate, w[:, 4 * hidden :], 1, 1
        )
        total[:, : 2 * hidden] += dot(values, grads, 0, 0)
        total[:, 2 * hidden : 3 * hidden] += dot(values, grad_gate, 0, 0)
        total[:, 3 * hidden :] += dot(tri, outs[:, i].reshape(halves * padded, hidden), 0, 0)

    by_rows(here, body)


def right_gradient_kernel(slot, lengths, normed, w, early, own_a, own_b, *refs):
    arrived, (grads, keep, give, mask, total) = refs[:4], refs[4:]
    here, half, hidden = normed.shape
    short = here // 2
    mask[...] = present_columns(lengths, slot, half)
    total[...] = jnp.zeros_like(total)

    for own, others, first in ((own_a, arrived[:2], 0), (own_b, arrived[2:], short)):
        for t in range(short):
            j = first + t
            values = normed[j]
            proj = dot(values, w[:, 2 * hidden : 4 * hidden], 1, 0)
            sig_right = jax.nn.sigmoid(proj[:, :hidden])
            val_right = proj[:, hidden:]
            shown = mask[...] * present_row(lengths, slot, first_row(here) + j)
            masked = shown * (own[t] + others[0][t].astype(f32) + others[1][t].astype(f32))
            result = jnp.concatenate(
                [masked * val_right * sig_right * (1.0 - sig_right), masked * sig_right], axis=1
            ).astype(bf16)
            grads[j] = result
            total[...] += dot(values, result, 0, 0)
    rows, wide = keep.shape[0], early.shape[1]
    col = lax.axis_index("col")
    for out, start in ((keep, col * rows), (give, (1 - col) * rows)):
        chosen = pl.ds(pl.multiple_of(start, rows), rows)
        out[:, :wide] = early[chosen, :].astype(bf16)
        out[:, wide:] = total[chosen, :].astype(bf16)


def pair_gradient_kernel(pair, grads, gain, w, *refs):
    gradients, out = refs[:-1], refs[-1]
    hidden = pair.shape[2]

    i = 0
    for gradient in gradients:
        for at in range(gradient.shape[0]):
            standard, inverse = standardize(pair[i].astype(f32))
            total = gradient[at] + dot(grads[i], w[:, 2 * hidden : 4 * hidden], 1, 1)
            out[i] = layer_norm_backward(total, standard, inverse, gain[...]).astype(bf16)
            i += 1


def weights_kernel(mine, other, w_in, w_out):
    rows, hidden = mine.shape[0], w_out.shape[0]
    col = lax.axis_index("col")
    for part, start in ((mine, col * rows), (other, (1 - col) * rows)):
        chosen = pl.ds(pl.multiple_of(start, rows), rows)
        w_in[chosen, : 2 * hidden] = part[:, : 2 * hidden].astype(f32)
        w_in[chosen, 2 * hidden : 4 * hidden] = part[:, 4 * hidden :].astype(f32)
        w_in[chosen, 4 * hidden :] = part[:, 2 * hidden : 3 * hidden].astype(f32)
        w_out[chosen, :] = part[:, 3 * hidden : 4 * hidden].astype(f32)


def shards(
    pair,
    cotangent,
    chain_lengths,
    input_norm_gain,
    input_norm_bias,
    w_in,
    output_norm_gain,
    output_norm_bias,
    w_out,
):
    here, half, channels = pair.shape
    hidden = w_out.shape[0]
    row_count = lax.axis_size("row")
    slot = here * row_count // chain_lengths.shape[0]
    order = ring_order(row_count)
    short = here // 2
    padded = (short + 15) // 16 * 16
    forward = [(order[p], order[(p + 1) % row_count]) for p in range(row_count)]
    backward = [(order[p], order[(p - 1) % row_count]) for p in range(row_count)]
    in_gain, in_bias = input_norm_gain.reshape(1, -1), input_norm_bias.reshape(1, -1)
    out_gain, out_bias = output_norm_gain.reshape(1, -1), output_norm_bias.reshape(1, -1)
    block = (here, half, hidden)
    mask = pltpu.VMEM((half, 128), f32)

    def ahead(x):
        return lax.ppermute(x, "row", forward)

    def behind(x):
        return lax.ppermute(x, "row", backward)

    right_a, right_b, normed = call(
        functools.partial(input_kernel, slot),
        "input_side",
        [chain_lengths, pair, in_gain, in_bias, w_in],
        [SMEM] + [VMEM] * 4,
        [shape_of((short, half, hidden), bf16)] * 2 + [shape_of(block, bf16)],
        [mask],
    )

    hops = row_count // 2
    steps = 2 * hops
    groups = [[right_a, right_b]]
    halves = [[(0, 0, (0, 0)), (1, 0, (0, 1))]]
    for s in range(1, hops + 1):
        halves.append([(0, 0, (-s, 0)), (1, 0, (s, 1))])
        if s < hops:
            halves.append([(0, 0, (-s, 1)), (1, 0, (s, 0))])

    def gather(x, y):
        groups.append([ahead(x), behind(y)])

    gather(right_a, right_b)
    gather(right_b, right_a)
    left, mine_out = call(
        functools.partial(left_kernel, slot),
        "left_side",
        [chain_lengths, normed, cotangent, w_in],
        [SMEM] + [VMEM] * 3,
        [shape_of(block, bf16), shape_of((row_count, here, padded, hidden), bf16)],
        [mask],
        microseconds=4,
    )
    other_out = swap_col(mine_out)

    norms, grads, partials, others = [], [], [], []
    last = [left]
    pieces = []

    def triangles(s):
        partials.append(
            triangle(row_count, slot, halves[s], chain_lengths, left, groups[s], padded, last)
        )
        others.append(swap_col(partials[s]))
        last[:] = [partials[s]]

    def normal(s):
        places = [place for _, _, place in halves[s]]
        grad, norm = triangle_norm(
            row_count, places, partials[s], others[s], [mine_out, other_out], w_out, out_gain, out_bias, last
        )
        grads.append(grad)
        norms.append(norm)
        last[:] = [grad]

    def add_left(s):
        picks = range(len(halves[s]))
        pieces[:] = [
            left_gradient(halves[s], picks, grads[s], groups[s], pieces[:], last)
        ]
        last[:] = pieces

    def scatter(s, picks, arrived, dtype=bf16):
        x, y = hop(
            row_count,
            slot,
            [halves[s][pick][2] for pick in picks],
            chain_lengths,
            left,
            [grads[s]] * 2,
            picks,
            arrived,
            (short, half, hidden),
            dtype,
            last,
        )
        last[:] = [x]
        return x, y

    arrived = {0: [], 1: []}

    prepared = {}

    def prepare(s, chain):
        prepared[s, chain] = scatter(2 * s - 1 + chain, [0, 1], [], f32)

    def send(s, chain, after=()):
        if arrived[chain]:
            x, y = call(
                add_kernel,
                "scatter_add",
                [*prepared[s, chain], *arrived[chain]],
                [VMEM] * 4,
                [shape_of((short, half, hidden), bf16)] * 2,
                (),
                [*last, *after],
            )
            last[:] = [x]
        else:
            x, y = scatter(2 * s - 1 + chain, [0, 1], [])
        arrived[chain] = [behind(x), ahead(y)]

    def output_side():
        return call(
            functools.partial(output_kernel, row_count, slot, [len(h) for h in halves]),
            "output_side",
            [chain_lengths, normed, cotangent, pieces[0], w_in, w_out, mine_out, *norms],
            [SMEM] + [VMEM] * (6 + len(norms)),
            [
                shape_of(block, bf16),
                shape_of(block, f32),
                shape_of((channels, 4 * hidden), f32),
            ],
            [
                mask,
                pltpu.VMEM((row_count, here, padded, hidden), bf16),
            ],
            last,
            microseconds=6,
        )

    for s in range(steps):
        if s and s + 2 < steps:
            x, y, _ = lax.optimization_barrier((*groups[s], last[0]))
            gather(x, y)
        if s == steps - 1:
            normal(s - 1)
            send(hops - 1, 1)
        triangles(s)
        if 0 < s < steps - 1:
            normal(s - 1)
    waiting = list(range(steps))

    def add_lefts(count):
        for _ in range(min(count, len(waiting))):
            add_left(waiting.pop(0))

    add_lefts(1)
    normal(steps - 1)
    send(hops, 0)
    add_lefts(1)
    prepare(hops - 2, 1)
    prepare(hops - 1, 0)
    for s in range(hops - 1, 0, -1):
        if s > 1:
            send(s - 1, 1)
        send(s, 0, arrived[1] if s == 1 else ())
        if s == 2:
            own_a, own_b = scatter(0, [0, 1], [], f32)
        if s > 1:
            add_lefts(1)
            if s > 2:
                prepare(s - 2, 1)
            prepare(s - 1, 0)
            add_lefts(1 if s > 2 else 2)
    add_lefts(steps)
    update, gradient, early = output_side()
    arrived1, arrived2 = arrived[0], [arrived[1][1], arrived[1][0]]

    late, keep, give = call(
        functools.partial(right_gradient_kernel, slot),
        "right_gradient",
        [chain_lengths, normed, w_in, early, own_a, own_b]
        + [arrived1[0], arrived2[0], arrived1[1], arrived2[1]],
        [SMEM] + [VMEM] * 9,
        [shape_of((here, half, 2 * hidden), bf16)]
        + [shape_of((channels // 2, 6 * hidden), bf16)] * 2,
        [mask, pltpu.VMEM((channels, 2 * hidden), f32)],
    )
    mine = add(keep, swap_col(give))

    def from_row(apart):
        return lax.ppermute(mine, "row", [(r, r ^ apart) for r in range(row_count)])

    step = 1
    if row_count % 4 == 0:
        one, two, three = [from_row(apart).astype(f32) for apart in (1, 2, 3)]
        mine = ((mine.astype(f32) + one) + (two + three)).astype(bf16)
        step = 4
    while step < row_count:
        mine = add(mine, from_row(step))
        step *= 2
    (pair_gradient,) = call(
        pair_gradient_kernel,
        "pair_gradient",
        [pair, late, in_gain, w_in, gradient],
        [VMEM] * 5,
        [shape_of(block, bf16)],
        microseconds=3,
    )
    mine, pair_gradient = lax.optimization_barrier((mine, pair_gradient))
    grad_w_in, grad_w_out = call(
        weights_kernel,
        "weight_gradients",
        [mine, swap_col(mine)],
        [VMEM] * 2,
        [shape_of(w_in.shape, f32), shape_of(w_out.shape, f32)],
    )
    return (update, pair_gradient, grad_w_in, grad_w_out)


def solution(mesh):
    placed = (
        P(("grp", "row"), "col", None),
        P(("grp", "row"), "col", None),
        P("grp"),
        P(),
        P(),
        P(),
        P(),
        P(),
        P(),
    )
    return jax.shard_map(
        shards,
        mesh=mesh,
        in_specs=placed,
        out_specs=(
            P(("grp", "row"), "col", None),
            P(("grp", "row"), "col", None),
            P("grp", None),
            P("grp", None),
        ),
        check_vma=False,
    )
```

```python
import functools
import math

import jax
import jax.numpy as jnp
from jax import lax
from jax.experimental import pallas as pl
from jax.experimental.pallas import tpu as pltpu
from jax.sharding import PartitionSpec as P

eps = 1e-05
f32 = jnp.float32
bf16 = jnp.bfloat16
VMEM = pl.BlockSpec(memory_space=pltpu.VMEM)
SMEM = pl.BlockSpec(memory_space=pltpu.SMEM)
ANY = pl.BlockSpec(memory_space=pl.ANY)
MIB = 1 << 20


def layer_norm_backward(output_gradient, standardized_input, inverse_deviation, norm_gain):
    scaled_output = output_gradient * norm_gain
    first_operand = jnp.mean(scaled_output, axis=-1, keepdims=True)
    second_operand = jnp.mean(scaled_output * standardized_input, axis=-1, keepdims=True)
    return inverse_deviation * (scaled_output - first_operand - standardized_input * second_operand)


def standardize(values):
    centered = values - jnp.mean(values, axis=-1, keepdims=True)
    inverse = lax.rsqrt(jnp.mean(centered * centered, axis=-1, keepdims=True) + eps)
    return centered * inverse, inverse


def dot(a, b, ca, cb):
    return lax.dot_general(a, b, (((ca,), (cb,)), ((), ())), preferred_element_type=f32)


def ring_order(row_count):
    if row_count == 8:
        return [0, 2, 4, 6, 7, 5, 3, 1]
    return list(range(row_count))


def ring_place(row_count, row):
    if row_count == 8:
        return jnp.where(row % 2 == 0, row // 2, row_count - 1 - row // 2)
    return row


def ring_row(row_count, place):
    if row_count == 8:
        return jnp.where(place < row_count // 2, 2 * place, 2 * (row_count - 1 - place) + 1)
    return place


def half_index(row_count, offset, letter):
    place = ring_place(row_count, lax.axis_index("row"))
    return ring_row(row_count, (place + offset + row_count) % row_count) * 2 + letter


def arrival_slot(row_count, index):
    hops = row_count // 2
    letter = index % 2
    apart = ring_place(row_count, index // 2) - ring_place(row_count, lax.axis_index("row"))
    apart = (apart + row_count) % row_count
    near = jnp.where(letter == 0, row_count - apart, apart)
    first = 4 * near - 2 + letter
    second = 4 * (row_count - near) + 1 - letter
    return jnp.where(apart == 0, letter, jnp.where(near <= hops, first, second))


def present_count(row_count, lengths, slot, short, where):
    start = half_index(row_count, *where) * short
    return jnp.clip(lengths[start // slot] - start % slot, 0, short)


def swap_col(x):
    return lax.ppermute(x, "col", [(0, 1), (1, 0)])


def add(a, b):
    return (a.astype(f32) + b.astype(f32)).astype(bf16)


def call(kernel, name, args, specs, outs, scratch=(), after=(), microseconds=0, limit=0):
    held = sum(a.size * a.dtype.itemsize for a, s in zip(args, specs) if s is VMEM)
    after = [x for x in after if x is not None]
    held += sum(int(o.size) * o.dtype.itemsize for o in outs)
    held += sum(math.prod(s.inner_aval.shape) * 4 for s in scratch)

    def body(*refs):
        kernel(*refs[: len(args)], *refs[len(args) + len(after) :])

    return pl.pallas_call(
        body,
        out_shape=list(outs),
        in_specs=list(specs) + [ANY] * len(after),
        out_specs=[VMEM] * len(outs),
        scratch_shapes=list(scratch),
        compiler_params=pltpu.CompilerParams(vmem_limit_bytes=limit or min(56 * MIB, held * 5 // 4 + 6 * MIB)),
        cost_estimate=pl.CostEstimate(
            flops=int(microseconds * 1.1e9) + 1024, bytes_accessed=1024, transcendentals=0
        ),
        name=name,
    )(*args, *after)


def tiles(half):
    return [(k, min(16, half - k)) for k in range(0, half, 16)]


def parts(short):
    return [(0, (short + 1) // 2), ((short + 1) // 2, short)]


def joined(terms):
    chains = [terms[0::2], terms[1::2]]
    sums = []
    for chain in chains:
        total = chain[0]
        for term in chain[1:]:
            total = total + term
        sums.append(total.astype(f32))
    return sums[0] + sums[1]


def wide_row(ref, *at):
    return jnp.broadcast_to(ref[at], (16, ref.shape[-1])).astype(bf16)


def shape_of(dims, dtype):
    return jax.ShapeDtypeStruct(dims, dtype)


def present_row(lengths, slot, position):
    return (position % slot < lengths[position // slot]).astype(f32)


def present_columns(lengths, slot, half):
    at = lax.axis_index("col") * half + lax.broadcasted_iota(jnp.int32, (half, 128), 0)
    chain = at // slot
    held = jnp.zeros((half, 128), jnp.int32)
    for c in range(lengths.shape[0]):
        held = jnp.where(chain == c, lengths[c], held)
    return (at - chain * slot < held).astype(f32)


def first_row(here):
    return lax.axis_index("row") * here


def input_kernel(slot, lengths, pair, gain, bias, w, right_a, right_b, normed, mask):
    here, half, hidden = pair.shape
    mask[...] = present_columns(lengths, slot, half)

    for i in range(here):
        standard, _ = standardize(pair[i].astype(f32))
        values = (standard * gain[...] + bias[...]).astype(bf16)
        normed[i] = values
        proj = dot(values, w[:, 2 * hidden : 4 * hidden], 1, 0)
        shown = mask[...] * present_row(lengths, slot, first_row(here) + i)
        gated = jax.nn.sigmoid(proj[:, :hidden]) * proj[:, hidden:]
        out, at = (right_a, i) if i < here // 2 else (right_b, i - here // 2)
        out[at] = (shown * gated).astype(bf16)


def by_rows(here, body):
    def step(t, carry):
        for x in range(here // 2):
            body(t * (here // 2) + x)
        return carry

    lax.fori_loop(0, 2, step, 0)


def left_kernel(slot, lengths, normed, cotangent, w, left, outs, mask):
    here, half, hidden = normed.shape
    halves, _, padded, _ = outs.shape
    short = half // halves
    mask[...] = present_columns(lengths, slot, half)

    def body(i):
        proj = dot(normed[i], w[:, : 2 * hidden], 1, 0)
        shown = mask[...] * present_row(lengths, slot, first_row(here) + i)
        gated = shown * jax.nn.sigmoid(proj[:, :hidden]) * proj[:, hidden:]
        left[i] = gated.astype(bf16)
        gate = jax.nn.sigmoid(dot(normed[i], w[:, 4 * hidden :], 1, 0))
        grads = cotangent[i].astype(f32) * gate
        empty = jnp.zeros((padded - short, hidden), f32)
        for m in range(halves):
            part = grads[m * short : (m + 1) * short]
            outs[m, i] = jnp.concatenate([part, empty], axis=0).astype(bf16)

    by_rows(here, body)


def triangle_kernel(row_count, slot, halves, arrays, lengths, left, *refs):
    rights, (out, partial, rows) = refs[:arrays], refs[arrays:]
    here, half, hidden = left.shape
    padded = out.shape[2]
    short = here // 2
    cuts = tiles(half)
    for s, (array, first, place) in enumerate(halves):
        rows[...] = jnp.zeros_like(rows)

        def columns(pair, carry, right=rights[array], first=first):
            at = [jnp.minimum(2 * pair + x, short - 1) for x in range(2)]
            held = [[right[first + j, pl.ds(k, size), :] for k, size in cuts] for j in at]
            for i in range(here):
                given = [left[i, pl.ds(k, size), :] for k, size in cuts]
                for x in range(2):
                    products = [a * b for a, b in zip(given, held[x])]
                    rest = products.pop() if half % 16 else None
                    total = products[0]
                    for product in products[1:]:
                        total = total + product
                    total = total.astype(f32)
                    total = total[:8] + total[8:]
                    if rest is not None:
                        total += rest.astype(f32)
                    partial[x, pl.ds(8 * i, 8), :] = total
            for x in range(2):
                total = partial[x, pl.ds(0, here, stride=8), :]
                for sub in range(1, 8):
                    total += partial[x, pl.ds(sub, here, stride=8), :]
                rows[pl.ds(at[x], here, stride=padded), :] = total
            return carry

        present = present_count(row_count, lengths, slot, short, place)
        lax.fori_loop(0, (present + 1) // 2, columns, 0)
        out[s] = rows[...].astype(bf16).reshape(here, padded, hidden)


def triangle(row_count, slot, halves, lengths, left, rights, padded, after):
    count, (here, half, hidden) = len(halves), left.shape
    return call(
        functools.partial(triangle_kernel, row_count, slot, halves, len(rights)),
        "triangle",
        [lengths, left, *rights],
        [SMEM] + [VMEM] * (len(rights) + 1),
        [shape_of((count, here, padded, hidden), bf16)],
        [
            pltpu.VMEM((2, here * 8, hidden), f32),
            pltpu.VMEM((here * padded, hidden), f32),
        ],
        after,
    )[0]


def triangle_norm_kernel(
    row_count, places, mine, other, mine_out, other_out, w_out, gain, bias, grad, normed
):
    count, here, padded, hidden = mine.shape
    flat = (here * padded, hidden)

    for s in range(count):
        index = half_index(row_count, *places[s])
        outs = jnp.where(
            index // row_count == lax.axis_index("col"),
            mine_out[index % row_count],
            other_out[index % row_count],
        )
        total = (mine[s].astype(f32) + other[s].astype(f32)).reshape(flat)
        standard, inverse = standardize(total)
        normed[s] = (standard * gain[...] + bias[...]).astype(bf16).reshape(here, padded, hidden)
        grad_norm = dot(outs.reshape(flat), w_out[...], 1, 1)
        result = layer_norm_backward(grad_norm, standard, inverse, gain[...])
        grad[s] = result.astype(bf16).reshape(here, padded, hidden)


def triangle_norm(row_count, places, mine, other, outs, w_out, gain, bias, after):
    return call(
        functools.partial(triangle_norm_kernel, row_count, places),
        "triangle_norm",
        [mine, other, *outs, w_out, gain, bias],
        [VMEM] * 7,
        [shape_of(mine.shape, bf16)] * 2,
        (),
        after,
    )


def hop_kernel(row_count, slot, places, picks, carried, lengths, left, *refs):
    count = len(picks)
    grads, refs = refs[:count], refs[count:]
    arrived, refs = refs[: count * carried], refs[count * carried :]
    outs, wide = refs[:count], refs[count]
    here = left.shape[0]
    short, half, hidden = outs[0].shape
    for s in range(count):
        wide[...] = grads[s][picks[s]].astype(f32)
        out = outs[s]

        def columns(at, s=s, out=out):
            totals = []
            for j in at:
                total = []
                for k, size in tiles(half):
                    start = jnp.zeros((size, hidden), f32)
                    for more in range(carried):
                        start += arrived[s + more * count][j, pl.ds(k, size), :].astype(f32)
                    total.append(start)
                totals.append(total)
            for low in range(0, here, short):
                chosen = range(low, min(low + short, here))
                weights = [[wide_row(wide, i, pl.ds(j, 1)) for i in chosen] for j in at]
                for t, (k, size) in enumerate(tiles(half)):
                    held = [left[i, pl.ds(k, size), :] for i in chosen]
                    for total, weight in zip(totals, weights):
                        total[t] += joined([w[:size] * h for w, h in zip(weight, held)])
            for j, total in zip(at, totals):
                for t, (k, size) in enumerate(tiles(half)):
                    out[j, pl.ds(k, size), :] = total[t].astype(out.dtype)

        present = present_count(row_count, lengths, slot, short, places[s])
        for low, high in parts(short):

            @pl.when(present > low)
            def _(low=low, high=high, columns=columns):
                for j in range(low, high, 2):
                    columns(range(j, min(j + 2, high)))

            @pl.when(present <= low)
            def _(low=low, high=high, out=out):
                out[pl.ds(low, high - low)] = jnp.zeros((high - low, half, hidden), out.dtype)


def hop(row_count, slot, places, lengths, left, grads, picks, arrived, out, dtype, after):
    count = len(grads)
    carried = len(arrived) // count
    return call(
        functools.partial(hop_kernel, row_count, slot, places, picks, carried),
        "scatter_hop",
        [lengths, left, *grads, *arrived],
        [SMEM] + [VMEM] * (1 + count + len(arrived)),
        [shape_of(out, dtype)] * count,
        [pltpu.VMEM(grads[0].shape[1:], f32)],
        after,
    )


def add_kernel(one, two, first, second, out_one, out_two):
    out_one[...] = (one[...] + first[...].astype(f32)).astype(bf16)
    out_two[...] = (two[...] + second[...].astype(f32)).astype(bf16)


def left_gradient_kernel(halves, picks, arrays, carried, grads, *refs):
    count = len(picks)
    rights, refs = refs[:arrays], refs[arrays:]
    before, (out, wide) = refs[:carried], refs[carried:]
    here, half, hidden = out.shape
    short = here // 2
    for s, pick in enumerate(picks):
        wide[s] = grads[pick].astype(f32)

    def row(pair, carry):
        rows = (2 * pair, 2 * pair + 1)
        for s, pick in enumerate(picks):
            array, first, _ = halves[pick]
            weights = [[wide_row(wide, s, i, pl.ds(j, 1)) for j in range(short)] for i in rows]
            for k, size in tiles(half):
                held = [rights[array][first + j, pl.ds(k, size), :] for j in range(short)]
                for i, weight in zip(rows, weights):
                    total = joined([w[:size] * h for w, h in zip(weight, held)])
                    if s:
                        total += out[i, pl.ds(k, size), :]
                    elif carried:
                        total += before[0][i, pl.ds(k, size), :]
                    out[i, pl.ds(k, size), :] = total
        return carry

    lax.fori_loop(0, here // 2, row, 0)


def left_gradient(halves, picks, grads, rights, before, after):
    count, here = len(picks), grads.shape[1]
    half, hidden = rights[0].shape[1:]
    return call(
        functools.partial(left_gradient_kernel, halves, picks, len(rights), len(before)),
        "left_gradient",
        [grads, *rights, *before],
        [VMEM] * (1 + len(rights) + len(before)),
        [shape_of((here, half, hidden), f32)],
        [pltpu.VMEM((count,) + grads.shape[1:], f32)],
        after,
    )[0]


def output_kernel(
    row_count, slot, counts, lengths, normed, cotangent, grad_left, w, w_out, outs, *refs
):
    norms, (update, gradient, total, mask, picked) = refs[: len(counts)], refs[len(counts) :]
    here, half, hidden = normed.shape
    halves, _, padded, _ = picked.shape
    short = half // halves
    mask[...] = present_columns(lengths, slot, half)
    total[...] = jnp.zeros_like(total)
    for m in range(halves):
        low = 0
        stands = arrival_slot(row_count, lax.axis_index("col") * row_count + m)
        for norm, count in zip(norms, counts):

            @pl.when((stands >= low) & (stands < low + count))
            def _(m=m, norm=norm, low=low, stands=stands):
                picked[m] = norm[stands - low]

            low += count

    def body(i):
        values = normed[i]
        proj = dot(values, w[:, : 2 * hidden], 1, 0)
        sig_left = jax.nn.sigmoid(proj[:, :hidden])
        val_left = proj[:, hidden:]
        gate = jax.nn.sigmoid(dot(values, w[:, 4 * hidden :], 1, 0))
        tri = picked[:, i].reshape(halves * padded, hidden)
        product = dot(tri, w_out[...], 1, 0)
        projected = jnp.concatenate(
            [product[m * padded : m * padded + short] for m in range(halves)], axis=0
        )
        update[i] = (gate * projected).astype(bf16)
        grad_gate = (cotangent[i].astype(f32) * projected * gate * (1.0 - gate)).astype(bf16)
        shown = mask[...] * present_row(lengths, slot, first_row(here) + i)
        masked = grad_left[i] * shown
        grads = jnp.concatenate(
            [masked * val_left * sig_left * (1.0 - sig_left), masked * sig_left], axis=1
        ).astype(bf16)
        gradient[i] = dot(grads, w[:, : 2 * hidden], 1, 1) + dot(
            grad_gate, w[:, 4 * hidden :], 1, 1
        )
        total[:, : 2 * hidden] += dot(values, grads, 0, 0)
        total[:, 2 * hidden : 3 * hidden] += dot(values, grad_gate, 0, 0)
        total[:, 3 * hidden :] += dot(tri, outs[:, i].reshape(halves * padded, hidden), 0, 0)

    by_rows(here, body)


def right_gradient_kernel(slot, lengths, normed, w, early, own_a, own_b, *refs):
    arrived, (grads, keep, give, mask, total) = refs[:4], refs[4:]
    here, half, hidden = normed.shape
    short = here // 2
    mask[...] = present_columns(lengths, slot, half)
    total[...] = jnp.zeros_like(total)

    for own, others, first in ((own_a, arrived[:2], 0), (own_b, arrived[2:], short)):
        for t in range(short):
            j = first + t
            values = normed[j]
            proj = dot(values, w[:, 2 * hidden : 4 * hidden], 1, 0)
            sig_right = jax.nn.sigmoid(proj[:, :hidden])
            val_right = proj[:, hidden:]
            shown = mask[...] * present_row(lengths, slot, first_row(here) + j)
            masked = shown * (own[t] + others[0][t].astype(f32) + others[1][t].astype(f32))
            result = jnp.concatenate(
                [masked * val_right * sig_right * (1.0 - sig_right), masked * sig_right], axis=1
            ).astype(bf16)
            grads[j] = result
            total[...] += dot(values, result, 0, 0)
    rows, wide = keep.shape[0], early.shape[1]
    col = lax.axis_index("col")
    for out, start in ((keep, col * rows), (give, (1 - col) * rows)):
        chosen = pl.ds(pl.multiple_of(start, rows), rows)
        out[:, :wide] = early[chosen, :].astype(bf16)
        out[:, wide:] = total[chosen, :].astype(bf16)


def pair_gradient_kernel(pair, grads, gain, w, *refs):
    gradients, out = refs[:-1], refs[-1]
    hidden = pair.shape[2]

    i = 0
    for gradient in gradients:
        for at in range(gradient.shape[0]):
            standard, inverse = standardize(pair[i].astype(f32))
            total = gradient[at] + dot(grads[i], w[:, 2 * hidden : 4 * hidden], 1, 1)
            out[i] = layer_norm_backward(total, standard, inverse, gain[...]).astype(bf16)
            i += 1


def weights_kernel(mine, other, w_in, w_out):
    rows, hidden = mine.shape[0], w_out.shape[0]
    col = lax.axis_index("col")
    for part, start in ((mine, col * rows), (other, (1 - col) * rows)):
        chosen = pl.ds(pl.multiple_of(start, rows), rows)
        w_in[chosen, : 2 * hidden] = part[:, : 2 * hidden].astype(f32)
        w_in[chosen, 2 * hidden : 4 * hidden] = part[:, 4 * hidden :].astype(f32)
        w_in[chosen, 4 * hidden :] = part[:, 2 * hidden : 3 * hidden].astype(f32)
        w_out[chosen, :] = part[:, 3 * hidden : 4 * hidden].astype(f32)


def shards(
    pair,
    cotangent,
    chain_lengths,
    input_norm_gain,
    input_norm_bias,
    w_in,
    output_norm_gain,
    output_norm_bias,
    w_out,
):
    here, half, channels = pair.shape
    hidden = w_out.shape[0]
    row_count = lax.axis_size("row")
    slot = here * row_count // chain_lengths.shape[0]
    order = ring_order(row_count)
    short = here // 2
    padded = (short + 15) // 16 * 16
    forward = [(order[p], order[(p + 1) % row_count]) for p in range(row_count)]
    backward = [(order[p], order[(p - 1) % row_count]) for p in range(row_count)]
    in_gain, in_bias = input_norm_gain.reshape(1, -1), input_norm_bias.reshape(1, -1)
    out_gain, out_bias = output_norm_gain.reshape(1, -1), output_norm_bias.reshape(1, -1)
    block = (here, half, hidden)
    mask = pltpu.VMEM((half, 128), f32)

    def ahead(x):
        return lax.ppermute(x, "row", forward)

    def behind(x):
        return lax.ppermute(x, "row", backward)

    right_a, right_b, normed = call(
        functools.partial(input_kernel, slot),
        "input_side",
        [chain_lengths, pair, in_gain, in_bias, w_in],
        [SMEM] + [VMEM] * 4,
        [shape_of((short, half, hidden), bf16)] * 2 + [shape_of(block, bf16)],
        [mask],
    )

    hops = row_count // 2
    steps = 2 * hops
    groups = [[right_a, right_b]]
    halves = [[(0, 0, (0, 0)), (1, 0, (0, 1))]]
    for s in range(1, hops + 1):
        halves.append([(0, 0, (-s, 0)), (1, 0, (s, 1))])
        if s < hops:
            halves.append([(0, 0, (-s, 1)), (1, 0, (s, 0))])

    def gather(x, y):
        groups.append([ahead(x), behind(y)])

    gather(right_a, right_b)
    gather(right_b, right_a)
    left, mine_out = call(
        functools.partial(left_kernel, slot),
        "left_side",
        [chain_lengths, normed, cotangent, w_in],
        [SMEM] + [VMEM] * 3,
        [shape_of(block, bf16), shape_of((row_count, here, padded, hidden), bf16)],
        [mask],
        microseconds=4,
    )
    other_out = swap_col(mine_out)

    norms, grads, partials, others = [], [], [], []
    last = [left]
    pieces = []

    def triangles(s):
        partials.append(
            triangle(row_count, slot, halves[s], chain_lengths, left, groups[s], padded, last)
        )
        last[:] = [partials[s]]

    def normal(s):
        places = [place for _, _, place in halves[s]]
        grad, norm = triangle_norm(
            row_count, places, partials[s], others[s], [mine_out, other_out], w_out, out_gain, out_bias, last
        )
        grads.append(grad)
        norms.append(norm)
        last[:] = [grad]

    def add_left(s):
        picks = range(len(halves[s]))
        pieces[:] = [
            left_gradient(halves[s], picks, grads[s], groups[s], pieces[:], last)
        ]
        last[:] = pieces

    def scatter(s, picks, arrived, dtype=bf16):
        x, y = hop(
            row_count,
            slot,
            [halves[s][pick][2] for pick in picks],
            chain_lengths,
            left,
            [grads[s]] * 2,
            picks,
            arrived,
            (short, half, hidden),
            dtype,
            last,
        )
        last[:] = [x]
        return x, y

    arrived = {0: [], 1: []}

    prepared = {}

    def prepare(s, chain):
        prepared[s, chain] = scatter(2 * s - 1 + chain, [0, 1], [], f32)

    def send(s, chain, after=()):
        if arrived[chain]:
            x, y = call(
                add_kernel,
                "scatter_add",
                [*prepared[s, chain], *arrived[chain]],
                [VMEM] * 4,
                [shape_of((short, half, hidden), bf16)] * 2,
                (),
                [*last, *after],
            )
            last[:] = [x]
        else:
            x, y = scatter(2 * s - 1 + chain, [0, 1], [])
        arrived[chain] = [behind(x), ahead(y)]

    def output_side():
        return call(
            functools.partial(output_kernel, row_count, slot, [len(h) for h in halves]),
            "output_side",
            [chain_lengths, normed, cotangent, pieces[0], w_in, w_out, mine_out, *norms],
            [SMEM] + [VMEM] * (6 + len(norms)),
            [
                shape_of(block, bf16),
                shape_of(block, f32),
                shape_of((channels, 4 * hidden), f32),
            ],
            [
                mask,
                pltpu.VMEM((row_count, here, padded, hidden), bf16),
            ],
            last,
            microseconds=6,
        )

    for s in range(steps):
        if s and s + 2 < steps:
            x, y, _ = lax.optimization_barrier((*groups[s], last[0]))
            gather(x, y)
        if s == steps - 1:
            normal(s - 1)
            send(hops - 1, 1)
        triangles(s)
        sent = partials[s]
        if 0 < s < steps - 1:
            normal(s - 1)
        if 2 < s < steps - 2:
            sent, _ = lax.optimization_barrier((sent, last[0]))
        others.append(swap_col(sent))
    waiting = list(range(steps))

    def add_lefts(count):
        for _ in range(min(count, len(waiting))):
            add_left(waiting.pop(0))

    add_lefts(1)
    normal(steps - 1)
    send(hops, 0)
    add_lefts(2)
    prepare(hops - 2, 1)
    prepare(hops - 1, 0)
    for s in range(hops - 1, 0, -1):
        if s > 1:
            send(s - 1, 1)
        send(s, 0, arrived[1] if s == 1 else ())
        if s == 2:
            own_a, own_b = scatter(0, [0, 1], [], f32)
        if s > 1:
            add_lefts(1)
            if s > 2:
                prepare(s - 2, 1)
            prepare(s - 1, 0)
            add_lefts(1 if s > 2 else 2)
    add_lefts(steps)
    update, gradient, early = output_side()
    arrived1, arrived2 = arrived[0], [arrived[1][1], arrived[1][0]]

    late, keep, give = call(
        functools.partial(right_gradient_kernel, slot),
        "right_gradient",
        [chain_lengths, normed, w_in, early, own_a, own_b]
        + [arrived1[0], arrived2[0], arrived1[1], arrived2[1]],
        [SMEM] + [VMEM] * 9,
        [shape_of((here, half, 2 * hidden), bf16)]
        + [shape_of((channels // 2, 6 * hidden), bf16)] * 2,
        [mask, pltpu.VMEM((channels, 2 * hidden), f32)],
    )
    mine = add(keep, swap_col(give))

    def from_row(apart):
        return lax.ppermute(mine, "row", [(r, r ^ apart) for r in range(row_count)])

    step = 1
    if row_count % 4 == 0:
        one, two, three = [from_row(apart).astype(f32) for apart in (1, 2, 3)]
        mine = ((mine.astype(f32) + one) + (two + three)).astype(bf16)
        step = 4
    while step < row_count:
        mine = add(mine, from_row(step))
        step *= 2
    (pair_gradient,) = call(
        pair_gradient_kernel,
        "pair_gradient",
        [pair, late, in_gain, w_in, gradient],
        [VMEM] * 5,
        [shape_of(block, bf16)],
        microseconds=3,
    )
    mine, pair_gradient = lax.optimization_barrier((mine, pair_gradient))
    grad_w_in, grad_w_out = call(
        weights_kernel,
        "weight_gradients",
        [mine, swap_col(mine)],
        [VMEM] * 2,
        [shape_of(w_in.shape, f32), shape_of(w_out.shape, f32)],
    )
    return (update, pair_gradient, grad_w_in, grad_w_out)


def solution(mesh):
    placed = (
        P(("grp", "row"), "col", None),
        P(("grp", "row"), "col", None),
        P("grp"),
        P(),
        P(),
        P(),
        P(),
        P(),
        P(),
    )
    return jax.shard_map(
        shards,
        mesh=mesh,
        in_specs=placed,
        out_specs=(
            P(("grp", "row"), "col", None),
            P(("grp", "row"), "col", None),
            P("grp", None),
            P("grp", None),
        ),
        check_vma=False,
    )
```
